32 devices in a mesh: gene: 4 (over y, x), bin: 8 (over z, core).
Axes of the slice: x: 2, y: 2, z: 4, core: 2. Of those that a mesh axis runs over, the one named last changes fastest.
Arguments:
- counts: bfloat16 [24576, 18432], P('bin', 'gene'), may hold values from 2 to 80
- factors: float32 [24576, 256], P('bin'), may hold values from 0.01 to 1
- loadings: float32 [256, 18432], P(None, 'gene'), may hold values from 0.01 to 1
- position: int32 [24576], P('bin'), may hold values from 0 to 24575, as said below
- edge_codes: int32 [96, 256], P('bin'), may hold values from 1 to 15
Outputs:
- factors_new: float32 [24576, 256], P('bin')
- loadings_new: float32 [256, 18432], P(None, 'gene')
The draws below stay inside these ranges and needn't reach their ends.
Inputs may be any that keep to these rules, and one draw needn't show every extreme that they name: Each grid position is named by exactly one barcode. The barcodes of one index s of bin (rows s * 3072 on) fall in 8 aligned groups of 384; group t holds positions in grid rows t * 12 to (t + 1) * 12 - 1, 384 from every such index.
All inputs are finite; a program needn't handle non-finite values.
Results may differ from the reference program's by a relative error of at most 0.0003.
Values sent between devices are 32-bit elements; how exact they have to be, the bound alone decides.
No kernel may reach another device: no remote copies, remote signals or barrier semaphores. Data moves between devices by JAX's collectives and lax.ppermute only.
A program may use at most 128 MiB of HBM per device.

```python
import math
import jax
import jax.numpy as jnp
from jax import lax

K = 256
G = 18432
GCOL = 256
NROWS = 96
BINS_DEV = 3072
BINS = 24576
GROUP = 384
N_BIN = 8


def draw_position(key, part):
    orders = jax.vmap(lambda band: jax.random.permutation(jax.random.fold_in(key, band), BINS_DEV))(jnp.arange(N_BIN))
    blocks = orders.astype(jnp.int32).reshape(N_BIN, N_BIN, GROUP)
    blocks = blocks + (jnp.arange(N_BIN, dtype=jnp.int32) * BINS_DEV)[:, None, None]
    return jnp.transpose(blocks, (1, 0, 2)).reshape(BINS).astype(jnp.int32)


def set_ends(values, stream_key, least, largest):
    index_at = [jax.random.randint(jax.random.fold_in(stream_key, axis), (), 0, length) for axis, length in enumerate(values.shape)]
    longest = values.shape.index(max(values.shape))
    beside = index_at[:longest] + [(index_at[longest] + 1) % values.shape[longest]] + index_at[longest + 1:]
    return values.at[tuple(index_at)].set(least).at[tuple(beside)].set(largest)


def shard_levels(key, extent, pieces, smallest, high):
    level, own = 1.0, jax.random.fold_in(key, 6)
    for axis_at, parts in pieces:
        steps = jnp.exp(jax.random.uniform(jax.random.fold_in(own, axis_at), (parts,), jnp.float32, smallest / len(pieces), high / len(pieces)))
        level = level * jnp.repeat(steps, extent[axis_at] // parts).reshape([-1 if axis == axis_at else 1 for axis in range(len(extent))])
    return level


def setup_inputs(seed: int = 0) -> dict:
    streams_of = jax.random.split(jax.random.key(seed), 6)
    counts = jnp.clip(jnp.exp(math.log(80.0) - 3.6888795 * jax.random.uniform(streams_of[0], (BINS, G), jnp.float32) ** shard_levels(streams_of[0], (BINS, G), ((0, 8), (1, 4)), -0.2, 0.2)), 2.0, 80.0).astype(jnp.bfloat16)
    factors = jnp.clip(jnp.exp(math.log(1.0) - 4.6051702 * jax.random.uniform(streams_of[1], (BINS, K), jnp.float32) ** shard_levels(streams_of[1], (BINS, K), ((0, 8),), -0.2, 0.2)), 0.01, 1.0)
    loadings = jnp.clip(jnp.exp(math.log(1.0) - 4.6051702 * jax.random.uniform(streams_of[2], (K, G), jnp.float32) ** shard_levels(streams_of[2], (K, G), ((1, 4),), -0.2, 0.2)), 0.01, 1.0)
    position = draw_position(jax.random.fold_in(streams_of[5], 71), 0)
    edge_codes = set_ends(jax.random.randint(streams_of[4], (NROWS, GCOL), 1, 16), jax.random.fold_in(streams_of[4], 1), 1, 15).astype(jnp.int32)
    return {"counts": counts, "factors": factors, "loadings": loadings, "position": position, "edge_codes": edge_codes}


def neighbours(values):
    beside = jnp.pad(values[:, 1:], ((0, 0), (0, 1), (0, 0))) + jnp.pad(values[:, :-1], ((0, 0), (1, 0), (0, 0)))
    vertical = jnp.pad(values[1:], ((0, 1), (0, 0), (0, 0))) + jnp.pad(values[:-1], ((1, 0), (0, 0), (0, 0)))
    return beside + 0.5 * vertical


def reference(counts, factors, loadings, position, edge_codes):
    load_bf = loadings.astype(jnp.bfloat16)
    numer = jnp.dot(counts, load_bf.T, preferred_element_type=jnp.float32)
    load_gram = jnp.dot(load_bf, load_bf.T, preferred_element_type=jnp.float32)
    grid_w = jnp.zeros((BINS, K), jnp.float32).at[position].set(factors).reshape(NROWS, GCOL, K)
    cell_scale = edge_codes.astype(jnp.float32) / 8.0
    weighted = cell_scale[:, :, None] * grid_w
    smooth_grid = cell_scale[:, :, None] * neighbours(weighted)
    degree_grid = cell_scale * neighbours(cell_scale[:, :, None])[:, :, 0]
    smooth = smooth_grid.reshape(BINS, K)[position]
    degree = degree_grid.reshape(BINS)[position]
    penalty = float(G * K) / 64.0
    denom = jnp.dot(factors, load_gram, precision=lax.Precision.HIGHEST) + penalty * degree[:, None] * factors
    factors_new = factors * (numer + penalty * smooth) / denom
    fac_bf = factors_new.astype(jnp.bfloat16)
    cross = jnp.dot(fac_bf.T, counts, preferred_element_type=jnp.float32)
    fac_gram = jnp.dot(fac_bf.T, fac_bf, preferred_element_type=jnp.float32)
    loadings_new = loadings * cross / jnp.dot(fac_gram, loadings, precision=lax.Precision.HIGHEST)
    return factors_new, loadings_new
```

```python
import functools
import jax
import jax.numpy as jnp
from jax import lax
from jax.experimental import pallas as pl
from jax.experimental.pallas import tpu as pltpu
from jax.sharding import PartitionSpec as P

K = 256
G = 18432
PENALTY = float(G * K) / 64.0
EXTRA = 8
CHUNKS = 6
VMEM = 48 * 1024 * 1024
MINOR = (((1,), (1,)), ((), ()))
PLAIN = (((1,), (0,)), ((), ()))
F32 = jnp.float32
BF16 = jnp.bfloat16


def dot(a, b, dims, precision=None):
    return lax.dot_general(a, b, dims, precision=precision, preferred_element_type=F32)


def kernel_call(body, out_shape, flops, nbytes, **kw):
    return pl.pallas_call(
        body,
        out_shape=out_shape,
        compiler_params=pltpu.CompilerParams(vmem_limit_bytes=VMEM),
        cost_estimate=pl.CostEstimate(flops=int(flops), bytes_accessed=int(nbytes), transcendentals=0),
        **kw,
    )


def shape(*dims, dtype=F32):
    return jax.ShapeDtypeStruct(dims, dtype)


SMEM_SPEC = pl.BlockSpec(memory_space=pltpu.SMEM)


def pack(factors, position, me, width, bins):
    rows, width_all = factors.shape
    group = rows // bins
    lanes = 128 if width_all % 128 == 0 and 128 % width == 0 else width_all

    def body(me_ref, fac_ref, pos_ref, out_ref, turned):
        turned[...] = fac_ref[...].T
        first = pl.multiple_of(lax.rem(me_ref[0] * width, lanes), width)
        out_ref[0, :width, :] = turned[pl.ds(first, width), :]
        out_ref[0, width:, :] = jnp.broadcast_to(pos_ref[0], (EXTRA, group))

    grid_spec = pltpu.PrefetchScalarGridSpec(
        num_scalar_prefetch=1,
        grid=(bins,),
        in_specs=[
            pl.BlockSpec((group, lanes), lambda t, m: (t, m[0] * width // lanes)),
            pl.BlockSpec((1, 1, group), lambda t, m: (t, 0, 0)),
        ],
        out_specs=pl.BlockSpec((1, width + EXTRA, group), lambda t, m: (t, 0, 0)),
        scratch_shapes=[pltpu.VMEM((lanes, group), F32)],
    )
    return kernel_call(
        body, shape(bins, width + EXTRA, group), 0, 6 * rows * width * 4, grid_spec=grid_spec
    )(me, factors, position.astype(F32).reshape(bins, 1, group))


def to_grid(got, edge_codes, bin_me):
    bins, wide, group = got.shape
    width = wide - EXTRA
    grid_rows, grid_cols = edge_codes.shape
    rows = bins * group

    def body(me_ref, got_ref, code_ref, grid_ref, first_ref, last_ref, cell_ref, masked):
        block = jnp.concatenate([got_ref[s] for s in range(bins)], axis=1)
        cell = block[width : width + 1].astype(jnp.int32) - me_ref[0] * rows
        cell_ref[...] = cell
        at_row, at_col = cell // grid_cols, cell % grid_cols
        col_hot = jnp.where(
            lax.broadcasted_iota(jnp.int32, (grid_cols, rows), 0) == at_col, 1.0, 0.0
        ).astype(BF16)
        values = block[:width]
        high = values.astype(BF16)
        both = jnp.concatenate([high, (values - high.astype(F32)).astype(BF16)], axis=0)
        for r in range(grid_rows):
            mask = jnp.where(at_row == r, 1.0, 0.0).astype(BF16)
            masked[r * 2 * width : (r + 1) * 2 * width, :] = both * mask
        placed = dot(masked[...], col_hot, MINOR)
        scale = code_ref[...].astype(F32) / 8.0
        for r in range(grid_rows):
            at = r * 2 * width
            line = placed[at : at + width] + placed[at + width : at + 2 * width]
            row_scale = scale[r : r + 1]
            weighted = jnp.concatenate(
                [line * row_scale, jnp.broadcast_to(row_scale, (EXTRA, grid_cols))], axis=0
            )
            grid_ref[r] = weighted
            if r == 0:
                first_ref[...] = weighted
            if r == grid_rows - 1:
                last_ref[...] = weighted

    vm = pl.BlockSpec(memory_space=pltpu.VMEM)
    return kernel_call(
        body,
        (
            shape(grid_rows, wide, grid_cols),
            shape(wide, grid_cols),
            shape(wide, grid_cols),
            shape(1, rows, dtype=jnp.int32),
        ),
        4 * rows * rows * width,
        8 * rows * wide,
        in_specs=[SMEM_SPEC, vm, vm],
        out_specs=(vm, vm, vm, vm),
        scratch_shapes=[pltpu.VMEM((grid_rows * 2 * width, rows), BF16)],
    )(bin_me, got, edge_codes)


def from_grid(grid, above, below, cell, edge_codes, bins):
    grid_rows, wide, grid_cols = grid.shape
    rows = cell.shape[1]
    group = rows // bins

    def body(grid_ref, above_ref, below_ref, cell_ref, code_ref, out_ref, halves):
        scale = code_ref[...].astype(F32) / 8.0
        lane = lax.broadcasted_iota(jnp.int32, (wide, grid_cols), 1)
        for r in range(grid_rows):
            here = grid_ref[r]
            upper = above_ref[...] if r == 0 else grid_ref[r - 1]
            lower = below_ref[...] if r == grid_rows - 1 else grid_ref[r + 1]
            left = jnp.where(lane == 0, 0.0, pltpu.roll(here, 1, 1))
            right = jnp.where(lane == grid_cols - 1, 0.0, pltpu.roll(here, grid_cols - 1, 1))
            value = scale[r : r + 1] * (left + right + 0.5 * (upper + lower))
            high = value.astype(BF16)
            halves[r * wide : (r + 1) * wide, :grid_cols] = high
            halves[r * wide : (r + 1) * wide, grid_cols:] = (value - high.astype(F32)).astype(BF16)
        cell = cell_ref[...]
        at_row, at_col = cell // grid_cols, cell % grid_cols
        for s in range(bins // 2):
            lo, hi = 2 * s * group, (2 * s + 2) * group
            hot = jnp.where(
                lax.broadcasted_iota(jnp.int32, (grid_cols, hi - lo), 0) == at_col[:, lo:hi], 1.0, 0.0
            ).astype(BF16)
            lines = dot(halves[...], jnp.concatenate([hot, hot], axis=0), PLAIN)
            row_here = at_row[:, lo:hi]
            total = jnp.zeros((wide, hi - lo), F32)
            for r in range(grid_rows):
                total = total + jnp.where(row_here == r, lines[r * wide : (r + 1) * wide], 0.0)
            out_ref[2 * s] = total[:, :group]
            out_ref[2 * s + 1] = total[:, group:]

    vm = pl.BlockSpec(memory_space=pltpu.VMEM)
    return kernel_call(
        body,
        shape(bins, wide, group),
        4 * rows * rows * wide,
        8 * rows * wide,
        in_specs=[vm] * 5,
        out_specs=vm,
        scratch_shapes=[pltpu.VMEM((grid_rows * wide, 2 * grid_cols), BF16)],
    )(grid, above, below, cell, edge_codes)


def numer_part(counts, loadings, me, genes_n, half, send_ids, with_gram):
    rows, genes = counts.shape
    width_all = loadings.shape[0]
    width = width_all // genes_n
    step = 256
    steps = rows // 2 // step
    keep_ids = [k for k in range(genes_n) if k not in send_ids]
    total_cols = (steps + with_gram) * step

    def body(me_ref, counts_ref, load_ref, send_ref, keep_ref, load_bf):
        at = pl.program_id(0)

        @pl.when(at == 0)
        def _():
            for k in range(genes_n):
                first = pl.multiple_of((k ^ me_ref[0]) * width, width)
                load_bf[k * width : (k + 1) * width, :] = load_ref[pl.ds(first, width), :].astype(BF16)

        def put(other):
            part = dot(load_bf[...], other, MINOR)
            for i, k in enumerate(send_ids):
                send_ref[i] = part[k * width : (k + 1) * width]
            for i, k in enumerate(keep_ids):
                keep_ref[i] = part[k * width : (k + 1) * width]

        if with_gram:
            pl.when(at < steps)(lambda: put(counts_ref[...]))
            pl.when(at == steps)(lambda: put(load_ref[...].astype(BF16)))
        else:
            put(counts_ref[...])

    out_spec = pl.BlockSpec((genes_n // 2, width, step), lambda i, m: (0, 0, i))
    grid_spec = pltpu.PrefetchScalarGridSpec(
        num_scalar_prefetch=1,
        grid=(steps + with_gram,),
        in_specs=[
            pl.BlockSpec((step, genes), lambda i, m: (jnp.minimum(i, steps - 1) + half * steps, 0)),
            pl.BlockSpec((width_all, genes), lambda i, m: (0, 0)),
        ],
        out_specs=(out_spec, out_spec),
        scratch_shapes=[pltpu.VMEM((width_all, genes), BF16)],
    )
    out = shape(genes_n // 2, width, total_cols)
    return kernel_call(
        body,
        (out, out),
        2 * total_cols * genes * width_all,
        rows * genes + 4 * genes * width_all + 4 * total_cols * width_all,
        grid_spec=grid_spec,
    )(me, counts, loadings)


def swap(block, axis, bit):
    return lax.ppermute(block, axis, [(i, i ^ bit) for i in range(lax.axis_size(axis))])


def scatter_sum(send, keep, send_ids, keep_ids, bits):
    got = swap(send, "gene", bits[0])
    for bit in bits[1:]:
        out_ids = [i for i, k in enumerate(keep_ids) if k & bit]
        in_ids = [i for i, k in enumerate(keep_ids) if not k & bit]
        pick = lambda x, ids: jnp.stack([x[i] for i in ids])
        send = pick(keep, out_ids) + pick(got, out_ids)
        keep = pick(keep, in_ids) + pick(got, in_ids)
        keep_ids = [keep_ids[i] for i in in_ids]
        got = swap(send, "gene", bit)
    return keep[0] + got[0]


def gather_blocks(block, bits):
    have, ids = block[None], [0]
    for bit in bits[:-1]:
        have = jnp.concatenate([have, swap(have, "gene", bit)])
        ids = ids + [k | bit for k in ids]
    return have, ids, swap(have, "gene", bits[-1]), [k | bits[-1] for k in ids]


def new_factors(payload, back, numer, gram, factors, half):
    bins, wide, group = payload.shape
    width = wide - EXTRA
    cols = numer.shape[1]
    steps = bins // 4
    width_all = factors.shape[1]

    def body(pay_ref, back_ref, numer_ref, gram_ref, fac_ref, out_ref):
        plain = dot(gram_ref[...], fac_ref[...], MINOR, lax.Precision.HIGHEST)
        pay = jnp.concatenate([pay_ref[0], pay_ref[1]], axis=1)
        got = jnp.concatenate([back_ref[0], back_ref[1]], axis=1)
        fac, smooth, degree = pay[:width], got[:width], got[width : width + 1]
        out_ref[...] = (
            fac * (numer_ref[...] + PENALTY * smooth) / (plain + PENALTY * degree * fac)
        )

    pair = pl.BlockSpec((2, wide, group), lambda i: (i + half * steps, 0, 0))
    return kernel_call(
        body,
        shape(width, steps * 2 * group),
        12 * width * width_all * steps * 2 * group,
        4 * steps * 2 * group * (width_all + 4 * width),
        grid=(steps,),
        in_specs=[
            pair,
            pair,
            pl.BlockSpec((width, 2 * group), lambda i: (0, i)),
            pl.BlockSpec((width, width_all), lambda i: (0, 0)),
            pl.BlockSpec((2 * group, width_all), lambda i: (i + half * steps, 0)),
        ],
        out_specs=pl.BlockSpec((width, 2 * group), lambda i: (0, i)),
    )(payload, back, numer, gram, factors)


def rounded(parts, ids, width):
    cols = parts[0].shape[2]
    blocks = len(ids[0]) + len(ids[1])

    def body(a0, a1, b0, b1, out_ref):
        for j, (x, y) in enumerate(((a0, a1), (b0, b1))):
            for ref, its in ((x, ids[2 * j]), (y, ids[2 * j + 1])):
                for i, k in enumerate(its):
                    out_ref[k * width : (k + 1) * width, j * cols : (j + 1) * cols] = ref[i].astype(BF16)

    vm = pl.BlockSpec(memory_space=pltpu.VMEM)
    return kernel_call(
        body,
        shape(blocks * width, 2 * cols, dtype=BF16),
        0,
        blocks * width * 2 * cols * 6,
        in_specs=[vm] * 4,
        out_specs=vm,
    )(*parts)


def turned_back(parts, ids, width, me):
    cols = parts[0].shape[2]
    blocks = len(ids[0]) + len(ids[1])
    step = 384
    steps = cols // step

    def body(me_ref, a0, a1, b0, b1, out_ref, block):
        at = pl.program_id(0)

        def put(refs, its):
            for ref, ks in zip(refs, its):
                for i, k in enumerate(ks):
                    first = pl.multiple_of((k ^ me_ref[0]) * width, width)
                    block[pl.ds(first, width), :] = ref[i]

        pl.when(at < steps)(lambda: put((a0, a1), ids[:2]))
        pl.when(at >= steps)(lambda: put((b0, b1), ids[2:]))
        out_ref[...] = block[...].T

    spec_a = pl.BlockSpec((blocks // 2, width, step), lambda i, m: (0, 0, jnp.minimum(i, steps - 1)))
    spec_b = pl.BlockSpec((blocks // 2, width, step), lambda i, m: (0, 0, jnp.maximum(i - steps, 0)))
    grid_spec = pltpu.PrefetchScalarGridSpec(
        num_scalar_prefetch=1,
        grid=(2 * steps,),
        in_specs=[spec_a, spec_a, spec_b, spec_b],
        out_specs=pl.BlockSpec((step, blocks * width), lambda i, m: (i, 0)),
        scratch_shapes=[pltpu.VMEM((blocks * width, step), F32)],
    )
    return kernel_call(
        body,
        shape(2 * cols, blocks * width),
        0,
        blocks * width * 2 * cols * 8,
        grid_spec=grid_spec,
    )(me, *parts)


def cross_part(fac_bf, counts, core, chunk, cols, with_gram):
    width_all, rows = fac_bf.shape
    half = width_all // 2
    extra = width_all if with_gram else 0

    def body(core_ref, fac_ref, counts_ref, send_ref, keep_ref):
        for ref, which in ((send_ref, 1 - core_ref[0]), (keep_ref, core_ref[0])):
            mine = fac_ref[pl.ds(pl.multiple_of(which * half, half), half), :]
            ref[:, :cols] = dot(mine, counts_ref[...], PLAIN)
            if with_gram:
                ref[:, cols:] = dot(mine, fac_ref[...], MINOR)

    out_spec = pl.BlockSpec((half, cols + extra), lambda i, c: (0, 0))
    grid_spec = pltpu.PrefetchScalarGridSpec(
        num_scalar_prefetch=1,
        grid=(1,),
        in_specs=[
            pl.BlockSpec((width_all, rows), lambda i, c: (0, 0)),
            pl.BlockSpec((rows, cols), lambda i, c: (0, chunk)),
        ],
        out_specs=(out_spec, out_spec),
    )
    return kernel_call(
        body,
        (shape(half, cols + extra),) * 2,
        2 * rows * width_all * (cols + extra),
        2 * rows * (cols + width_all) + 4 * width_all * (cols + extra),
        grid_spec=grid_spec,
    )(core, fac_bf, counts)


def bin_sum(send, keep):
    bins = lax.axis_size("bin")
    line = bins // 2
    own = keep + swap(send, "bin", 1)
    total, got = own, None
    for step in range(1, line):
        hops = [(step - 1, step), (line - step, line - step - 1)]
        route = [(2 * a + c, 2 * b + c) for a, b in hops for c in range(2)]
        got = lax.ppermute(own if got is None else own + got, "bin", route)
        total = total + got
    return total, swap(total, "bin", 1)


def new_loadings(loadings, mine, other, gram_mine, gram_other, before, flags, genes_n, chunk, cols):
    width_all, genes = loadings.shape
    width = width_all // genes_n
    half = width_all // 2

    def body(flag_ref, load_ref, mine_ref, other_ref, gm_ref, go_ref, *rest):
        out_ref, load, cross, gram = rest[-4:]
        me, core = flag_ref[0], flag_ref[1]
        at_mine = pl.ds(pl.multiple_of(core * half, half), half)
        at_other = pl.ds(pl.multiple_of((1 - core) * half, half), half)
        cross[at_mine, :] = mine_ref[...]
        cross[at_other, :] = other_ref[...]
        gram[at_mine, :] = gm_ref[...]
        gram[at_other, :] = go_ref[...]
        firsts = [pl.multiple_of((k ^ me) * width, width) for k in range(genes_n)]
        for k, first in enumerate(firsts):
            load[k * width : (k + 1) * width, :] = load_ref[pl.ds(first, width), :]
        below = dot(gram[...], load[...], PLAIN, lax.Precision.HIGHEST)
        cross[...] = load[...] * cross[...] / below
        for k, first in enumerate(firsts):
            out_ref[pl.ds(first, width), :] = cross[k * width : (k + 1) * width, :]

    full = pl.BlockSpec((width_all, cols), lambda i, f: (0, chunk))
    part = pl.BlockSpec((half, cols), lambda i, f: (0, 0))
    gram_at = gram_mine.shape[1] // width_all - 1
    gram_spec = pl.BlockSpec((half, width_all), lambda i, f: (0, gram_at))
    operands = [flags, loadings, mine, other, gram_mine, gram_other]
    in_specs = [full, part, part, gram_spec, gram_spec]
    aliases = {}
    if before is not None:
        operands.append(before)
        in_specs.append(pl.BlockSpec(memory_space=pl.ANY))
        aliases = {len(operands) - 1: 0}
    grid_spec = pltpu.PrefetchScalarGridSpec(
        num_scalar_prefetch=1,
        grid=(1,),
        in_specs=in_specs,
        out_specs=full,
        scratch_shapes=[
            pltpu.VMEM((width_all, cols), F32),
            pltpu.VMEM((width_all, cols), F32),
            pltpu.VMEM((width_all, width_all), F32),
        ],
    )
    return kernel_call(
        body,
        shape(width_all, genes),
        12 * width_all * width_all * cols,
        12 * width_all * cols,
        grid_spec=grid_spec,
        input_output_aliases=aliases,
    )(*operands)


def on_device(counts, factors, loadings, position, edge_codes):
    bins, genes_n = lax.axis_size("bin"), lax.axis_size("gene")
    me, bin_me = lax.axis_index("gene"), lax.axis_index("bin")
    rows, width_all = factors.shape
    genes = counts.shape[1]
    width = width_all // genes_n
    scalar = lambda x: jnp.asarray(x, jnp.int32).reshape(1)
    me1, bin1, core1 = scalar(me), scalar(bin_me), scalar(bin_me % 2)
    flags = jnp.concatenate([me1, core1])
    bits = [1 << b for b in range(genes_n.bit_length() - 1)]
    orders = (bits, bits[::-1])

    payload = pack(factors, position, me1, width, bins)
    got = lax.all_to_all(payload, "bin", split_axis=0, concat_axis=0, tiled=True)

    numer, gram = [], None
    for half in (0, 1):
        bit = orders[half][0]
        send_ids = [k for k in range(genes_n) if k & bit]
        keep_ids = [k for k in range(genes_n) if not k & bit]
        send, keep = numer_part(counts, loadings, me1, genes_n, half, send_ids, half == 0)
        numer.append(scatter_sum(send, keep, send_ids, keep_ids, orders[half]))
    gram = numer[0][:, rows // 2 :]

    grid, first, last, cell = to_grid(got, edge_codes, bin1)
    above = lax.ppermute(last, "bin", [(i, i + 1) for i in range(bins - 1)])
    below = lax.ppermute(first, "bin", [(i + 1, i) for i in range(bins - 1)])
    smooth = from_grid(grid, above, below, cell, edge_codes, bins)
    back = lax.all_to_all(smooth, "bin", split_axis=0, concat_axis=0, tiled=True)

    parts, ids = [], []
    for half in (0, 1):
        block = new_factors(payload, back, numer[half], gram, factors, half)
        have, have_ids, more, more_ids = gather_blocks(block, orders[half][::-1])
        parts += [have, more]
        ids += [have_ids, more_ids]
    fac_bf = rounded(parts, ids, width)
    factors_new = turned_back(parts, ids, width, me1)

    cols = genes // CHUNKS
    loadings_new = None
    for chunk in range(CHUNKS):
        send, keep = cross_part(fac_bf, counts, core1, chunk, cols, chunk == 0)
        mine, other = bin_sum(send, keep)
        if chunk == 0:
            gram_mine, gram_other = mine, other
            gram_mine, gram_other = mine[:, cols:], other[:, cols:]
        loadings_new = new_loadings(
            loadings, mine, other, gram_mine, gram_other, loadings_new, flags, genes_n, chunk, cols
        )
    return factors_new, loadings_new


def solution(mesh):
    placed = (P("bin", "gene"), P("bin", None), P(None, "gene"), P("bin"), P("bin", None))
    return jax.shard_map(
        on_device,
        mesh=mesh,
        in_specs=placed,
        out_specs=(P("bin", None), P(None, "gene")),
        check_vma=False,
    )
```

```python
import functools
import jax
import jax.numpy as jnp
from jax import lax
from jax.experimental import pallas as pl
from jax.experimental.pallas import tpu as pltpu
from jax.sharding import PartitionSpec as P

K = 256
G = 18432
PENALTY = float(G * K) / 64.0
EXTRA = 8
HALVES = 2
VMEM = 48 * 1024 * 1024
MINOR = (((1,), (1,)), ((), ()))
PLAIN = (((1,), (0,)), ((), ()))
F32 = jnp.float32
BF16 = jnp.bfloat16


def dot(a, b, dims, precision=None):
    return lax.dot_general(a, b, dims, precision=precision, preferred_element_type=F32)


def kernel_call(body, out_shape, flops, nbytes, **kw):
    return pl.pallas_call(
        body,
        out_shape=out_shape,
        compiler_params=pltpu.CompilerParams(vmem_limit_bytes=VMEM),
        cost_estimate=pl.CostEstimate(flops=int(flops), bytes_accessed=int(nbytes), transcendentals=0),
        **kw,
    )


def shape(*dims, dtype=F32):
    return jax.ShapeDtypeStruct(dims, dtype)


SMEM_SPEC = pl.BlockSpec(memory_space=pltpu.SMEM)


def pack(factors, position, me, width, bins):
    rows, width_all = factors.shape
    group = rows // bins
    lanes = 128 if width_all % 128 == 0 and 128 % width == 0 else width_all

    def body(me_ref, fac_ref, pos_ref, out_ref, turned):
        turned[...] = fac_ref[...].T
        first = pl.multiple_of(lax.rem(me_ref[0] * width, lanes), width)
        out_ref[0, :width, :] = turned[pl.ds(first, width), :]
        out_ref[0, width:, :] = jnp.broadcast_to(pos_ref[0], (EXTRA, group))

    grid_spec = pltpu.PrefetchScalarGridSpec(
        num_scalar_prefetch=1,
        grid=(bins,),
        in_specs=[
            pl.BlockSpec((group, lanes), lambda t, m: (t, m[0] * width // lanes)),
            pl.BlockSpec((1, 1, group), lambda t, m: (t, 0, 0)),
        ],
        out_specs=pl.BlockSpec((1, width + EXTRA, group), lambda t, m: (t, 0, 0)),
        scratch_shapes=[pltpu.VMEM((lanes, group), F32)],
    )
    return kernel_call(
        body, shape(bins, width + EXTRA, group), 0, 6 * rows * width * 4, grid_spec=grid_spec
    )(me, factors, position.astype(F32).reshape(bins, 1, group))


def to_grid(got, edge_codes, bin_me):
    bins, wide, group = got.shape
    width = wide - EXTRA
    grid_rows, grid_cols = edge_codes.shape
    rows = bins * group

    def body(me_ref, got_ref, code_ref, grid_ref, first_ref, last_ref, cell_ref, masked):
        block = jnp.concatenate([got_ref[s] for s in range(bins)], axis=1)
        cell = block[width : width + 1].astype(jnp.int32) - me_ref[0] * rows
        cell_ref[...] = cell
        at_row, at_col = cell // grid_cols, cell % grid_cols
        col_hot = jnp.where(
            lax.broadcasted_iota(jnp.int32, (grid_cols, rows), 0) == at_col, 1.0, 0.0
        ).astype(BF16)
        values = block[:width]
        high = values.astype(BF16)
        both = jnp.concatenate([high, (values - high.astype(F32)).astype(BF16)], axis=0)
        for r in range(grid_rows):
            mask = jnp.where(at_row == r, 1.0, 0.0).astype(BF16)
            masked[r * 2 * width : (r + 1) * 2 * width, :] = both * mask
        placed = dot(masked[...], col_hot, MINOR)
        scale = code_ref[...].astype(F32) / 8.0
        for r in range(grid_rows):
            at = r * 2 * width
            line = placed[at : at + width] + placed[at + width : at + 2 * width]
            row_scale = scale[r : r + 1]
            weighted = jnp.concatenate(
                [line * row_scale, jnp.broadcast_to(row_scale, (EXTRA, grid_cols))], axis=0
            )
            grid_ref[r] = weighted
            if r == 0:
                first_ref[...] = weighted
            if r == grid_rows - 1:
                last_ref[...] = weighted

    vm = pl.BlockSpec(memory_space=pltpu.VMEM)
    return kernel_call(
        body,
        (
            shape(grid_rows, wide, grid_cols),
            shape(wide, grid_cols),
            shape(wide, grid_cols),
            shape(1, rows, dtype=jnp.int32),
        ),
        4 * rows * rows * width,
        8 * rows * wide,
        in_specs=[SMEM_SPEC, vm, vm],
        out_specs=(vm, vm, vm, vm),
        scratch_shapes=[pltpu.VMEM((grid_rows * 2 * width, rows), BF16)],
    )(bin_me, got, edge_codes)


def from_grid(grid, above, below, cell, edge_codes, bins):
    grid_rows, wide, grid_cols = grid.shape
    rows = cell.shape[1]
    group = rows // bins

    def body(grid_ref, above_ref, below_ref, cell_ref, code_ref, out_ref, halves):
        scale = code_ref[...].astype(F32) / 8.0
        lane = lax.broadcasted_iota(jnp.int32, (wide, grid_cols), 1)
        for r in range(grid_rows):
            here = grid_ref[r]
            upper = above_ref[...] if r == 0 else grid_ref[r - 1]
            lower = below_ref[...] if r == grid_rows - 1 else grid_ref[r + 1]
            left = jnp.where(lane == 0, 0.0, pltpu.roll(here, 1, 1))
            right = jnp.where(lane == grid_cols - 1, 0.0, pltpu.roll(here, grid_cols - 1, 1))
            value = scale[r : r + 1] * (left + right + 0.5 * (upper + lower))
            high = value.astype(BF16)
            halves[r * wide : (r + 1) * wide, :grid_cols] = high
            halves[r * wide : (r + 1) * wide, grid_cols:] = (value - high.astype(F32)).astype(BF16)
        cell = cell_ref[...]
        at_row, at_col = cell // grid_cols, cell % grid_cols
        for s in range(bins // 2):
            lo, hi = 2 * s * group, (2 * s + 2) * group
            hot = jnp.where(
                lax.broadcasted_iota(jnp.int32, (grid_cols, hi - lo), 0) == at_col[:, lo:hi], 1.0, 0.0
            ).astype(BF16)
            lines = dot(halves[...], jnp.concatenate([hot, hot], axis=0), PLAIN)
            row_here = at_row[:, lo:hi]
            total = jnp.zeros((wide, hi - lo), F32)
            for r in range(grid_rows):
                total = total + jnp.where(row_here == r, lines[r * wide : (r + 1) * wide], 0.0)
            out_ref[2 * s] = total[:, :group]
            out_ref[2 * s + 1] = total[:, group:]

    vm = pl.BlockSpec(memory_space=pltpu.VMEM)
    return kernel_call(
        body,
        shape(bins, wide, group),
        4 * rows * rows * wide,
        8 * rows * wide,
        in_specs=[vm] * 5,
        out_specs=vm,
        scratch_shapes=[pltpu.VMEM((grid_rows * wide, 2 * grid_cols), BF16)],
    )(grid, above, below, cell, edge_codes)


def numer_part(counts, loadings, me, genes_n, half, send_ids, with_gram):
    rows, genes = counts.shape
    width_all = loadings.shape[0]
    width = width_all // genes_n
    step = 512
    steps = rows // 2 // step
    keep_ids = [k for k in range(genes_n) if k not in send_ids]
    total_cols = steps * step + with_gram * width_all
    first_call = loadings.dtype == F32

    def body(me_ref, counts_ref, load_ref, send_ref, keep_ref, *rest):
        at = pl.program_id(0)
        load_bf = rest[0] if first_call else load_ref
        firsts = [pl.multiple_of((k ^ me_ref[0]) * width, width) for k in range(genes_n)]

        if first_call:

            @pl.when(at == 0)
            def _():
                for k, first in enumerate(firsts):
                    load_bf[k * width : (k + 1) * width, :] = load_ref[pl.ds(first, width), :].astype(BF16)

        def put(part, cols):
            for i, k in enumerate(send_ids):
                send_ref[i, :, cols] = part[k * width : (k + 1) * width]
            for i, k in enumerate(keep_ids):
                keep_ref[i, :, cols] = part[k * width : (k + 1) * width]

        put(dot(counts_ref[...], load_bf[...], MINOR).T, pl.ds(pl.multiple_of(at * step, step), step))

        if with_gram:
            turned = rest[-1]

            @pl.when(at == steps - 1)
            def _():
                local = dot(load_bf[...], load_bf[...], MINOR)
                for k, first in enumerate(firsts):
                    turned[pl.ds(first, width), :] = local[k * width : (k + 1) * width]
                put(turned[...].T, slice(steps * step, total_cols))

    out = shape(genes_n // 2, width, total_cols)
    out_spec = pl.BlockSpec(out.shape, lambda i, m: (0, 0, 0))
    load_spec = pl.BlockSpec((width_all, genes), lambda i, m: (0, 0))
    grid_spec = pltpu.PrefetchScalarGridSpec(
        num_scalar_prefetch=1,
        grid=(steps,),
        in_specs=[pl.BlockSpec((step, genes), lambda i, m: (i + half * steps, 0)), load_spec],
        out_specs=(out_spec, out_spec) + (load_spec,) * first_call,
        scratch_shapes=[pltpu.VMEM((width_all, width_all), F32)] * with_gram,
    )
    return kernel_call(
        body,
        (out, out) + (shape(width_all, genes, dtype=BF16),) * first_call,
        2 * total_cols * genes * width_all,
        rows * genes + 4 * genes * width_all + 4 * total_cols * width_all,
        grid_spec=grid_spec,
    )(me, counts, loadings)


def swap(block, axis, bit):
    return lax.ppermute(block, axis, [(i, i ^ bit) for i in range(lax.axis_size(axis))])


def picked_sum(arrays, ids):
    _, width, cols = arrays[0].shape

    def body(*refs):
        total = refs[0][...]
        for ref in refs[1:-1]:
            total = total + ref[...]
        refs[-1][...] = total

    first, step = ids[0], (ids[1] - ids[0] if len(ids) > 1 else 1)
    return kernel_call(
        body,
        shape(len(ids), width, cols),
        0,
        4 * (len(arrays) + 1) * len(ids) * width * cols,
        grid=(len(ids),),
        in_specs=[pl.BlockSpec((1, width, cols), lambda i: (first + step * i, 0, 0))] * len(arrays),
        out_specs=pl.BlockSpec((1, width, cols), lambda i: (i, 0, 0)),
    )(*arrays)


def scatter_sum(send, keep, keep_ids, bits):
    arrays = [keep, swap(send, "gene", bits[0])]
    for bit in bits[1:]:
        out_ids = [i for i, k in enumerate(keep_ids) if k & bit]
        in_ids = [i for i, k in enumerate(keep_ids) if not k & bit]
        got = swap(picked_sum(arrays, out_ids), "gene", bit)
        if len(in_ids) == 1:
            arrays = arrays + [got]
        else:
            arrays = [picked_sum(arrays, in_ids), got]
        keep_ids = [keep_ids[i] for i in in_ids]
    return arrays


def plain_terms(numer, factors, rows, width):
    width_all = factors.shape[1]
    half_rows = rows // 2
    counts_in = [len(x) for x in numer]

    def body(*refs):
        parts = (refs[: counts_in[0]], refs[counts_in[0] : sum(counts_in)])
        fac_ref, numer_ref, plain_ref, gram = refs[-4:]
        at = pl.program_id(0)

        def total(half, cols):
            out = parts[half][0][0, :, cols]
            for ref in parts[half][1:]:
                out = out + ref[0, :, cols]
            return out

        @pl.when(at == 0)
        def _():
            gram[...] = total(0, slice(half_rows, half_rows + width_all))
            numer_ref[...] = total(0, slice(0, half_rows))

        @pl.when(at == 1)
        def _():
            numer_ref[...] = total(1, slice(0, half_rows))

        plain_ref[...] = dot(fac_ref[...], gram[...], MINOR, lax.Precision.HIGHEST).T

    whole = lambda x: pl.BlockSpec((1,) + x.shape[1:], lambda i: (0, 0, 0))
    out_spec = pl.BlockSpec((width, half_rows), lambda i: (0, i))
    arrays = list(numer[0]) + list(numer[1])
    return kernel_call(
        body,
        (shape(width, rows),) * 2,
        12 * width * width_all * rows,
        4 * rows * (width_all + 5 * width),
        grid=(2,),
        in_specs=[whole(x) for x in arrays] + [pl.BlockSpec((half_rows, width_all), lambda i: (i, 0))],
        out_specs=(out_spec, out_spec),
        scratch_shapes=[pltpu.VMEM((width, width_all), F32)],
    )(*arrays, factors)


def new_factors(payload, back, numer, plain):
    bins, wide, group = payload.shape
    width = wide - EXTRA

    def body(pay_ref, back_ref, numer_ref, plain_ref, out_ref):
        pay = jnp.concatenate([pay_ref[s] for s in range(bins)], axis=1)
        got = jnp.concatenate([back_ref[s] for s in range(bins)], axis=1)
        fac, smooth, degree = pay[:width], got[:width], got[width : width + 1]
        out_ref[...] = (
            fac * (numer_ref[...] + PENALTY * smooth) / (plain_ref[...] + PENALTY * degree * fac)
        )

    vm = pl.BlockSpec(memory_space=pltpu.VMEM)
    return kernel_call(
        body,
        shape(width, bins * group),
        0,
        4 * 5 * wide * bins * group,
        in_specs=[vm] * 4,
        out_specs=vm,
    )(payload, back, numer, plain)


def halves_out(blocks, token):
    width, rows = blocks[0][0].shape
    half_rows = rows // 2

    def body(*refs):
        n = len(blocks)
        for src, dst in zip(refs[:n], refs[n + 1 :]):
            dst[...] = src[...]

    spec = lambda half: pl.BlockSpec((width, half_rows), lambda i: (0, half))
    return kernel_call(
        body,
        (shape(width, half_rows),) * len(blocks),
        0,
        8 * len(blocks) * width * half_rows,
        grid=(1,),
        in_specs=[spec(h) for _, h in blocks] + [pl.BlockSpec(memory_space=pl.ANY)],
        out_specs=tuple(spec(0) for _ in blocks),
    )(*[b for b, _ in blocks], token)


def turned_back(blocks, ids, width, me, token):
    arrays = [x for b in blocks for x in b]
    rows = sum(x.shape[1] for x in blocks[0])
    width_all = len(ids) * width
    step = 384
    steps = rows // step

    def body(me_ref, *refs):
        out_ref, block = refs[-2:]
        at = pl.program_id(0)
        pos = 0
        for b, k in zip(blocks, ids):
            first = pl.multiple_of((k ^ me_ref[0]) * width, width)
            if len(b) == 1:
                block[pl.ds(first, width), :] = refs[pos][...]
            else:
                block[pl.ds(first, width), :] = jnp.where(at < steps // 2, refs[pos][...], refs[pos + 1][...])
            pos += len(b)
        out_ref[...] = block[...].T

    specs = []
    for b in blocks:
        if len(b) == 1:
            specs.append(pl.BlockSpec((width, step), lambda i, m: (0, i)))
        else:
            specs.append(pl.BlockSpec((width, step), lambda i, m: (0, jnp.minimum(i, steps // 2 - 1))))
            specs.append(pl.BlockSpec((width, step), lambda i, m: (0, jnp.maximum(i - steps // 2, 0))))
    grid_spec = pltpu.PrefetchScalarGridSpec(
        num_scalar_prefetch=1,
        grid=(steps,),
        in_specs=specs + [pl.BlockSpec(memory_space=pl.ANY)],
        out_specs=pl.BlockSpec((step, width_all), lambda i, m: (i, 0)),
        scratch_shapes=[pltpu.VMEM((width_all, step), F32)],
    )
    return kernel_call(
        body, shape(rows, width_all), 0, 8 * rows * width_all, grid_spec=grid_spec
    )(me, *arrays, token)


def cross_part(blocks, n_old, counts, flags, half, with_gram, width_all, token):
    arrays = [x for b in blocks for x in b]
    width = arrays[0].shape[0]
    rows, genes = counts.shape
    cols = genes // HALVES
    steps = 3
    step = cols // steps
    n_new = len(blocks) - n_old
    extra = width_all if with_gram else 0
    part = width // 2

    def body(flag_ref, counts_ref, *refs):
        send_ref, keep_ref, fac = refs[-3:]
        at = pl.program_id(0)
        core = flag_ref[1]

        @pl.when(at == 0)
        def _():
            pos = 0
            for j, b in enumerate(blocks):
                col = 0
                for x in b:
                    fac[j * width : (j + 1) * width, col : col + x.shape[1]] = refs[pos][...].astype(BF16)
                    col += x.shape[1]
                    pos += 1

        def put(result, where):
            for i in range(n_new):
                lo = result[i * width : i * width + part]
                hi = result[i * width + part : (i + 1) * width]
                send_ref[i, :, where] = jnp.where(core == 0, hi, lo)
                keep_ref[i, :, where] = jnp.where(core == 0, lo, hi)

        new = fac[n_old * width :, :]
        put(dot(new, counts_ref[...], PLAIN), pl.ds(pl.multiple_of(at * step, step), step))

        if with_gram:

            @pl.when(at == 0)
            def _():
                near = dot(new, fac[...], MINOR)
                if near.shape[1] < width_all:
                    gap = jnp.zeros((near.shape[0], width_all - near.shape[1]), F32)
                    near = jnp.concatenate([near, gap], axis=1)
                put(near, slice(cols, cols + extra))

    out = shape(n_new, part, cols + extra)
    out_spec = pl.BlockSpec(out.shape, lambda i, f: (0, 0, 0))
    grid_spec = pltpu.PrefetchScalarGridSpec(
        num_scalar_prefetch=1,
        grid=(steps,),
        in_specs=[pl.BlockSpec((rows, step), lambda i, f: (0, half * steps + i))]
        + [pl.BlockSpec(x.shape, lambda i, f: (0, 0)) for x in arrays]
        + [pl.BlockSpec(memory_space=pl.ANY)],
        out_specs=(out_spec, out_spec),
        scratch_shapes=[pltpu.VMEM((len(blocks) * width, rows), BF16)],
    )
    return kernel_call(
        body,
        (out, out),
        2 * rows * n_new * width * (cols + extra),
        2 * rows * cols + 4 * rows * len(blocks) * width + 8 * n_new * part * (cols + extra),
        grid_spec=grid_spec,
    )(flags, counts, *arrays, token)


def line_slot(flags, t, chunks, own, got, token):
    line = lax.axis_size("bin") // 2
    right = [z for z in range(line - 1) if 0 <= t - z < chunks]
    left = [line - 1 - z for z in right]
    merged = not set(right) & set(left) and not {z + 1 for z in right} & {z - 1 for z in left}
    need = sorted({t - z for z in right})
    _, part, cols = own[need[0]][0].shape

    def body(flag_ref, *refs):
        z = flag_ref[2]
        come = dict(zip(("right", "left"), refs[2 * len(need) :]))
        outs = refs[-1:] * 2 if merged else refs[-2:]
        for name, active, out in (("right", right, outs[0]), ("left", left, outs[1])):
            for place in active:
                c = t - (place if name == "right" else line - 1 - place)
                a, b = refs[2 * need.index(c)], refs[2 * need.index(c) + 1]

                @pl.when(z == place)
                def _():
                    value = a[0] + b[0]
                    if c != t:
                        value = value + come[name][...]
                    out[...] = value

    block = lambda i: pl.BlockSpec((1, part, cols), lambda g, f: (i, 0, 0))
    flat = pl.BlockSpec((part, cols), lambda g, f: (0, 0))
    operands, specs = [], []
    for c in need:
        keep, came, i = own[c]
        operands += [keep, came]
        specs += [block(i)] * 2
    if got is not None:
        operands += list(got)
        specs += [flat] * 2
    operands.append(token)
    specs.append(pl.BlockSpec(memory_space=pl.ANY))
    n_out = 1 if merged else 2
    sends = kernel_call(
        body,
        (shape(part, cols),) * n_out,
        0,
        4 * part * cols * (len(operands) + n_out),
        grid_spec=pltpu.PrefetchScalarGridSpec(
            num_scalar_prefetch=1, grid=(1,), in_specs=specs, out_specs=(flat,) * n_out
        ),
    )(flags, *operands)
    pairs = lambda hops: [(2 * a + c, 2 * b + c) for a, b in hops for c in range(2)]
    to_right = pairs([(z, z + 1) for z in right])
    to_left = pairs([(z, z - 1) for z in left])
    if merged:
        come = lax.ppermute(sends[0], "bin", to_right + to_left)
        return (come, come), sends[0]
    return (lax.ppermute(sends[0], "bin", to_right), lax.ppermute(sends[1], "bin", to_left)), sends[1]


def line_total(flags, own, come, token):
    line = lax.axis_size("bin") // 2
    keep, came, index = own
    _, part, cols = keep.shape

    def body(flag_ref, a, b, *refs):
        out = refs[-1]
        z = flag_ref[2]
        out[...] = a[0] + b[0]
        for d in range(line - 1):

            @pl.when(z == d + 1)
            def _():
                out[...] += refs[2 * d][...]

            @pl.when(z == line - 2 - d)
            def _():
                out[...] += refs[2 * d + 1][...]

    block = pl.BlockSpec((1, part, cols), lambda g, f: (index, 0, 0))
    flat = pl.BlockSpec((part, cols), lambda g, f: (0, 0))
    operands = [keep, came] + [x for pair in come for x in pair] + [token]
    return kernel_call(
        body,
        shape(part, cols),
        0,
        4 * part * cols * len(operands),
        grid_spec=pltpu.PrefetchScalarGridSpec(
            num_scalar_prefetch=1,
            grid=(1,),
            in_specs=[block] * 2
            + [flat] * (2 * len(come))
            + [pl.BlockSpec(memory_space=pl.ANY)],
            out_specs=flat,
        ),
    )(flags, *operands)


def shares(loadings, totals, ids, flags, cols):
    width_all, genes = loadings.shape
    width = width_all // len(ids)
    part = width // 2
    extra = width_all
    steps = 6
    step = genes // steps

    def body(flag_ref, load_ref, *refs):
        out_ref, gram, load = refs[-3:]
        me, core = flag_ref[0], flag_ref[1]
        firsts = [pl.multiple_of((k ^ me) * width, width) for k in ids]

        @pl.when(pl.program_id(0) == 0)
        def _():
            for j in range(len(ids)):
                for ref, which in ((refs[2 * j], core), (refs[2 * j + 1], 1 - core)):
                    at = pl.multiple_of(j * width + which * part, part)
                    gram[pl.ds(at, part), :] = ref[...]
            low = gram[...]
            row = lax.broadcasted_iota(jnp.int32, low.shape, 0) // width
            col = lax.broadcasted_iota(jnp.int32, low.shape, 1) // width
            gram[...] = jnp.where(col <= row, low, low.T)

        for j, first in enumerate(firsts):
            load[j * width : (j + 1) * width, :] = load_ref[pl.ds(first, width), :]
        value = load[...]
        value = value / dot(gram[...], value, PLAIN, lax.Precision.HIGHEST)
        for j, first in enumerate(firsts):
            out_ref[pl.ds(first, width), :] = value[j * width : (j + 1) * width]

    gram_spec = pl.BlockSpec((part, extra), lambda i, f: (0, 0))
    block = pl.BlockSpec((width_all, step), lambda i, f: (0, i))
    pieces = [x[:, cols:] for pair in totals for x in pair]
    return kernel_call(
        body,
        shape(width_all, genes),
        12 * width_all * width_all * genes,
        8 * width_all * genes,
        grid_spec=pltpu.PrefetchScalarGridSpec(
            num_scalar_prefetch=1,
            grid=(steps,),
            in_specs=[block] + [gram_spec] * len(pieces),
            out_specs=block,
            scratch_shapes=[
                pltpu.VMEM((width_all, width_all), F32),
                pltpu.VMEM((width_all, step), F32),
            ],
        ),
    )(flags, loadings, *pieces)


def new_loadings(share, mine, other, k, half, width, flags, before):
    width_all, genes = share.shape
    cols = genes // HALVES
    part = width // 2

    def body(flag_ref, share_ref, mine_ref, other_ref, *rest):
        out_ref = rest[-1]
        for ref, which in ((mine_ref, flag_ref[1]), (other_ref, 1 - flag_ref[1])):
            at = pl.ds(pl.multiple_of(which * part, part), part)
            out_ref[at, :] = share_ref[at, :] * ref[...]

    rows_at = pl.BlockSpec((width, cols), lambda i, f: (k ^ f[0], half))
    flat = pl.BlockSpec((part, cols), lambda i, f: (0, 0))
    operands, specs, aliases = [flags, share, mine, other], [rows_at, flat, flat], {}
    if before is not None:
        operands.append(before)
        specs.append(pl.BlockSpec(memory_space=pl.ANY))
        aliases = {len(operands) - 1: 0}
    return kernel_call(
        body,
        shape(width_all, genes),
        0,
        16 * width * cols,
        grid_spec=pltpu.PrefetchScalarGridSpec(
            num_scalar_prefetch=1, grid=(1,), in_specs=specs, out_specs=rows_at
        ),
        input_output_aliases=aliases,
    )(*operands)


def on_device(counts, factors, loadings, position, edge_codes):
    bins, genes_n = lax.axis_size("bin"), lax.axis_size("gene")
    line = bins // 2
    me, bin_me = lax.axis_index("gene"), lax.axis_index("bin")
    rows, width_all = factors.shape
    genes = counts.shape[1]
    width = width_all // genes_n
    scalar = lambda x: jnp.asarray(x, jnp.int32).reshape(1)
    me1, bin1 = scalar(me), scalar(bin_me)
    flags = jnp.concatenate([me1, bin1 % 2, bin1 // 2])
    bits = [1 << b for b in range(genes_n.bit_length() - 1)]
    orders = (bits, bits[::-1])

    payload = pack(factors, position, me1, width, bins)
    got = lax.all_to_all(payload, "bin", split_axis=0, concat_axis=0, tiled=True)

    numer, load = [None, None], loadings
    for half in (1, 0):
        bit = orders[half][0]
        send_ids = [k for k in range(genes_n) if k & bit]
        keep_ids = [k for k in range(genes_n) if not k & bit]
        send, keep, *more = numer_part(counts, load, me1, genes_n, half, send_ids, half == 0)
        load = more[0] if more else load
        numer[half] = scatter_sum(send, keep, keep_ids, orders[half])

    grid, first, last, cell = to_grid(got, edge_codes, bin1)
    above = lax.ppermute(last, "bin", [(i, i + 1) for i in range(bins - 1)])
    below = lax.ppermute(first, "bin", [(i + 1, i) for i in range(bins - 1)])
    smooth = from_grid(grid, above, below, cell, edge_codes, bins)
    back = lax.all_to_all(smooth, "bin", split_axis=0, concat_axis=0, tiled=True)
    numer_own, plain = plain_terms(numer, factors, rows, width)
    own_block = new_factors(payload, back, numer_own, plain)

    ids = sorted(range(genes_n), key=lambda k: (bin(k).count("1"), k))
    groups = [[k for k in ids if bin(k).count("1") == n] for n in range(len(bits) + 1)]
    blocks = {0: (own_block,)}
    for k in bits:
        blocks[k] = (swap(own_block, "gene", k),)

    def come_on(group, token):
        for k in group:
            low, high = k & -k, 1 << (k.bit_length() - 1)
            pick = lambda b, h: (b[0], h) if len(b) == 1 else (b[h], None)
            sources = [pick(blocks[k ^ low], 0), pick(blocks[k ^ high], 1)]
            if sources[0][1] is not None:
                outs = halves_out(sources, token)
            else:
                outs = [s for s, _ in sources]
            blocks[k] = (swap(outs[0], "gene", low), swap(outs[1], "gene", high))
            token = outs[0]
        return token

    cols = genes // HALVES
    chunks = len(ids)
    own = [{} for _ in range(HALVES)]
    came = [[] for _ in range(HALVES)]
    totals = [{} for _ in range(HALVES)]
    token = own_block
    factors_new = None

    def product(group, half, token):
        upto = ids.index(group[-1]) + 1
        n_old = upto - len(group)
        send, keep = cross_part(
            [blocks[k] for k in ids[:upto]], n_old, counts, flags, half, half == 0, width_all, token
        )
        other = swap(send, "bin", 1)
        for i in range(len(group)):
            own[half][n_old + i] = (keep, other, i)
        return keep

    def finish(c, half, token):
        total = line_total(flags, own[half][c], came[half][c : c + line - 1], token)
        totals[half][c] = (total, swap(total, "bin", 1))
        return total

    for t in range(chunks + line - 2):
        for half in range(HALVES):
            if t < chunks and t not in own[half]:
                if t == 0 and half == 0:
                    for h in range(HALVES):
                        token = product(groups[0], h, token)
                else:
                    token = product(next(g for g in groups if ids[t] in g), half, token)
            sends, token = line_slot(
                flags, t, chunks, own[half], came[half][-1] if came[half] else None, token
            )
            came[half].append(sends)
        if t + 2 < len(groups):
            token = come_on(groups[t + 2], token)
        if t == chunks - 1:
            factors_new = turned_back([blocks[k] for k in ids], ids, width, me1, token)
            token = factors_new
        for half in range(HALVES):
            c = t - (line - 1)
            if 0 <= c < chunks:
                token = finish(c, half, token)
    for c in range(chunks):
        for half in range(HALVES):
            if c not in totals[half]:
                token = finish(c, half, token)
    share = shares(loadings, [totals[0][c] for c in range(chunks)], ids, flags, cols)
    loadings_new = None
    for c, k in enumerate(ids):
        for half in range(HALVES):
            mine, other = totals[half][c]
            loadings_new = new_loadings(share, mine, other, k, half, width, flags, loadings_new)
    return factors_new, loadings_new


def solution(mesh):
    placed = (P("bin", "gene"), P("bin", None), P(None, "gene"), P("bin"), P("bin", None))
    return jax.shard_map(
        on_device,
        mesh=mesh,
        in_specs=placed,
        out_specs=(P("bin", None), P(None, "gene")),
        check_vma=False,
    )
```

```python
import jax
import jax.numpy as jnp
from jax import lax
from jax.experimental import pallas as pl
from jax.experimental.pallas import tpu as pltpu
from jax.sharding import PartitionSpec as P

K = 256
G = 18432
PENALTY = float(G * K) / 64.0
EXTRA = 8
HALVES = 2
MIB = 1024 * 1024
MINOR = (((1,), (1,)), ((), ()))
PLAIN = (((1,), (0,)), ((), ()))
F32 = jnp.float32
BF16 = jnp.bfloat16
ANY_SPEC = pl.BlockSpec(memory_space=pl.ANY)
VMEM_SPEC = pl.BlockSpec(memory_space=pltpu.VMEM)
SMEM_SPEC = pl.BlockSpec(memory_space=pltpu.SMEM)


def dot(a, b, dims, precision=None):
    return lax.dot_general(a, b, dims, precision=precision, preferred_element_type=F32)


def kernel_call(body, out_shape, us, limit=10, **kw):
    return pl.pallas_call(
        body,
        out_shape=out_shape,
        compiler_params=pltpu.CompilerParams(vmem_limit_bytes=limit * MIB),
        cost_estimate=pl.CostEstimate(flops=0, bytes_accessed=int(us * 3.69e6), transcendentals=0),
        **kw,
    )


def shape(*dims, dtype=F32):
    return jax.ShapeDtypeStruct(dims, dtype)


def pack(factors, position, me, width, bins):
    rows, width_all = factors.shape
    group = rows // bins
    lanes = 128 if width_all % 128 == 0 and 128 % width == 0 else width_all

    def body(me_ref, fac_ref, pos_ref, out_ref, turned):
        turned[...] = fac_ref[...].T
        first = pl.multiple_of(lax.rem(me_ref[0] * width, lanes), width)
        out_ref[0, :width, :] = turned[pl.ds(first, width), :]
        out_ref[0, width:, :] = jnp.broadcast_to(pos_ref[0], (EXTRA, group))

    grid_spec = pltpu.PrefetchScalarGridSpec(
        num_scalar_prefetch=1,
        grid=(bins,),
        in_specs=[
            pl.BlockSpec((group, lanes), lambda t, m: (t, m[0] * width // lanes)),
            pl.BlockSpec((1, 1, group), lambda t, m: (t, 0, 0)),
        ],
        out_specs=pl.BlockSpec((1, width + EXTRA, group), lambda t, m: (t, 0, 0)),
        scratch_shapes=[pltpu.VMEM((lanes, group), F32)],
    )
    return kernel_call(
        body, shape(bins, width + EXTRA, group), 3, grid_spec=grid_spec
    )(me, factors, position.astype(F32).reshape(bins, 1, group))


def to_grid(got, edge_codes, bin_me, token):
    bins, wide, group = got.shape
    width = wide - EXTRA
    grid_rows, grid_cols = edge_codes.shape
    rows = bins * group
    per = 4

    def body(me_ref, got_ref, code_ref, _, grid_ref, first_ref, last_ref, cell_ref, masked):
        block = jnp.concatenate([got_ref[s] for s in range(bins)], axis=1)
        cell = block[width : width + 1].astype(jnp.int32) - me_ref[0] * rows
        cell_ref[...] = cell
        at_row, at_col = cell // grid_cols, cell % grid_cols
        col_hot = jnp.where(
            lax.broadcasted_iota(jnp.int32, (grid_cols, rows), 0) == at_col, 1.0, 0.0
        ).astype(BF16)
        values = block[:width]
        high = values.astype(BF16)
        both = jnp.concatenate([high, (values - high.astype(F32)).astype(BF16)], axis=0)
        scale = code_ref[...].astype(F32) / 8.0
        for r in range(grid_rows):
            at = r % per * 2 * width
            if at == 0:
                for i in range(per):
                    mask = jnp.where(at_row == r + i, 1.0, 0.0).astype(BF16)
                    masked[i * 2 * width : (i + 1) * 2 * width, :] = both * mask
                placed = dot(masked[...], col_hot, MINOR)
            line = placed[at : at + width] + placed[at + width : at + 2 * width]
            row_scale = scale[r : r + 1]
            weighted = jnp.concatenate(
                [line * row_scale, jnp.broadcast_to(row_scale, (EXTRA, grid_cols))], axis=0
            )
            grid_ref[r] = weighted
            if r == 0:
                first_ref[...] = weighted
            if r == grid_rows - 1:
                last_ref[...] = weighted

    return kernel_call(
        body,
        (
            shape(grid_rows, wide, grid_cols),
            shape(wide, grid_cols),
            shape(wide, grid_cols),
            shape(1, rows, dtype=jnp.int32),
        ),
        3,
        limit=12,
        in_specs=[SMEM_SPEC, VMEM_SPEC, VMEM_SPEC, ANY_SPEC],
        out_specs=(VMEM_SPEC,) * 4,
        scratch_shapes=[pltpu.VMEM((per * 2 * width, rows), BF16)],
    )(bin_me, got, edge_codes, token)


def from_grid(grid, above, below, cell, edge_codes, bins, token):
    grid_rows, wide, grid_cols = grid.shape
    rows = cell.shape[1]
    group = rows // bins

    def body(grid_ref, above_ref, below_ref, cell_ref, code_ref, _, out_ref, halves):
        scale = code_ref[...].astype(F32) / 8.0
        lane = lax.broadcasted_iota(jnp.int32, (wide, grid_cols), 1)
        for r in range(grid_rows):
            here = grid_ref[r]
            upper = above_ref[...] if r == 0 else grid_ref[r - 1]
            lower = below_ref[...] if r == grid_rows - 1 else grid_ref[r + 1]
            left = jnp.where(lane == 0, 0.0, pltpu.roll(here, 1, 1))
            right = jnp.where(lane == grid_cols - 1, 0.0, pltpu.roll(here, grid_cols - 1, 1))
            value = scale[r : r + 1] * (left + right + 0.5 * (upper + lower))
            high = value.astype(BF16)
            halves[r * wide : (r + 1) * wide, :grid_cols] = high
            halves[r * wide : (r + 1) * wide, grid_cols:] = (value - high.astype(F32)).astype(BF16)
        cell = cell_ref[...]
        at_row, at_col = cell // grid_cols, cell % grid_cols
        for s in range(bins // 2):
            lo, hi = 2 * s * group, (2 * s + 2) * group
            hot = jnp.where(
                lax.broadcasted_iota(jnp.int32, (grid_cols, hi - lo), 0) == at_col[:, lo:hi], 1.0, 0.0
            ).astype(BF16)
            lines = dot(halves[...], jnp.concatenate([hot, hot], axis=0), PLAIN)
            row_here = at_row[:, lo:hi]
            total = jnp.zeros((wide, hi - lo), F32)
            for r in range(grid_rows):
                total = total + jnp.where(row_here == r, lines[r * wide : (r + 1) * wide], 0.0)
            out_ref[2 * s] = total[:, :group]
            out_ref[2 * s + 1] = total[:, group:]

    return kernel_call(
        body,
        shape(bins, wide, group),
        4,
        in_specs=[VMEM_SPEC] * 5 + [ANY_SPEC],
        out_specs=VMEM_SPEC,
        scratch_shapes=[pltpu.VMEM((grid_rows * wide, 2 * grid_cols), BF16)],
    )(grid, above, below, cell, edge_codes, token)


def numer_part(counts, loadings, me, genes_n, half, send_ids, with_gram, token):
    rows, genes = counts.shape
    width_all = loadings.shape[0]
    width = width_all // genes_n
    step = 256
    half_rows = rows // 2
    steps = half_rows // step
    keep_ids = [k for k in range(genes_n) if k not in send_ids]
    total_cols = half_rows + with_gram * width_all
    first_call = loadings.dtype == F32

    def body(me_ref, counts_ref, load_ref, _, send_ref, keep_ref, held, *rest):
        firsts = [pl.multiple_of((k ^ me_ref[0]) * width, width) for k in range(genes_n)]
        sems = rest[-1]
        copies = [
            pltpu.make_async_copy(
                counts_ref.at[pl.ds(half * half_rows + i * step, step), :],
                held.at[pl.ds(i * step, step), :],
                sems.at[i],
            )
            for i in range(steps)
        ]
        if first_call:
            load_bf, blocks = rest[0], rest[1]
            reads = [
                pltpu.make_async_copy(
                    load_ref.at[pl.ds(first, width), :],
                    blocks.at[pl.ds(k * width, width), :],
                    sems.at[steps + k],
                )
                for k, first in enumerate(firsts)
            ]
            for copy in reads + copies:
                copy.start()
            for k, copy in enumerate(reads):
                copy.wait()
                load_bf[k * width : (k + 1) * width, :] = blocks[k * width : (k + 1) * width, :].astype(BF16)
        else:
            load_bf = load_ref
            for copy in copies:
                copy.start()

        def put(part, cols):
            for i, k in enumerate(send_ids):
                send_ref[i, :, cols] = part[k * width : (k + 1) * width]
            for i, k in enumerate(keep_ids):
                keep_ref[i, :, cols] = part[k * width : (k + 1) * width]

        if with_gram:
            turned = rest[0]
            local = dot(load_bf[...], load_bf[...], MINOR)
            for k, first in enumerate(firsts):
                turned[pl.ds(first, width), :] = local[k * width : (k + 1) * width]
            put(turned[...].T, slice(half_rows, total_cols))
        for i, copy in enumerate(copies):
            copy.wait()
            at = slice(i * step, (i + 1) * step)
            put(dot(held[at, :], load_bf[...], MINOR).T, at)

    out = shape(genes_n // 2, width, total_cols)
    outs = (out, out, pltpu.VMEM((half_rows, genes), BF16))
    scratch = []
    if first_call:
        outs += (pltpu.VMEM((width_all, genes), BF16),)
        scratch.append(pltpu.VMEM((width_all, genes), F32))
    if with_gram:
        scratch.append(pltpu.VMEM((width_all, width_all), F32))
    scratch.append(pltpu.SemaphoreType.DMA((steps + genes_n,)))
    return kernel_call(
        body,
        outs,
        7,
        limit=12,
        in_specs=[SMEM_SPEC, ANY_SPEC, ANY_SPEC if first_call else VMEM_SPEC, ANY_SPEC],
        out_specs=(VMEM_SPEC,) * len(outs),
        scratch_shapes=scratch,
    )(me, counts, loadings, token)


def swap(block, axis, bit):
    return lax.ppermute(block, axis, [(i, i ^ bit) for i in range(lax.axis_size(axis))])


def picked_sum(arrays, ids, token):
    _, width, cols = arrays[0].shape

    def body(*refs):
        for j, i in enumerate(ids):
            total = refs[0][i]
            for ref in refs[1:-2]:
                total = total + ref[i]
            refs[-1][j] = total

    return kernel_call(
        body,
        shape(len(ids), width, cols),
        1,
        in_specs=[VMEM_SPEC] * len(arrays) + [ANY_SPEC],
        out_specs=VMEM_SPEC,
    )(*arrays, token)


def plain_terms(first, second, factors, width, token):
    rows, width_all = factors.shape
    half_rows = rows // 2

    def body(*refs):
        parts = refs[: len(first)]
        second_ref, fac_ref, _, numer_ref, plain_ref, gram = refs[len(first) :]
        at = pl.program_id(0)

        def total(cols):
            out = parts[0][0, :, cols]
            for ref in parts[1:]:
                out = out + ref[0, :, cols]
            return out

        @pl.when(at == 0)
        def _():
            gram[...] = total(slice(half_rows, half_rows + width_all))
            numer_ref[...] = total(slice(0, half_rows))

        @pl.when(at == 1)
        def _():
            numer_ref[...] = second_ref[0]

        plain_ref[...] = dot(fac_ref[...], gram[...], MINOR, lax.Precision.HIGHEST).T

    out_spec = pl.BlockSpec((width, half_rows), lambda i: (0, i))
    return kernel_call(
        body,
        (shape(width, rows),) * 2,
        4,
        grid=(2,),
        in_specs=[VMEM_SPEC] * (len(first) + 1)
        + [pl.BlockSpec((half_rows, width_all), lambda i: (i, 0)), ANY_SPEC],
        out_specs=(out_spec, out_spec),
        scratch_shapes=[pltpu.VMEM((width, width_all), F32)],
    )(*first, second, factors, token)


def new_factors(payload, back, numer, plain):
    bins, wide, group = payload.shape
    width = wide - EXTRA

    def body(pay_ref, back_ref, numer_ref, plain_ref, out_ref):
        pay = jnp.concatenate([pay_ref[s] for s in range(bins)], axis=1)
        got = jnp.concatenate([back_ref[s] for s in range(bins)], axis=1)
        fac, smooth, degree = pay[:width], got[:width], got[width : width + 1]
        out_ref[...] = (
            fac * (numer_ref[...] + PENALTY * smooth) / (plain_ref[...] + PENALTY * degree * fac)
        )

    return kernel_call(
        body,
        shape(width, bins * group),
        0.02,
        in_specs=[VMEM_SPEC] * 4,
        out_specs=VMEM_SPEC,
    )(payload, back, numer, plain)


def sent_on(blocks, token):
    n = len(blocks)

    def body(*refs):
        for src, dst in zip(refs[:n], refs[n + 1 :]):
            dst[...] = src[...]

    return kernel_call(
        body,
        tuple(shape(*b.shape) for b in blocks),
        0.02,
        in_specs=[VMEM_SPEC] * n + [ANY_SPEC],
        out_specs=(VMEM_SPEC,) * n,
    )(*blocks, token)


def turned_back(blocks, ids, width, me, token):
    rows = blocks[0].shape[1]
    width_all = len(ids) * width
    step = 384
    steps = rows // step

    def body(me_ref, *refs):
        out_ref, _, block = refs[-3:]
        for ref, k in zip(refs, ids):
            block[pl.ds(pl.multiple_of((k ^ me_ref[0]) * width, width), width), :] = ref[...]
        out_ref[...] = block[...].T

    grid_spec = pltpu.PrefetchScalarGridSpec(
        num_scalar_prefetch=1,
        grid=(steps,),
        in_specs=[pl.BlockSpec((width, step), lambda i, m: (0, i))] * len(ids) + [ANY_SPEC],
        out_specs=(pl.BlockSpec((step, width_all), lambda i, m: (i, 0)), VMEM_SPEC),
        scratch_shapes=[pltpu.VMEM((width_all, step), F32)],
    )
    outs = (pltpu.HBM((rows, width_all), F32), shape(8, 128))
    return kernel_call(body, outs, 0.02, limit=8, grid_spec=grid_spec)(me, *blocks, token)


def put_rounded(fac, refs, width):
    for j, ref in enumerate(refs):
        fac[j * width : (j + 1) * width, :] = ref[...].astype(BF16)


def cross_part(blocks, held, half, tokens):
    width = blocks[0].shape[0]
    half_rows, genes = held[0].shape
    cols = genes // HALVES
    steps = 3
    step = cols // steps
    n = len(blocks)

    def body(top_ref, low_ref, *refs):
        out_ref, fac = refs[-2:]
        put_rounded(fac, refs[:n], width)
        for i in range(steps):
            at = slice(half * cols + i * step, half * cols + (i + 1) * step)
            part = dot(fac[:, :half_rows], top_ref[:, at], PLAIN)
            part = part + dot(fac[:, half_rows:], low_ref[:, at], PLAIN)
            for j in range(n):
                out_ref[j, :, i * step : (i + 1) * step] = part[j * width : (j + 1) * width]

    return kernel_call(
        body,
        shape(n, width, cols),
        0.02,
        limit=6,
        in_specs=[VMEM_SPEC] * (2 + n) + [ANY_SPEC] * len(tokens),
        out_specs=VMEM_SPEC,
        scratch_shapes=[pltpu.VMEM((n * width, 2 * half_rows), BF16)],
    )(*held, *blocks, *tokens)


def gram_part(blocks, token):
    width, rows = blocks[0].shape
    width_all = len(blocks) * width

    def body(*refs):
        out_ref, fac = refs[-2:]
        put_rounded(fac, refs[: len(blocks)], width)
        out_ref[0] = dot(fac[...], fac[...], MINOR)

    return kernel_call(
        body,
        shape(1, width_all, width_all),
        0.02,
        limit=8,
        in_specs=[VMEM_SPEC] * len(blocks) + [ANY_SPEC],
        out_specs=VMEM_SPEC,
        scratch_shapes=[pltpu.VMEM((width_all, rows), BF16)],
    )(*blocks, token)


def both_cores(part, came, token):
    def body(a, b, _, out):
        out[...] = a[...] + b[...]

    return kernel_call(
        body,
        shape(*part.shape),
        0.02,
        in_specs=[VMEM_SPEC, VMEM_SPEC, ANY_SPEC],
        out_specs=VMEM_SPEC,
    )(part, came, token)


def line_slot(flags, t, chunks, own, come, token):
    line = lax.axis_size("bin") // 2
    places = [q for q in range(line - 1) if 0 <= t - q < chunks]
    hops = [(2 * q, 2 * q + 2) for q in places]
    hops += [(2 * (line - 1 - q) + 1, 2 * (line - 2 - q) + 1) for q in places]
    _, width, cols = own[t - places[0]][0].shape
    if t == 0:
        return lax.ppermute(own[0][0].reshape(width, cols), "bin", hops), token
    arrays = [own[t - q][0] for q in places]

    def body(flag_ref, come_ref, _, *refs):
        for i, q in enumerate(places):

            @pl.when(flag_ref[2] == q)
            def _():
                value = refs[i][own[t - q][1]]
                refs[-1][...] = value if q == 0 else value + come_ref[...]

    send = kernel_call(
        body,
        shape(width, cols),
        0.02,
        in_specs=[SMEM_SPEC, VMEM_SPEC, ANY_SPEC] + [VMEM_SPEC] * len(arrays),
        out_specs=VMEM_SPEC,
    )(flags, come, token, *arrays)
    return lax.ppermute(send, "bin", hops), send


def line_end(flags, come, token):
    def body(flag_ref, _, *refs):
        out = refs[-1]

        @pl.when(flag_ref[2] == 0)
        def _():
            out[...] = jnp.zeros(out.shape, F32)

        for d in range(len(come)):

            @pl.when(flag_ref[2] == d + 1)
            def _():
                out[...] = refs[d][...]

    end = kernel_call(
        body,
        shape(*come[0].shape),
        0.02,
        in_specs=[SMEM_SPEC, ANY_SPEC] + [VMEM_SPEC] * len(come),
        out_specs=VMEM_SPEC,
    )(flags, token, *come)
    return end, swap(end, "bin", 1)


def shares(loadings, gram, ids, me, token):
    width_all, genes = loadings.shape
    width = width_all // len(ids)
    steps = 6
    step = genes // steps

    def body(me_ref, load_ref, own_ref, end_ref, other_ref, _, out_ref, tiny, load, gram):

        @pl.when(pl.program_id(0) == 0)
        def _():
            gram[...] = own_ref[0] + (end_ref[...] + other_ref[...])

        firsts = [pl.multiple_of((k ^ me_ref[0]) * width, width) for k in ids]
        for j, first in enumerate(firsts):
            load[j * width : (j + 1) * width, :] = load_ref[pl.ds(first, width), :]
        value = load[...]
        value = value / dot(gram[...], value, PLAIN, lax.Precision.HIGHEST)
        for j, first in enumerate(firsts):
            out_ref[pl.ds(first, width), :] = value[j * width : (j + 1) * width]

    block = pl.BlockSpec((width_all, step), lambda i, f: (0, i))
    return kernel_call(
        body,
        (shape(width_all, genes), shape(8, 128)),
        0.02,
        limit=12,
        grid_spec=pltpu.PrefetchScalarGridSpec(
            num_scalar_prefetch=1,
            grid=(steps,),
            in_specs=[block] + [VMEM_SPEC] * 3 + [ANY_SPEC],
            out_specs=(block, VMEM_SPEC),
            scratch_shapes=[
                pltpu.VMEM((width_all, step), F32),
                pltpu.VMEM((width_all, width_all), F32),
            ],
        ),
    )(me, loadings, *gram, token)


def new_loadings(share, parts, k, width, me, before, token):
    width_all, genes = share.shape
    halves = sorted(parts)
    cols = genes // HALVES
    arrays = [x for h in halves for x in (parts[h][0][0],) + parts[h][1:]]

    def body(me_ref, share_ref, _, *refs):
        out_ref = refs[-2]
        at = pl.ds(pl.multiple_of((k ^ me_ref[0]) * width, width), width)
        for i, h in enumerate(halves):
            own, end, other = refs[3 * i : 3 * i + 3]
            here = slice(h * cols, (h + 1) * cols)
            total = own[parts[h][0][1]] + (end[...] + other[...])
            out_ref[:, i * cols : (i + 1) * cols] = share_ref[at, here] * total

    operands = [me, share, token] + arrays
    specs = [VMEM_SPEC, ANY_SPEC] + [VMEM_SPEC] * len(arrays)
    aliases = {}
    if before is not None:
        operands.append(before)
        specs.append(ANY_SPEC)
        aliases = {len(operands) - 1: 0}
    column = 0 if len(halves) == HALVES else halves[0]
    return kernel_call(
        body,
        (pltpu.HBM((width_all, genes), F32), shape(8, 128)),
        0.02,
        limit=6,
        grid_spec=pltpu.PrefetchScalarGridSpec(
            num_scalar_prefetch=1,
            grid=(1,),
            in_specs=specs,
            out_specs=(
                pl.BlockSpec((width, len(halves) * cols), lambda i, m: (k ^ m[0], column)),
                VMEM_SPEC,
            ),
        ),
        input_output_aliases=aliases,
    )(*operands)


def on_device(counts, factors, loadings, position, edge_codes):
    bins, genes_n = lax.axis_size("bin"), lax.axis_size("gene")
    line = bins // 2
    me, bin_me = lax.axis_index("gene"), lax.axis_index("bin")
    rows, width_all = factors.shape
    width = width_all // genes_n
    scalar = lambda x: jnp.asarray(x, jnp.int32).reshape(1)
    me1, bin1 = scalar(me), scalar(bin_me)
    core, chip = bin1 & 1, bin1 >> 1
    flags = jnp.concatenate([me1, core, jnp.where(core == 0, chip, line - 1 - chip)])
    bits = [1 << b for b in range(genes_n.bit_length() - 1)]
    orders = (bits, bits[::-1])

    payload = pack(pltpu.with_memory_space_constraint(factors, pltpu.HBM), position, me1, width, bins)
    got = lax.all_to_all(payload, "bin", split_axis=0, concat_axis=0, tiled=True)

    counts = pltpu.with_memory_space_constraint(counts, pltpu.HBM)
    token, load = payload, pltpu.with_memory_space_constraint(loadings, pltpu.HBM)
    held, parts, keeps = [None, None], [None, None], [None, None]
    for half in (1, 0):
        bit = orders[half][0]
        send_ids = [k for k in range(genes_n) if k & bit]
        keeps[half] = [k for k in range(genes_n) if not k & bit]
        send, keep, held[half], *more = numer_part(
            counts, load, me1, genes_n, half, send_ids, half == 0, token
        )
        load = more[0] if more else load
        token = keep
        parts[half] = [keep, swap(send, "gene", bit)]

    def scatter_more(half, bit, token):
        out_ids = [i for i, k in enumerate(keeps[half]) if k & bit]
        in_ids = [i for i, k in enumerate(keeps[half]) if not k & bit]
        keeps[half] = [keeps[half][i] for i in in_ids]
        send = picked_sum(parts[half], out_ids, token)
        if len(in_ids) > 1:
            parts[half] = [picked_sum(parts[half], in_ids, send)]
        parts[half] = parts[half] + [swap(send, "gene", bit)]
        return send

    grid, first, last, cell = to_grid(got, edge_codes, bin1, token)
    above = lax.ppermute(last, "bin", [(i, i + 1) for i in range(bins - 1)])
    below = lax.ppermute(first, "bin", [(i + 1, i) for i in range(bins - 1)])
    token = scatter_more(1, orders[1][1], grid)
    smooth = from_grid(grid, above, below, cell, edge_codes, bins, token)
    back = lax.all_to_all(smooth, "bin", split_axis=0, concat_axis=0, tiled=True)
    token = scatter_more(0, orders[0][1], smooth)
    for i in range(2, len(bits)):
        for half in (1, 0):
            token = scatter_more(half, orders[half][i], token)
    second = picked_sum(parts[1], [0], token)
    numer, plain = plain_terms(parts[0], second, factors, width, second)
    own_block = new_factors(payload, back, numer, plain)

    ids = sorted(range(genes_n), key=lambda k: (bin(k).count("1"), k))
    groups = [[k for k in ids if bin(k).count("1") == n] for n in range(len(bits) + 1)]
    chunks = len(ids)
    blocks = {0: own_block}
    for k in bits:
        blocks[k] = swap(own_block, "gene", k)

    def come_on(group, token):
        outs = sent_on([blocks[k & (k - 1)] for k in group], token)
        for k, out in zip(group, outs):
            blocks[k] = swap(out, "gene", k & -k)
        return outs[-1]

    pending = [[None] * len(groups) for _ in range(HALVES)]
    own = [{} for _ in range(HALVES)]
    come = [[] for _ in range(HALVES)]
    ends = [{} for _ in range(HALVES)]

    def product(g, half, *tokens):
        part = cross_part([blocks[k] for k in groups[g]], held, half, tokens)
        pending[half][g] = (part, swap(part, "bin", 1))
        return part

    def own_chunks(g, half, token):
        array = both_cores(*pending[half][g], token)
        for i, k in enumerate(groups[g]):
            own[half][ids.index(k)] = (array, i)
        return array

    def slot(half, t, token):
        before = come[half][-1] if come[half] else None
        got, token = line_slot(flags, t, chunks, own[half], before, token)
        come[half].append(got)
        return token

    def end(c, half, token):
        ends[half][c] = line_end(flags, come[half][c : c + line - 1], token)
        return ends[half][c][0]

    def final(c, before, token, halves=range(HALVES)):
        sums = {h: (own[h][c],) + ends[h][c] for h in halves}
        return new_loadings(share, sums, ids[c], width, me1, before, token)

    def both(step, *args):
        nonlocal token
        for half in range(HALVES):
            token = step(*args, half, token)

    token = own_block
    both(product, 0)
    for half in range(HALVES):
        token = own_chunks(0, half, token)
        token = slot(half, 0, token)
    factors_new = share = loadings_new = None
    firsts = {ids.index(group[0]): g for g, group in enumerate(groups)}
    last_slot = chunks + line - 3
    done = 0
    for t in range(1, last_slot + 1):
        if t == 1:
            if len(groups) > 2:
                token = come_on(groups[2], token)
            for half in range(HALVES):
                token = product(1, half, token, come[0][0], come[1][0])
        for half in range(HALVES):
            if t in firsts:
                token = own_chunks(firsts[t], half, token)
            token = slot(half, t, token)
        g = firsts.get(t + 2, 0)
        if g > 1:
            both(product, g)
            if g + 1 < len(groups):
                token = come_on(groups[g + 1], token)
            else:
                gram = gram_part([blocks[k] for k in ids], token)
                gram_swapped = swap(gram, "bin", 1)
                gram_come, gram_from, token = [], t + 1, gram
        if t >= chunks - 2:
            g_t = t - gram_from
            if g_t == 0:
                gram_own = {0: (both_cores(gram, gram_swapped, token), 0)}
                token = gram_own[0][0]
            if 0 <= g_t <= line - 2:
                before = gram_come[-1] if gram_come else None
                got, token = line_slot(flags, g_t, 1, gram_own, before, token)
                gram_come.append(got)
        if t == chunks - 1:
            factors_new, token = turned_back([blocks[k] for k in ids], ids, width, me1, token)
        c = t - (line - 1)
        if 0 <= c < chunks:
            both(end, c)
    gram_end = line_end(flags, gram_come, token)
    token = gram_end[0]
    share, token = shares(loadings, (gram_own[0][0],) + gram_end, ids, me1, token)
    for c in range(chunks):
        if c not in ends[0]:
            both(end, c)
        if c < chunks - 1:
            loadings_new, token = final(c, loadings_new, token)
        else:
            for half in range(HALVES):
                loadings_new, token = final(c, loadings_new, token, [half])
    return factors_new, loadings_new


def solution(mesh):
    placed = (P("bin", "gene"), P("bin", None), P(None, "gene"), P("bin"), P("bin", None))
    return jax.shard_map(
        on_device,
        mesh=mesh,
        in_specs=placed,
        out_specs=(P("bin", None), P(None, "gene")),
        check_vma=False,
    )
```

```python
import jax
import jax.numpy as jnp
from jax import lax
from jax.experimental import pallas as pl
from jax.experimental.pallas import tpu as pltpu
from jax.sharding import PartitionSpec as P

K = 256
G = 18432
PENALTY = float(G * K) / 64.0
EXTRA = 8
HALVES = 2
STEP = 512
READS = 4
MIB = 1024 * 1024
MINOR = (((1,), (1,)), ((), ()))
PLAIN = (((1,), (0,)), ((), ()))
F32 = jnp.float32
BF16 = jnp.bfloat16
ANY_SPEC = pl.BlockSpec(memory_space=pl.ANY)
VMEM_SPEC = pl.BlockSpec(memory_space=pltpu.VMEM)
SMEM_SPEC = pl.BlockSpec(memory_space=pltpu.SMEM)


def dot(a, b, dims, precision=None):
    return lax.dot_general(a, b, dims, precision=precision, preferred_element_type=F32)


def kernel_call(body, out_shape, us, limit=10, **kw):
    return pl.pallas_call(
        body,
        out_shape=out_shape,
        compiler_params=pltpu.CompilerParams(vmem_limit_bytes=limit * MIB),
        cost_estimate=pl.CostEstimate(flops=0, bytes_accessed=int(us * 3.69e6), transcendentals=0),
        **kw,
    )


def shape(*dims, dtype=F32):
    return jax.ShapeDtypeStruct(dims, dtype)


def pack(factors, position, me, width, bins):
    rows, width_all = factors.shape
    group = rows // bins
    lanes = 128 if width_all % 128 == 0 and 128 % width == 0 else width_all

    def body(me_ref, fac_ref, pos_ref, out_ref, turned):
        turned[...] = fac_ref[...].T
        first = pl.multiple_of(lax.rem(me_ref[0] * width, lanes), width)
        out_ref[0, :width, :] = turned[pl.ds(first, width), :]
        out_ref[0, width:, :] = jnp.broadcast_to(pos_ref[0], (EXTRA, group))

    grid_spec = pltpu.PrefetchScalarGridSpec(
        num_scalar_prefetch=1,
        grid=(bins,),
        in_specs=[
            pl.BlockSpec((group, lanes), lambda t, m: (t, m[0] * width // lanes)),
            pl.BlockSpec((1, 1, group), lambda t, m: (t, 0, 0)),
        ],
        out_specs=pl.BlockSpec((1, width + EXTRA, group), lambda t, m: (t, 0, 0)),
        scratch_shapes=[pltpu.VMEM((lanes, group), F32)],
    )
    return kernel_call(
        body, shape(bins, width + EXTRA, group), 3, grid_spec=grid_spec
    )(me, factors, position.astype(F32).reshape(bins, 1, group))


def to_grid(got, edge_codes, bin_me, token):
    bins, wide, group = got.shape
    width = wide - EXTRA
    grid_rows, grid_cols = edge_codes.shape
    rows = bins * group
    per = 4

    def body(me_ref, got_ref, code_ref, _, grid_ref, first_ref, last_ref, cell_ref, masked):
        block = jnp.concatenate([got_ref[s] for s in range(bins)], axis=1)
        cell = block[width : width + 1].astype(jnp.int32) - me_ref[0] * rows
        cell_ref[...] = cell
        at_row, at_col = cell // grid_cols, cell % grid_cols
        col_hot = jnp.where(
            lax.broadcasted_iota(jnp.int32, (grid_cols, rows), 0) == at_col, 1.0, 0.0
        ).astype(BF16)
        values = block[:width]
        high = values.astype(BF16)
        both = jnp.concatenate([high, (values - high.astype(F32)).astype(BF16)], axis=0)
        scale = code_ref[...].astype(F32) / 8.0
        for r in range(grid_rows):
            at = r % per * 2 * width
            if at == 0:
                for i in range(per):
                    mask = jnp.where(at_row == r + i, 1.0, 0.0).astype(BF16)
                    masked[i * 2 * width : (i + 1) * 2 * width, :] = both * mask
                placed = dot(masked[...], col_hot, MINOR)
            line = placed[at : at + width] + placed[at + width : at + 2 * width]
            row_scale = scale[r : r + 1]
            weighted = jnp.concatenate(
                [line * row_scale, jnp.broadcast_to(row_scale, (EXTRA, grid_cols))], axis=0
            )
            grid_ref[r] = weighted
            if r == 0:
                first_ref[...] = weighted
            if r == grid_rows - 1:
                last_ref[...] = weighted

    return kernel_call(
        body,
        (
            shape(grid_rows, wide, grid_cols),
            shape(wide, grid_cols),
            shape(wide, grid_cols),
            shape(1, rows, dtype=jnp.int32),
        ),
        3,
        limit=12,
        in_specs=[SMEM_SPEC, VMEM_SPEC, VMEM_SPEC, ANY_SPEC],
        out_specs=(VMEM_SPEC,) * 4,
        scratch_shapes=[pltpu.VMEM((per * 2 * width, rows), BF16)],
    )(bin_me, got, edge_codes, token)


def from_grid(grid, above, below, cell, edge_codes, bins, token):
    grid_rows, wide, grid_cols = grid.shape
    rows = cell.shape[1]
    group = rows // bins

    def body(grid_ref, above_ref, below_ref, cell_ref, code_ref, _, out_ref, halves):
        scale = code_ref[...].astype(F32) / 8.0
        lane = lax.broadcasted_iota(jnp.int32, (wide, grid_cols), 1)
        for r in range(grid_rows):
            here = grid_ref[r]
            upper = above_ref[...] if r == 0 else grid_ref[r - 1]
            lower = below_ref[...] if r == grid_rows - 1 else grid_ref[r + 1]
            left = jnp.where(lane == 0, 0.0, pltpu.roll(here, 1, 1))
            right = jnp.where(lane == grid_cols - 1, 0.0, pltpu.roll(here, grid_cols - 1, 1))
            value = scale[r : r + 1] * (left + right + 0.5 * (upper + lower))
            high = value.astype(BF16)
            halves[r * wide : (r + 1) * wide, :grid_cols] = high
            halves[r * wide : (r + 1) * wide, grid_cols:] = (value - high.astype(F32)).astype(BF16)
        cell = cell_ref[...]
        at_row, at_col = cell // grid_cols, cell % grid_cols
        for s in range(bins // 2):
            lo, hi = 2 * s * group, (2 * s + 2) * group
            hot = jnp.where(
                lax.broadcasted_iota(jnp.int32, (grid_cols, hi - lo), 0) == at_col[:, lo:hi], 1.0, 0.0
            ).astype(BF16)
            lines = dot(halves[...], jnp.concatenate([hot, hot], axis=0), PLAIN)
            row_here = at_row[:, lo:hi]
            total = jnp.zeros((wide, hi - lo), F32)
            for r in range(grid_rows):
                total = total + jnp.where(row_here == r, lines[r * wide : (r + 1) * wide], 0.0)
            out_ref[2 * s] = total[:, :group]
            out_ref[2 * s + 1] = total[:, group:]

    return kernel_call(
        body,
        shape(bins, wide, group),
        4,
        in_specs=[VMEM_SPEC] * 5 + [ANY_SPEC],
        out_specs=VMEM_SPEC,
        scratch_shapes=[pltpu.VMEM((grid_rows * wide, 2 * grid_cols), BF16)],
    )(grid, above, below, cell, edge_codes, token)


def numer_part(counts, loadings, me, genes_n, token):
    rows, genes = counts.shape
    width_all = loadings.shape[0]
    width = width_all // genes_n
    steps = rows // STEP
    side = genes // 2

    def body(me_ref, left_ref, right_ref, load_ref, _, *rest):
        outs, (load_f, load_bf, load_t, turned, sems) = rest[:genes_n], rest[genes_n:]
        at = pl.program_id(0)
        firsts = [pl.multiple_of((k ^ me_ref[0]) * width, width) for k in range(genes_n)]

        @pl.when(at == 0)
        def _():
            reads = [
                pltpu.make_async_copy(
                    load_ref.at[pl.ds(first, width), :], load_f.at[pl.ds(k * width, width), :], sems.at[k]
                )
                for k, first in enumerate(firsts)
            ]
            for copy in reads:
                copy.start()
            for copy in reads:
                copy.wait()
            load_bf[...] = load_f[...].astype(BF16)
            load_t[...] = load_bf[...].T

        def put(part):
            for k, out in enumerate(outs):
                out[...] = part[k * width : (k + 1) * width]

        @pl.when(at < steps)
        def _():
            part = dot(left_ref[...], load_t[:side, :], PLAIN)
            put((part + dot(right_ref[...], load_t[side:, :], PLAIN)).T)

        @pl.when(at == steps)
        def _():
            local = dot(load_bf[...], load_t[...], PLAIN)
            for k, first in enumerate(firsts):
                turned[pl.ds(first, width), :] = local[k * width : (k + 1) * width]
            put(jnp.concatenate([turned[...].T, jnp.zeros((width_all, STEP - width_all), F32)], axis=1))

    row_at = lambda i: jnp.minimum(i, steps - 1)
    grid_spec = pltpu.PrefetchScalarGridSpec(
        num_scalar_prefetch=1,
        grid=(steps + 1,),
        in_specs=[
            pl.BlockSpec((STEP, side), lambda i, m: (row_at(i), 0)),
            pl.BlockSpec((STEP, side), lambda i, m: (row_at(i), 1)),
            ANY_SPEC,
            ANY_SPEC,
        ],
        out_specs=(pl.BlockSpec((width, STEP), lambda i, m: (0, i)),) * genes_n,
        scratch_shapes=[
            pltpu.VMEM((width_all, genes), F32),
            pltpu.VMEM((width_all, genes), BF16),
            pltpu.VMEM((genes, width_all), BF16),
            pltpu.VMEM((width_all, width_all), F32),
            pltpu.SemaphoreType.DMA((genes_n,)),
        ],
    )
    return kernel_call(
        body, (shape(width, rows + STEP),) * genes_n, 14, limit=30, grid_spec=grid_spec
    )(me, counts, counts, loadings, token)


def swap(block, axis, bit):
    return lax.ppermute(block, axis, [(i, i ^ bit) for i in range(lax.axis_size(axis))])


def plain_terms(parts, factors, token):
    rows, width_all = factors.shape
    width = parts[0].shape[0]
    half_rows = rows // 2

    def body(*refs):
        n = len(parts)
        fac_ref, _, numer_ref, plain_ref, gram = refs[n:]

        def total(cols):
            out = refs[0][:, cols]
            for ref in refs[1:n]:
                out = out + ref[:, cols]
            return out

        @pl.when(pl.program_id(0) == 0)
        def _():
            gram[...] = total(slice(rows, rows + width_all))
            numer_ref[...] = total(slice(0, rows))

        plain_ref[...] = dot(fac_ref[...], gram[...], MINOR, lax.Precision.HIGHEST).T

    return kernel_call(
        body,
        (shape(width, rows),) * 2,
        60,
        limit=16,
        grid=(2,),
        in_specs=[VMEM_SPEC] * len(parts)
        + [pl.BlockSpec((half_rows, width_all), lambda i: (i, 0)), ANY_SPEC],
        out_specs=(VMEM_SPEC, pl.BlockSpec((width, half_rows), lambda i: (0, i))),
        scratch_shapes=[pltpu.VMEM((width, width_all), F32)],
    )(*parts, factors, token)


def new_factors(payload, back, numer, plain):
    bins, wide, group = payload.shape
    width = wide - EXTRA

    def body(pay_ref, back_ref, numer_ref, plain_ref, out_ref):
        pay = jnp.concatenate([pay_ref[s] for s in range(bins)], axis=1)
        got = jnp.concatenate([back_ref[s] for s in range(bins)], axis=1)
        fac, smooth, degree = pay[:width], got[:width], got[width : width + 1]
        out_ref[...] = (
            fac * (numer_ref[...] + PENALTY * smooth) / (plain_ref[...] + PENALTY * degree * fac)
        )

    return kernel_call(
        body,
        shape(width, bins * group),
        0.02,
        in_specs=[VMEM_SPEC] * 4,
        out_specs=VMEM_SPEC,
    )(payload, back, numer, plain)


def sent_on(blocks, token):
    n = len(blocks)

    def body(*refs):
        for src, dst in zip(refs[:n], refs[n + 1 :]):
            dst[...] = src[...]

    return kernel_call(
        body,
        tuple(shape(*b.shape) for b in blocks),
        0.02,
        in_specs=[VMEM_SPEC] * n + [ANY_SPEC],
        out_specs=(VMEM_SPEC,) * n,
    )(*blocks, token)


def turned_back(blocks, ids, width, me, token):
    rows = blocks[0].shape[1]
    width_all = len(ids) * width
    step = 384
    steps = rows // step

    def body(me_ref, *refs):
        out_ref, _, block = refs[-3:]
        for ref, k in zip(refs, ids):
            block[pl.ds(pl.multiple_of((k ^ me_ref[0]) * width, width), width), :] = ref[...]
        out_ref[...] = block[...].T

    grid_spec = pltpu.PrefetchScalarGridSpec(
        num_scalar_prefetch=1,
        grid=(steps,),
        in_specs=[pl.BlockSpec((width, step), lambda i, m: (0, i))] * len(ids) + [ANY_SPEC],
        out_specs=(pl.BlockSpec((step, width_all), lambda i, m: (i, 0)), VMEM_SPEC),
        scratch_shapes=[pltpu.VMEM((width_all, step), F32)],
    )
    outs = (pltpu.HBM((rows, width_all), F32), shape(8, 128))
    return kernel_call(body, outs, 0.02, limit=8, grid_spec=grid_spec)(me, *blocks, token)


def cross_part(blocks, n_old, counts, half, with_gram, width_all, tokens):
    width, rows = blocks[0].shape
    genes = counts.shape[1]
    cols = genes // HALVES
    step = 384
    steps = cols // step
    n = len(blocks) - n_old
    deep = rows // READS
    use = blocks if with_gram else blocks[n_old:]
    skip = len(use) - n

    def body(*refs):
        outs, fac = refs[-1 - n : -1], refs[-1]
        at = pl.program_id(0)

        @pl.when(at == 0)
        def _():
            for j, ref in enumerate(refs[READS : READS + len(use)]):
                fac[j * width : (j + 1) * width, :] = ref[...].astype(BF16)

        def put(part, where):
            for j, out in enumerate(outs):
                out[:, where] = part[j * width : (j + 1) * width]

        new = lambda i: fac[skip * width :, i * deep : (i + 1) * deep]
        part = dot(new(0), refs[0][...], PLAIN)
        for i in range(1, READS):
            part = part + dot(new(i), refs[i][...], PLAIN)
        put(part, pl.ds(pl.multiple_of(at * step, step), step))

        if with_gram:

            @pl.when(at == steps - 1)
            def _():
                near = dot(fac[skip * width :, :], fac[...], MINOR)
                if near.shape[1] < width_all:
                    gap = jnp.zeros((near.shape[0], width_all - near.shape[1]), F32)
                    near = jnp.concatenate([near, gap], axis=1)
                put(near, slice(cols, cols + width_all))

    read = lambda i: pl.BlockSpec((deep, step), lambda g: (i, half * steps + g))
    return kernel_call(
        body,
        (shape(width, cols + with_gram * width_all),) * n,
        0.02,
        limit=24,
        grid=(steps,),
        in_specs=[read(i) for i in range(READS)] + [VMEM_SPEC] * len(use) + [ANY_SPEC] * len(tokens),
        out_specs=(VMEM_SPEC,) * n,
        scratch_shapes=[pltpu.VMEM((len(use) * width, rows), BF16)],
    )(*[counts] * READS, *use, *tokens)


def tiny_token(arrays):
    def body(*refs):
        refs[-1][...] = jnp.zeros(refs[-1].shape, F32)

    return kernel_call(
        body, shape(8, 128), 0.02, in_specs=[ANY_SPEC] * len(arrays), out_specs=VMEM_SPEC
    )(*arrays)


def both_cores(parts, came, token):
    n = len(parts)

    def body(*refs):
        for a, b, out in zip(refs[:n], refs[n : 2 * n], refs[2 * n + 1 :]):
            out[...] = a[...] + b[...]

    return kernel_call(
        body,
        tuple(shape(*part.shape) for part in parts),
        0.02,
        in_specs=[VMEM_SPEC] * (2 * n) + [ANY_SPEC],
        out_specs=(VMEM_SPEC,) * n,
    )(*parts, *came, token)


def line_slot(flags, t, chunks, own, come, token):
    line = lax.axis_size("bin") // 2
    places = [q for q in range(line - 1) if 0 <= t - q < chunks]
    hops = [(2 * q, 2 * q + 2) for q in places]
    hops += [(2 * (line - 1 - q) + 1, 2 * (line - 2 - q) + 1) for q in places]
    if t == 0:
        return lax.ppermute(own[0], "bin", hops), token
    arrays = [own[t - q] for q in places]

    def body(flag_ref, come_ref, _, *refs):
        for i, q in enumerate(places):

            @pl.when(flag_ref[2] == q)
            def _():
                value = refs[i][...]
                refs[-1][...] = value if q == 0 else value + come_ref[...]

    send = kernel_call(
        body,
        shape(*come.shape),
        0.02,
        in_specs=[SMEM_SPEC, VMEM_SPEC, ANY_SPEC] + [VMEM_SPEC] * len(arrays),
        out_specs=VMEM_SPEC,
    )(flags, come, token, *arrays)
    return lax.ppermute(send, "bin", hops), send


def line_end(flags, come, token):
    def body(flag_ref, _, *refs):
        out = refs[-1]

        @pl.when(flag_ref[2] == 0)
        def _():
            out[...] = jnp.zeros(out.shape, F32)

        for d in range(len(come)):

            @pl.when(flag_ref[2] == d + 1)
            def _():
                out[...] = refs[d][...]

    end = kernel_call(
        body,
        shape(*come[0].shape),
        0.02,
        in_specs=[SMEM_SPEC, ANY_SPEC] + [VMEM_SPEC] * len(come),
        out_specs=VMEM_SPEC,
    )(flags, token, *come)
    return end, swap(end, "bin", 1)


def shares(loadings, sums, ids, cols, me, token):
    width_all, genes = loadings.shape
    width = width_all // len(ids)
    steps = 6
    step = genes // steps
    arrays = [x for terms in sums for x in terms]

    def body(me_ref, load_ref, *refs):
        out_ref, tiny, load, gram = refs[-4:]
        firsts = [pl.multiple_of((k ^ me_ref[0]) * width, width) for k in ids]

        @pl.when(pl.program_id(0) == 0)
        def _():
            behind = slice(cols, cols + width_all)
            for j in range(len(sums)):
                own, end, other = refs[3 * j : 3 * j + 3]
                gram[j * width : (j + 1) * width, :] = own[:, behind] + (end[:, behind] + other[:, behind])
            low = gram[...]
            row = lax.broadcasted_iota(jnp.int32, low.shape, 0) // width
            col = lax.broadcasted_iota(jnp.int32, low.shape, 1) // width
            gram[...] = jnp.where(col <= row, low, low.T)

        for j, first in enumerate(firsts):
            load[j * width : (j + 1) * width, :] = load_ref[pl.ds(first, width), :]
        value = load[...]
        value = value / dot(gram[...], value, PLAIN, lax.Precision.HIGHEST)
        for j, first in enumerate(firsts):
            out_ref[pl.ds(first, width), :] = value[j * width : (j + 1) * width]

    block = pl.BlockSpec((width_all, step), lambda i, f: (0, i))
    return kernel_call(
        body,
        (shape(width_all, genes), shape(8, 128)),
        0.02,
        limit=12,
        grid_spec=pltpu.PrefetchScalarGridSpec(
            num_scalar_prefetch=1,
            grid=(steps,),
            in_specs=[block] + [VMEM_SPEC] * len(arrays) + [ANY_SPEC],
            out_specs=(block, VMEM_SPEC),
            scratch_shapes=[
                pltpu.VMEM((width_all, step), F32),
                pltpu.VMEM((width_all, width_all), F32),
            ],
        ),
    )(me, loadings, *arrays, token)


def new_loadings(share, parts, k, width, me, before, token):
    width_all, genes = share.shape
    halves = sorted(parts)
    cols = genes // HALVES
    arrays = [x for h in halves for x in parts[h]]

    def body(me_ref, share_ref, _, *refs):
        out_ref = refs[-2]
        at = pl.ds(pl.multiple_of((k ^ me_ref[0]) * width, width), width)
        for i, h in enumerate(halves):
            own, end, other = refs[3 * i : 3 * i + 3]
            here = slice(h * cols, (h + 1) * cols)
            total = own[:, :cols] + (end[:, :cols] + other[:, :cols])
            out_ref[:, i * cols : (i + 1) * cols] = share_ref[at, here] * total

    operands = [me, share, token] + arrays
    specs = [VMEM_SPEC, ANY_SPEC] + [VMEM_SPEC] * len(arrays)
    aliases = {}
    if before is not None:
        operands.append(before)
        specs.append(ANY_SPEC)
        aliases = {len(operands) - 1: 0}
    column = 0 if len(halves) == HALVES else halves[0]
    return kernel_call(
        body,
        (pltpu.HBM((width_all, genes), F32), shape(8, 128)),
        0.02,
        limit=6,
        grid_spec=pltpu.PrefetchScalarGridSpec(
            num_scalar_prefetch=1,
            grid=(1,),
            in_specs=specs,
            out_specs=(
                pl.BlockSpec((width, len(halves) * cols), lambda i, m: (k ^ m[0], column)),
                VMEM_SPEC,
            ),
        ),
        input_output_aliases=aliases,
    )(*operands)


def on_device(counts, factors, loadings, position, edge_codes):
    bins, genes_n = lax.axis_size("bin"), lax.axis_size("gene")
    line = bins // 2
    me, bin_me = lax.axis_index("gene"), lax.axis_index("bin")
    rows, width_all = factors.shape
    width = width_all // genes_n
    scalar = lambda x: jnp.asarray(x, jnp.int32).reshape(1)
    me1, bin1 = scalar(me), scalar(bin_me)
    core, chip = bin1 & 1, bin1 >> 1
    flags = jnp.concatenate([me1, core, jnp.where(core == 0, chip, line - 1 - chip)])
    bits = [1 << b for b in range(genes_n.bit_length() - 1)]

    counts = pltpu.with_memory_space_constraint(counts, pltpu.HBM)
    payload = pack(factors, position, me1, width, bins)
    got = lax.all_to_all(payload, "bin", split_axis=0, concat_axis=0, tiled=True)
    parts = numer_part(
        counts, pltpu.with_memory_space_constraint(loadings, pltpu.HBM), me1, genes_n, payload
    )
    parts = [parts[0]] + [swap(parts[k], "gene", k) for k in range(1, genes_n)]
    grid, first, last, cell = to_grid(got, edge_codes, bin1, parts[0])
    above = lax.ppermute(last, "bin", [(i, i + 1) for i in range(bins - 1)])
    below = lax.ppermute(first, "bin", [(i + 1, i) for i in range(bins - 1)])
    smooth = from_grid(grid, above, below, cell, edge_codes, bins, grid)
    back = lax.all_to_all(smooth, "bin", split_axis=0, concat_axis=0, tiled=True)
    numer, plain = plain_terms(parts, factors, smooth)
    own_block = new_factors(payload, back, numer, plain)

    ids = sorted(range(genes_n), key=lambda k: (bin(k).count("1"), k))
    groups = [[k for k in ids if bin(k).count("1") == n] for n in range(len(bits) + 1)]
    chunks = len(ids)
    blocks = {0: own_block}
    for k in bits:
        blocks[k] = swap(own_block, "gene", k)

    def come_on(group, token):
        outs = sent_on([blocks[k & (k - 1)] for k in group], token)
        for k, out in zip(group, outs):
            blocks[k] = swap(out, "gene", k & -k)
        return outs[-1]

    pending = [[None] * len(groups) for _ in range(HALVES)]
    own = [{} for _ in range(HALVES)]
    come = [[] for _ in range(HALVES)]
    ends = [{} for _ in range(HALVES)]

    def product(g, half, *tokens):
        upto = ids.index(groups[g][-1]) + 1
        n_old = upto - len(groups[g])
        parts = cross_part(
            [blocks[k] for k in ids[:upto]], n_old, counts, half, half == 0, width_all, tokens
        )
        pending[half][g] = (parts, [swap(part, "bin", 1) for part in parts])
        return parts[-1]

    def own_chunks(g, half, token):
        arrays = both_cores(*pending[half][g], token)
        for k, array in zip(groups[g], arrays):
            own[half][ids.index(k)] = array
        return arrays[-1]

    def slot(half, t, token):
        before = come[half][-1] if come[half] else None
        got, token = line_slot(flags, t, chunks, own[half], before, token)
        come[half].append(got)
        return token

    def end(c, half, token):
        ends[half][c] = line_end(flags, come[half][c : c + line - 1], token)
        return ends[half][c][0]

    def final(c, before, token, halves=range(HALVES)):
        sums = {h: (own[h][c],) + ends[h][c] for h in halves}
        return new_loadings(share, sums, ids[c], width, me1, before, token)

    def both(step, *args):
        nonlocal token
        for half in range(HALVES):
            token = step(*args, half, token)

    def awaited(arrays, token):
        return tiny_token(list(arrays) + [token])

    token = own_block
    both(product, 0)
    token = awaited([blocks[k] for k in bits], token)
    if len(groups) > 2:
        token = come_on(groups[2], token)
    for half in range(HALVES):
        token = own_chunks(0, half, token)
        token = slot(half, 0, token)
    both(product, 1)
    firsts = {ids.index(group[0]): g for g, group in enumerate(groups)}
    last_slot = chunks + line - 3
    for t in range(1, last_slot + 1):
        if t in firsts:
            arrived = [come[half][-1] for half in range(HALVES)]
            if firsts[t] + 1 < len(groups):
                arrived += [blocks[k] for k in groups[firsts[t] + 1]]
            token = awaited(arrived, token)
        for half in range(HALVES):
            if t in firsts:
                token = own_chunks(firsts[t], half, token)
            token = slot(half, t, token)
        g = firsts.get(t, len(groups)) + 1
        if g < len(groups):
            both(product, g)
            if g + 1 < len(groups):
                token = come_on(groups[g + 1], token)
        if t == chunks - 1:
            factors_new, token = turned_back([blocks[k] for k in ids], ids, width, me1, token)
        c = t - (line - 1)
        if c - 1 in ends[0]:
            token = awaited([ends[half][c - 1][1] for half in range(HALVES)], token)
        if 0 <= c < chunks:
            both(end, c)
    share = loadings_new = None
    for c in range(chunks):
        if c not in ends[0]:
            both(end, c)
    sums = [(own[0][c],) + ends[0][c] for c in range(chunks)]
    share, token = shares(loadings, sums, ids, counts.shape[1] // HALVES, me1, token)
    for c in range(chunks - 1):
        loadings_new, token = final(c, loadings_new, token)
    for half in range(HALVES):
        loadings_new, token = final(chunks - 1, loadings_new, token, [half])
    return factors_new, loadings_new


def solution(mesh):
    placed = (P("bin", "gene"), P("bin", None), P(None, "gene"), P("bin"), P("bin", None))
    return jax.shard_map(
        on_device,
        mesh=mesh,
        in_specs=placed,
        out_specs=(P("bin", None), P(None, "gene")),
        check_vma=False,
    )
```

```python
import jax
import jax.numpy as jnp
from jax import lax
from jax.experimental import pallas as pl
from jax.experimental.pallas import tpu as pltpu
from jax.sharding import PartitionSpec as P

K = 256
G = 18432
PENALTY = float(G * K) / 64.0
EXTRA = 8
HALVES = 2
STEP = 512
READS = 2
MIB = 1024 * 1024
MINOR = (((1,), (1,)), ((), ()))
PLAIN = (((1,), (0,)), ((), ()))
F32 = jnp.float32
BF16 = jnp.bfloat16
ANY_SPEC = pl.BlockSpec(memory_space=pl.ANY)
VMEM_SPEC = pl.BlockSpec(memory_space=pltpu.VMEM)
SMEM_SPEC = pl.BlockSpec(memory_space=pltpu.SMEM)


def dot(a, b, dims, precision=None):
    return lax.dot_general(a, b, dims, precision=precision, preferred_element_type=F32)


def kernel_call(body, out_shape, us, limit=10, **kw):
    return pl.pallas_call(
        body,
        out_shape=out_shape,
        compiler_params=pltpu.CompilerParams(vmem_limit_bytes=limit * MIB),
        cost_estimate=pl.CostEstimate(flops=0, bytes_accessed=int(us * 3.69e6), transcendentals=0),
        **kw,
    )


def shape(*dims, dtype=F32):
    return jax.ShapeDtypeStruct(dims, dtype)


def pack(factors, position, me, width, bins):
    rows, width_all = factors.shape
    group = rows // bins
    lanes = 128 if width_all % 128 == 0 and 128 % width == 0 else width_all

    def body(me_ref, fac_ref, pos_ref, out_ref, turned):
        turned[...] = fac_ref[...].T
        first = pl.multiple_of(lax.rem(me_ref[0] * width, lanes), width)
        out_ref[0, :width, :] = turned[pl.ds(first, width), :]
        out_ref[0, width:, :] = jnp.broadcast_to(pos_ref[0], (EXTRA, group))

    grid_spec = pltpu.PrefetchScalarGridSpec(
        num_scalar_prefetch=1,
        grid=(bins,),
        in_specs=[
            pl.BlockSpec((group, lanes), lambda t, m: (t, m[0] * width // lanes)),
            pl.BlockSpec((1, 1, group), lambda t, m: (t, 0, 0)),
        ],
        out_specs=pl.BlockSpec((1, width + EXTRA, group), lambda t, m: (t, 0, 0)),
        scratch_shapes=[pltpu.VMEM((lanes, group), F32)],
    )
    return kernel_call(
        body, shape(bins, width + EXTRA, group), 3, grid_spec=grid_spec
    )(me, factors, position.astype(F32).reshape(bins, 1, group))


def to_grid(got, edge_codes, bin_me, token):
    bins, wide, group = got.shape
    width = wide - EXTRA
    grid_rows, grid_cols = edge_codes.shape
    rows = bins * group
    per = 4

    def body(me_ref, got_ref, code_ref, _, grid_ref, first_ref, last_ref, cell_ref, masked):
        block = jnp.concatenate([got_ref[s] for s in range(bins)], axis=1)
        cell = block[width : width + 1].astype(jnp.int32) - me_ref[0] * rows
        cell_ref[...] = cell
        at_row, at_col = cell // grid_cols, cell % grid_cols
        col_hot = jnp.where(
            lax.broadcasted_iota(jnp.int32, (grid_cols, rows), 0) == at_col, 1.0, 0.0
        ).astype(BF16)
        values = block[:width]
        high = values.astype(BF16)
        both = jnp.concatenate([high, (values - high.astype(F32)).astype(BF16)], axis=0)
        scale = code_ref[...].astype(F32) / 8.0
        for r in range(grid_rows):
            at = r % per * 2 * width
            if at == 0:
                for i in range(per):
                    mask = jnp.where(at_row == r + i, 1.0, 0.0).astype(BF16)
                    masked[i * 2 * width : (i + 1) * 2 * width, :] = both * mask
                placed = dot(masked[...], col_hot, MINOR)
            line = placed[at : at + width] + placed[at + width : at + 2 * width]
            row_scale = scale[r : r + 1]
            weighted = jnp.concatenate(
                [line * row_scale, jnp.broadcast_to(row_scale, (EXTRA, grid_cols))], axis=0
            )
            grid_ref[r] = weighted
            if r == 0:
                first_ref[...] = weighted
            if r == grid_rows - 1:
                last_ref[...] = weighted

    return kernel_call(
        body,
        (
            shape(grid_rows, wide, grid_cols),
            shape(wide, grid_cols),
            shape(wide, grid_cols),
            shape(1, rows, dtype=jnp.int32),
        ),
        3,
        limit=12,
        in_specs=[SMEM_SPEC, VMEM_SPEC, VMEM_SPEC, ANY_SPEC],
        out_specs=(VMEM_SPEC,) * 4,
        scratch_shapes=[pltpu.VMEM((per * 2 * width, rows), BF16)],
    )(bin_me, got, edge_codes, token)


def from_grid(grid, above, below, cell, edge_codes, bins, token):
    grid_rows, wide, grid_cols = grid.shape
    rows = cell.shape[1]
    group = rows // bins

    def body(grid_ref, above_ref, below_ref, cell_ref, code_ref, _, out_ref, halves):
        scale = code_ref[...].astype(F32) / 8.0
        lane = lax.broadcasted_iota(jnp.int32, (wide, grid_cols), 1)
        for r in range(grid_rows):
            here = grid_ref[r]
            upper = above_ref[...] if r == 0 else grid_ref[r - 1]
            lower = below_ref[...] if r == grid_rows - 1 else grid_ref[r + 1]
            left = jnp.where(lane == 0, 0.0, pltpu.roll(here, 1, 1))
            right = jnp.where(lane == grid_cols - 1, 0.0, pltpu.roll(here, grid_cols - 1, 1))
            value = scale[r : r + 1] * (left + right + 0.5 * (upper + lower))
            high = value.astype(BF16)
            halves[r * wide : (r + 1) * wide, :grid_cols] = high
            halves[r * wide : (r + 1) * wide, grid_cols:] = (value - high.astype(F32)).astype(BF16)
        cell = cell_ref[...]
        at_row, at_col = cell // grid_cols, cell % grid_cols
        for s in range(bins // 2):
            lo, hi = 2 * s * group, (2 * s + 2) * group
            hot = jnp.where(
                lax.broadcasted_iota(jnp.int32, (grid_cols, hi - lo), 0) == at_col[:, lo:hi], 1.0, 0.0
            ).astype(BF16)
            lines = dot(halves[...], jnp.concatenate([hot, hot], axis=0), PLAIN)
            row_here = at_row[:, lo:hi]
            total = jnp.zeros((wide, hi - lo), F32)
            for r in range(grid_rows):
                total = total + jnp.where(row_here == r, lines[r * wide : (r + 1) * wide], 0.0)
            out_ref[2 * s] = total[:, :group]
            out_ref[2 * s + 1] = total[:, group:]

    return kernel_call(
        body,
        shape(bins, wide, group),
        4,
        in_specs=[VMEM_SPEC] * 5 + [ANY_SPEC],
        out_specs=VMEM_SPEC,
        scratch_shapes=[pltpu.VMEM((grid_rows * wide, 2 * grid_cols), BF16)],
    )(grid, above, below, cell, edge_codes, token)


def numer_part(counts, loadings, me, genes_n, half, send_ids, token):
    rows, genes = counts.shape
    first_call = loadings.dtype == F32
    width_all = loadings.shape[0] if first_call else loadings.shape[1]
    width = width_all // genes_n
    half_rows = rows // 2
    steps = half_rows // STEP
    side = genes // 2
    keep_ids = [k for k in range(genes_n) if k not in send_ids]
    total_cols = half_rows + first_call * width_all

    def body(me_ref, left_ref, right_ref, *refs):
        at = pl.program_id(0)
        firsts = [pl.multiple_of((k ^ me_ref[0]) * width, width) for k in range(genes_n)]
        if first_call:
            load_ref, _, send_ref, keep_ref, load_t, load_bf, load_f, turned, sems = refs

            @pl.when(at == 0)
            def _():
                reads = [
                    pltpu.make_async_copy(
                        load_ref.at[pl.ds(first, width), :],
                        load_f.at[pl.ds(k * width, width), :],
                        sems.at[k],
                    )
                    for k, first in enumerate(firsts)
                ]
                for copy in reads:
                    copy.start()
                for k, copy in enumerate(reads):
                    copy.wait()
                    here = slice(k * width, (k + 1) * width)
                    load_bf[here, :] = load_f[here, :].astype(BF16)
                load_t[...] = load_bf[...].T

        else:
            load_t, _, send_ref, keep_ref = refs

        def put(part, cols):
            for i, k in enumerate(send_ids):
                send_ref[i, :, cols] = part[k * width : (k + 1) * width]
            for i, k in enumerate(keep_ids):
                keep_ref[i, :, cols] = part[k * width : (k + 1) * width]

        part = dot(left_ref[...], load_t[:side, :], PLAIN)
        part = part + dot(right_ref[...], load_t[side:, :], PLAIN)
        put(part.T, pl.ds(pl.multiple_of(at * STEP, STEP), STEP))

        if first_call:

            @pl.when(at == 0)
            def _():
                local = dot(load_bf[...], load_t[...], PLAIN)
                for k, first in enumerate(firsts):
                    turned[pl.ds(first, width), :] = local[k * width : (k + 1) * width]
                put(turned[...].T, slice(half_rows, total_cols))

    out = shape(genes_n // 2, width, total_cols)
    out_spec = pl.BlockSpec(out.shape, lambda i, m: (0, 0, 0))
    outs, out_specs, scratch = (out, out), (out_spec, out_spec), []
    if first_call:
        outs += (shape(genes, width_all, dtype=BF16),)
        out_specs += (pl.BlockSpec((genes, width_all), lambda i, m: (0, 0)),)
        scratch = [
            pltpu.VMEM((width_all, genes), BF16),
            pltpu.VMEM((width_all, genes), F32),
            pltpu.VMEM((width_all, width_all), F32),
            pltpu.SemaphoreType.DMA((genes_n,)),
        ]
        load_spec = ANY_SPEC
    else:
        load_spec = pl.BlockSpec((genes, width_all), lambda i, m: (0, 0))
    grid_spec = pltpu.PrefetchScalarGridSpec(
        num_scalar_prefetch=1,
        grid=(steps,),
        in_specs=[
            pl.BlockSpec((STEP, side), lambda i, m: (i + half * steps, 0)),
            pl.BlockSpec((STEP, side), lambda i, m: (i + half * steps, 1)),
            load_spec,
            ANY_SPEC,
        ],
        out_specs=out_specs,
        scratch_shapes=scratch,
    )
    return kernel_call(body, outs, 7, limit=36, grid_spec=grid_spec)(me, counts, counts, loadings, token)


def swap(block, axis, bit):
    return lax.ppermute(block, axis, [(i, i ^ bit) for i in range(lax.axis_size(axis))])


def picked_sum(arrays, ids, token):
    _, width, cols = arrays[0].shape
    first, step = ids[0], (ids[1] - ids[0] if len(ids) > 1 else 1)

    def body(*refs):
        total = refs[0][...]
        for ref in refs[1:-2]:
            total = total + ref[...]
        refs[-1][...] = total

    return kernel_call(
        body,
        shape(len(ids), width, cols),
        0.02,
        grid=(len(ids),),
        in_specs=[pl.BlockSpec((1, width, cols), lambda i: (first + step * i, 0, 0))] * len(arrays)
        + [ANY_SPEC],
        out_specs=pl.BlockSpec((1, width, cols), lambda i: (i, 0, 0)),
    )(*arrays, token)


def plain_terms(first, second, factors, token):
    rows, width_all = factors.shape
    width = first[0].shape[1]
    half_rows = rows // 2
    n = len(first)

    def body(*refs):
        fac_ref, _, numer_ref, plain_ref, gram = refs[2 * n :]

        def total(part, cols):
            out = part[0][0, :, cols]
            for ref in part[1:]:
                out = out + ref[0, :, cols]
            return out

        @pl.when(pl.program_id(0) == 0)
        def _():
            gram[...] = total(refs[n : 2 * n], slice(half_rows, half_rows + width_all))
            numer_ref[...] = total(refs[:n], slice(0, half_rows))

        @pl.when(pl.program_id(0) == 1)
        def _():
            numer_ref[...] = total(refs[n : 2 * n], slice(0, half_rows))

        plain_ref[...] = dot(fac_ref[...], gram[...], MINOR, lax.Precision.HIGHEST).T

    out_spec = pl.BlockSpec((width, half_rows), lambda i: (0, i))
    arrays = list(first) + list(second)
    return kernel_call(
        body,
        (shape(width, rows),) * 2,
        4,
        limit=24,
        grid=(2,),
        in_specs=[pl.BlockSpec((1,) + x.shape[1:], lambda i: (0, 0, 0)) for x in arrays]
        + [pl.BlockSpec((half_rows, width_all), lambda i: (i, 0)), ANY_SPEC],
        out_specs=(out_spec, out_spec),
        scratch_shapes=[pltpu.VMEM((width, width_all), F32)],
    )(*arrays, factors, token)


def new_factors(payload, back, numer, plain):
    bins, wide, group = payload.shape
    width = wide - EXTRA

    def body(pay_ref, back_ref, numer_ref, plain_ref, out_ref):
        pay = jnp.concatenate([pay_ref[0], pay_ref[1]], axis=1)
        got = jnp.concatenate([back_ref[0], back_ref[1]], axis=1)
        fac, smooth, degree = pay[:width], got[:width], got[width : width + 1]
        out_ref[...] = (
            fac * (numer_ref[...] + PENALTY * smooth) / (plain_ref[...] + PENALTY * degree * fac)
        )

    pair = pl.BlockSpec((2, wide, group), lambda i: (i, 0, 0))
    cols = pl.BlockSpec((width, 2 * group), lambda i: (0, i))
    return kernel_call(
        body,
        shape(width, bins * group),
        0.02,
        grid=(bins // 2,),
        in_specs=[pair, pair, cols, cols],
        out_specs=cols,
    )(payload, back, numer, plain)


def sent_on(blocks, token):
    n = len(blocks)

    def body(*refs):
        for src, dst in zip(refs[:n], refs[n + 1 :]):
            dst[...] = src[...]

    return kernel_call(
        body,
        tuple(shape(*b.shape) for b in blocks),
        0.02,
        in_specs=[VMEM_SPEC] * n + [ANY_SPEC],
        out_specs=(VMEM_SPEC,) * n,
    )(*blocks, token)


def turned_back(blocks, ids, width, me, token):
    rows = blocks[0].shape[1]
    width_all = len(ids) * width
    step = 384
    steps = rows // step

    def body(me_ref, *refs):
        out_ref, _, block = refs[-3:]
        for ref, k in zip(refs, ids):
            block[pl.ds(pl.multiple_of((k ^ me_ref[0]) * width, width), width), :] = ref[...]
        out_ref[...] = block[...].T

    grid_spec = pltpu.PrefetchScalarGridSpec(
        num_scalar_prefetch=1,
        grid=(steps,),
        in_specs=[pl.BlockSpec((width, step), lambda i, m: (0, i))] * len(ids) + [ANY_SPEC],
        out_specs=(pl.BlockSpec((step, width_all), lambda i, m: (i, 0)), VMEM_SPEC),
        scratch_shapes=[pltpu.VMEM((width_all, step), F32)],
    )
    outs = (pltpu.HBM((rows, width_all), F32), shape(8, 128))
    return kernel_call(body, outs, 0.02, limit=8, grid_spec=grid_spec)(me, *blocks, token)


def cross_part(blocks, n_old, counts, half, with_gram, width_all, tokens):
    width, rows = blocks[0].shape
    cols = counts.shape[1] // HALVES
    n = len(blocks) - n_old
    deep = STEP // READS
    use = blocks if with_gram else blocks[n_old:]
    skip = len(use) - n

    def body(*refs):
        outs, fac = refs[-1 - n : -1], refs[-1]
        at = pl.program_id(0)

        @pl.when(at == 0)
        def _():
            for j, ref in enumerate(refs[READS : READS + len(use)]):
                fac[j * width : (j + 1) * width, :] = ref[...].astype(BF16)

        def put(part, where, add):
            for j, out in enumerate(outs):
                value = part[j * width : (j + 1) * width]
                out[:, where] = out[:, where] + value if add else value

        part = None
        for i in range(READS):
            new = fac[skip * width :, pl.ds(pl.multiple_of(at * STEP + i * deep, deep), deep)]
            more = dot(new, refs[i][...], PLAIN)
            part = more if part is None else part + more
        pl.when(at == 0)(lambda: put(part, slice(0, cols), False))
        pl.when(at > 0)(lambda: put(part, slice(0, cols), True))

        if with_gram:

            @pl.when(at == 0)
            def _():
                near = dot(fac[skip * width :, :], fac[...], MINOR)
                if near.shape[1] < width_all:
                    gap = jnp.zeros((near.shape[0], width_all - near.shape[1]), F32)
                    near = jnp.concatenate([near, gap], axis=1)
                put(near, slice(cols, cols + width_all), False)

    read = lambda i: pl.BlockSpec((deep, cols), lambda g: (g * READS + i, half))
    return kernel_call(
        body,
        (shape(width, cols + with_gram * width_all),) * n,
        0.02,
        limit=24,
        grid=(rows // STEP,),
        in_specs=[read(i) for i in range(READS)] + [VMEM_SPEC] * len(use) + [ANY_SPEC] * len(tokens),
        out_specs=(VMEM_SPEC,) * n,
        scratch_shapes=[pltpu.VMEM((len(use) * width, rows), BF16)],
    )(*[counts] * READS, *use, *tokens)


def tiny_token(arrays):
    def body(*refs):
        refs[-1][...] = jnp.zeros(refs[-1].shape, F32)

    return kernel_call(
        body, shape(8, 128), 0.02, in_specs=[ANY_SPEC] * len(arrays), out_specs=VMEM_SPEC
    )(*arrays)


def both_cores(parts, came, token):
    n = len(parts)

    def body(*refs):
        for a, b, out in zip(refs[:n], refs[n : 2 * n], refs[2 * n + 1 :]):
            out[...] = a[...] + b[...]

    return kernel_call(
        body,
        tuple(shape(*part.shape) for part in parts),
        0.02,
        in_specs=[VMEM_SPEC] * (2 * n) + [ANY_SPEC],
        out_specs=(VMEM_SPEC,) * n,
    )(*parts, *came, token)


def line_slot(flags, t, chunks, own, come, token):
    line = lax.axis_size("bin") // 2
    places = [q for q in range(line - 1) if 0 <= t - q < chunks]
    hops = [(2 * q, 2 * q + 2) for q in places]
    hops += [(2 * (line - 1 - q) + 1, 2 * (line - 2 - q) + 1) for q in places]
    if t == 0:
        return lax.ppermute(own[0], "bin", hops), token
    arrays = [own[t - q] for q in places]

    def body(flag_ref, come_ref, _, *refs):
        for i, q in enumerate(places):

            @pl.when(flag_ref[2] == q)
            def _():
                value = refs[i][...]
                refs[-1][...] = value if q == 0 else value + come_ref[...]

    send = kernel_call(
        body,
        shape(*come.shape),
        0.02,
        in_specs=[SMEM_SPEC, VMEM_SPEC, ANY_SPEC] + [VMEM_SPEC] * len(arrays),
        out_specs=VMEM_SPEC,
    )(flags, come, token, *arrays)
    return lax.ppermute(send, "bin", hops), send


def line_end(flags, come, token):
    def body(flag_ref, _, *refs):
        out = refs[-1]

        @pl.when(flag_ref[2] == 0)
        def _():
            out[...] = jnp.zeros(out.shape, F32)

        for d in range(len(come)):

            @pl.when(flag_ref[2] == d + 1)
            def _():
                out[...] = refs[d][...]

    end = kernel_call(
        body,
        shape(*come[0].shape),
        0.02,
        in_specs=[SMEM_SPEC, ANY_SPEC] + [VMEM_SPEC] * len(come),
        out_specs=VMEM_SPEC,
    )(flags, token, *come)
    return end, swap(end, "bin", 1)


def shares(loadings, sums, ids, cols, me, token):
    width_all, genes = loadings.shape
    width = width_all // len(ids)
    steps = 6
    step = genes // steps
    arrays = [x for terms in sums for x in terms]

    def body(me_ref, load_ref, *refs):
        out_ref, tiny, load, gram = refs[-4:]
        firsts = [pl.multiple_of((k ^ me_ref[0]) * width, width) for k in ids]

        @pl.when(pl.program_id(0) == 0)
        def _():
            behind = slice(cols, cols + width_all)
            for j in range(len(sums)):
                own, end, other = refs[3 * j : 3 * j + 3]
                gram[j * width : (j + 1) * width, :] = own[:, behind] + (end[:, behind] + other[:, behind])
            low = gram[...]
            row = lax.broadcasted_iota(jnp.int32, low.shape, 0) // width
            col = lax.broadcasted_iota(jnp.int32, low.shape, 1) // width
            gram[...] = jnp.where(col <= row, low, low.T)

        for j, first in enumerate(firsts):
            load[j * width : (j + 1) * width, :] = load_ref[pl.ds(first, width), :]
        value = load[...]
        value = value / dot(gram[...], value, PLAIN, lax.Precision.HIGHEST)
        for j, first in enumerate(firsts):
            out_ref[pl.ds(first, width), :] = value[j * width : (j + 1) * width]

    block = pl.BlockSpec((width_all, step), lambda i, f: (0, i))
    return kernel_call(
        body,
        (shape(width_all, genes), shape(8, 128)),
        0.02,
        limit=12,
        grid_spec=pltpu.PrefetchScalarGridSpec(
            num_scalar_prefetch=1,
            grid=(steps,),
            in_specs=[block] + [VMEM_SPEC] * len(arrays) + [ANY_SPEC],
            out_specs=(block, VMEM_SPEC),
            scratch_shapes=[
                pltpu.VMEM((width_all, step), F32),
                pltpu.VMEM((width_all, width_all), F32),
            ],
        ),
    )(me, loadings, *arrays, token)


def new_loadings(share, parts, k, width, me, before, token):
    width_all, genes = share.shape
    halves = sorted(parts)
    cols = genes // HALVES
    arrays = [x for h in halves for x in parts[h]]

    def body(me_ref, share_ref, _, *refs):
        out_ref = refs[-2]
        at = pl.ds(pl.multiple_of((k ^ me_ref[0]) * width, width), width)
        for i, h in enumerate(halves):
            own, end, other = refs[3 * i : 3 * i + 3]
            here = slice(h * cols, (h + 1) * cols)
            total = own[:, :cols] + (end[:, :cols] + other[:, :cols])
            out_ref[:, i * cols : (i + 1) * cols] = share_ref[at, here] * total

    operands = [me, share, token] + arrays
    specs = [VMEM_SPEC, ANY_SPEC] + [VMEM_SPEC] * len(arrays)
    aliases = {}
    if before is not None:
        operands.append(before)
        specs.append(ANY_SPEC)
        aliases = {len(operands) - 1: 0}
    column = 0 if len(halves) == HALVES else halves[0]
    return kernel_call(
        body,
        (pltpu.HBM((width_all, genes), F32), shape(8, 128)),
        0.02,
        limit=6,
        grid_spec=pltpu.PrefetchScalarGridSpec(
            num_scalar_prefetch=1,
            grid=(1,),
            in_specs=specs,
            out_specs=(
                pl.BlockSpec((width, len(halves) * cols), lambda i, m: (k ^ m[0], column)),
                VMEM_SPEC,
            ),
        ),
        input_output_aliases=aliases,
    )(*operands)


def on_device(counts, factors, loadings, position, edge_codes):
    bins, genes_n = lax.axis_size("bin"), lax.axis_size("gene")
    line = bins // 2
    me, bin_me = lax.axis_index("gene"), lax.axis_index("bin")
    rows, width_all = factors.shape
    width = width_all // genes_n
    scalar = lambda x: jnp.asarray(x, jnp.int32).reshape(1)
    me1, bin1 = scalar(me), scalar(bin_me)
    core, chip = bin1 & 1, bin1 >> 1
    flags = jnp.concatenate([me1, core, jnp.where(core == 0, chip, line - 1 - chip)])
    bits = [1 << b for b in range(genes_n.bit_length() - 1)]

    counts = pltpu.with_memory_space_constraint(counts, pltpu.HBM)
    payload = pack(factors, position, me1, width, bins)
    got = lax.all_to_all(payload, "bin", split_axis=0, concat_axis=0, tiled=True)
    orders = (bits, bits[::-1])
    token, load = payload, pltpu.with_memory_space_constraint(loadings, pltpu.HBM)
    parts, keeps = [None, None], [None, None]
    for half in (1, 0):
        bit = orders[half][0]
        send_ids = [k for k in range(genes_n) if k & bit]
        keeps[half] = [k for k in range(genes_n) if not k & bit]
        send, keep, *made = numer_part(counts, load, me1, genes_n, half, send_ids, token)
        load = made[0] if made else load
        token = keep
        parts[half] = [keep, swap(send, "gene", bit)]

    def scatter_more(half, bit, token):
        out_ids = [i for i, k in enumerate(keeps[half]) if k & bit]
        in_ids = [i for i, k in enumerate(keeps[half]) if not k & bit]
        keeps[half] = [keeps[half][i] for i in in_ids]
        send = picked_sum(parts[half], out_ids, token)
        if len(in_ids) > 1:
            parts[half] = [picked_sum(parts[half], in_ids, send)]
        parts[half] = parts[half] + [swap(send, "gene", bit)]
        return send

    grid, first, last, cell = to_grid(got, edge_codes, bin1, token)
    above = lax.ppermute(last, "bin", [(i, i + 1) for i in range(bins - 1)])
    below = lax.ppermute(first, "bin", [(i + 1, i) for i in range(bins - 1)])
    token = grid
    for i in range(1, len(bits)):
        for half in (1, 0):
            token = scatter_more(half, orders[half][i], token)
    smooth = from_grid(grid, above, below, cell, edge_codes, bins, token)
    back = lax.all_to_all(smooth, "bin", split_axis=0, concat_axis=0, tiled=True)
    numer, plain = plain_terms(*parts, factors, smooth)
    own_block = new_factors(payload, back, numer, plain)

    ids = sorted(range(genes_n), key=lambda k: (bin(k).count("1"), k))
    groups = [[k for k in ids if bin(k).count("1") == n] for n in range(len(bits) + 1)]
    chunks = len(ids)
    blocks = {0: own_block}
    for k in bits:
        blocks[k] = swap(own_block, "gene", k)

    def come_on(group, token):
        outs = sent_on([blocks[k & (k - 1)] for k in group], token)
        for k, out in zip(group, outs):
            blocks[k] = swap(out, "gene", k & -k)
        return outs[-1]

    pending = [[None] * len(groups) for _ in range(HALVES)]
    own = [{} for _ in range(HALVES)]
    come = [[] for _ in range(HALVES)]
    ends = [{} for _ in range(HALVES)]

    def product(g, half, *tokens):
        upto = ids.index(groups[g][-1]) + 1
        n_old = upto - len(groups[g])
        parts = cross_part(
            [blocks[k] for k in ids[:upto]], n_old, counts, half, half == 0, width_all, tokens
        )
        pending[half][g] = (parts, [swap(part, "bin", 1) for part in parts])
        return parts[-1]

    def own_chunks(g, half, token):
        arrays = both_cores(*pending[half][g], token)
        for k, array in zip(groups[g], arrays):
            own[half][ids.index(k)] = array
        return arrays[-1]

    def slot(half, t, token):
        before = come[half][-1] if come[half] else None
        got, token = line_slot(flags, t, chunks, own[half], before, token)
        come[half].append(got)
        return token

    def end(c, half, token):
        ends[half][c] = line_end(flags, come[half][c : c + line - 1], token)
        return ends[half][c][0]

    def final(c, before, token, halves=range(HALVES)):
        sums = {h: (own[h][c],) + ends[h][c] for h in halves}
        return new_loadings(share, sums, ids[c], width, me1, before, token)

    def both(step, *args):
        nonlocal token
        for half in range(HALVES):
            token = step(*args, half, token)

    def awaited(arrays, token):
        return tiny_token(list(arrays) + [token])

    token = own_block
    both(product, 0)
    token = awaited([blocks[k] for k in bits], token)
    if len(groups) > 2:
        token = come_on(groups[2], token)
    for half in range(HALVES):
        token = own_chunks(0, half, token)
        token = slot(half, 0, token)
    both(product, 1)
    firsts = {ids.index(group[0]): g for g, group in enumerate(groups)}
    last_slot = chunks + line - 3
    for t in range(1, last_slot + 1):
        if t in firsts:
            arrived = [come[half][-1] for half in range(HALVES)]
            if firsts[t] + 1 < len(groups):
                arrived += [blocks[k] for k in groups[firsts[t] + 1]]
            token = awaited(arrived, token)
        for half in range(HALVES):
            if t in firsts:
                token = own_chunks(firsts[t], half, token)
            token = slot(half, t, token)
        g = firsts.get(t, len(groups)) + 1
        if g < len(groups):
            both(product, g)
            if g + 1 < len(groups):
                token = come_on(groups[g + 1], token)
        if t == chunks - 1:
            factors_new, token = turned_back([blocks[k] for k in ids], ids, width, me1, token)
        c = t - (line - 1)
        if c - 1 in ends[0]:
            token = awaited([ends[half][c - 1][1] for half in range(HALVES)], token)
        if 0 <= c < chunks:
            both(end, c)
    rest = [c for c in range(chunks) if c not in ends[0]]
    for c in rest:
        token = end(c, 0, token)
    sums = [(own[0][c],) + ends[0][c] for c in range(chunks)]
    loadings_new = None
    share, token = shares(loadings, sums, ids, counts.shape[1] // HALVES, me1, token)
    for c in rest:
        token = end(c, 1, token)
    for c in range(chunks - 1):
        loadings_new, token = final(c, loadings_new, token)
    for half in range(HALVES):
        loadings_new, token = final(chunks - 1, loadings_new, token, [half])
    return factors_new, loadings_new


def solution(mesh):
    placed = (P("bin", "gene"), P("bin", None), P(None, "gene"), P("bin"), P("bin", None))
    return jax.shard_map(
        on_device,
        mesh=mesh,
        in_specs=placed,
        out_specs=(P("bin", None), P(None, "gene")),
        check_vma=False,
    )
```

```python
import jax
import jax.numpy as jnp
from jax import lax
from jax.experimental import pallas as pl
from jax.experimental.pallas import tpu as pltpu
from jax.sharding import PartitionSpec as P

K = 256
G = 18432
PENALTY = float(G * K) / 64.0
EXTRA = 8
HALVES = 2
STEP = 512
READS = 2
MIB = 1024 * 1024
MINOR = (((1,), (1,)), ((), ()))
PLAIN = (((1,), (0,)), ((), ()))
F32 = jnp.float32
BF16 = jnp.bfloat16
ANY_SPEC = pl.BlockSpec(memory_space=pl.ANY)
VMEM_SPEC = pl.BlockSpec(memory_space=pltpu.VMEM)
SMEM_SPEC = pl.BlockSpec(memory_space=pltpu.SMEM)


def dot(a, b, dims, precision=None):
    return lax.dot_general(a, b, dims, precision=precision, preferred_element_type=F32)


def kernel_call(body, out_shape, us, limit=10, **kw):
    return pl.pallas_call(
        body,
        out_shape=out_shape,
        compiler_params=pltpu.CompilerParams(vmem_limit_bytes=limit * MIB),
        cost_estimate=pl.CostEstimate(flops=0, bytes_accessed=int(us * 3.69e6), transcendentals=0),
        **kw,
    )


def shape(*dims, dtype=F32):
    return jax.ShapeDtypeStruct(dims, dtype)


def pack(factors, position, me, width, bins):
    rows, width_all = factors.shape
    group = rows // bins
    lanes = 128 if width_all % 128 == 0 and 128 % width == 0 else width_all

    def body(me_ref, fac_ref, pos_ref, out_ref, turned):
        turned[...] = fac_ref[...].T
        first = pl.multiple_of(lax.rem(me_ref[0] * width, lanes), width)
        out_ref[0, :width, :] = turned[pl.ds(first, width), :]
        out_ref[0, width:, :] = jnp.broadcast_to(pos_ref[0], (EXTRA, group))

    grid_spec = pltpu.PrefetchScalarGridSpec(
        num_scalar_prefetch=1,
        grid=(bins,),
        in_specs=[
            pl.BlockSpec((group, lanes), lambda t, m: (t, m[0] * width // lanes)),
            pl.BlockSpec((1, 1, group), lambda t, m: (t, 0, 0)),
        ],
        out_specs=pl.BlockSpec((1, width + EXTRA, group), lambda t, m: (t, 0, 0)),
        scratch_shapes=[pltpu.VMEM((lanes, group), F32)],
    )
    return kernel_call(
        body, shape(bins, width + EXTRA, group), 3, grid_spec=grid_spec
    )(me, factors, position.astype(F32).reshape(bins, 1, group))


def to_grid(got, edge_codes, bin_me, token):
    bins, wide, group = got.shape
    width = wide - EXTRA
    grid_rows, grid_cols = edge_codes.shape
    rows = bins * group
    per = 4

    def body(me_ref, got_ref, code_ref, _, grid_ref, first_ref, last_ref, cell_ref, masked):
        block = jnp.concatenate([got_ref[s] for s in range(bins)], axis=1)
        cell = block[width : width + 1].astype(jnp.int32) - me_ref[0] * rows
        cell_ref[...] = cell
        at_row, at_col = cell // grid_cols, cell % grid_cols
        col_hot = jnp.where(
            lax.broadcasted_iota(jnp.int32, (grid_cols, rows), 0) == at_col, 1.0, 0.0
        ).astype(BF16)
        values = block[:width]
        high = values.astype(BF16)
        both = jnp.concatenate([high, (values - high.astype(F32)).astype(BF16)], axis=0)
        scale = code_ref[...].astype(F32) / 8.0
        for r in range(grid_rows):
            at = r % per * 2 * width
            if at == 0:
                for i in range(per):
                    mask = jnp.where(at_row == r + i, 1.0, 0.0).astype(BF16)
                    masked[i * 2 * width : (i + 1) * 2 * width, :] = both * mask
                placed = dot(masked[...], col_hot, MINOR)
            line = placed[at : at + width] + placed[at + width : at + 2 * width]
            row_scale = scale[r : r + 1]
            weighted = jnp.concatenate(
                [line * row_scale, jnp.broadcast_to(row_scale, (EXTRA, grid_cols))], axis=0
            )
            grid_ref[r] = weighted
            if r == 0:
                first_ref[...] = weighted
            if r == grid_rows - 1:
                last_ref[...] = weighted

    return kernel_call(
        body,
        (
            shape(grid_rows, wide, grid_cols),
            shape(wide, grid_cols),
            shape(wide, grid_cols),
            shape(1, rows, dtype=jnp.int32),
        ),
        3,
        limit=12,
        in_specs=[SMEM_SPEC, VMEM_SPEC, VMEM_SPEC, ANY_SPEC],
        out_specs=(VMEM_SPEC,) * 4,
        scratch_shapes=[pltpu.VMEM((per * 2 * width, rows), BF16)],
    )(bin_me, got, edge_codes, token)


def from_grid(grid, above, below, cell, edge_codes, bins, token):
    grid_rows, wide, grid_cols = grid.shape
    rows = cell.shape[1]
    group = rows // bins

    def body(grid_ref, above_ref, below_ref, cell_ref, code_ref, _, out_ref, halves):
        scale = code_ref[...].astype(F32) / 8.0
        lane = lax.broadcasted_iota(jnp.int32, (wide, grid_cols), 1)
        for r in range(grid_rows):
            here = grid_ref[r]
            upper = above_ref[...] if r == 0 else grid_ref[r - 1]
            lower = below_ref[...] if r == grid_rows - 1 else grid_ref[r + 1]
            left = jnp.where(lane == 0, 0.0, pltpu.roll(here, 1, 1))
            right = jnp.where(lane == grid_cols - 1, 0.0, pltpu.roll(here, grid_cols - 1, 1))
            value = scale[r : r + 1] * (left + right + 0.5 * (upper + lower))
            high = value.astype(BF16)
            halves[r * wide : (r + 1) * wide, :grid_cols] = high
            halves[r * wide : (r + 1) * wide, grid_cols:] = (value - high.astype(F32)).astype(BF16)
        cell = cell_ref[...]
        at_row, at_col = cell // grid_cols, cell % grid_cols
        for s in range(bins // 2):
            lo, hi = 2 * s * group, (2 * s + 2) * group
            hot = jnp.where(
                lax.broadcasted_iota(jnp.int32, (grid_cols, hi - lo), 0) == at_col[:, lo:hi], 1.0, 0.0
            ).astype(BF16)
            lines = dot(halves[...], jnp.concatenate([hot, hot], axis=0), PLAIN)
            row_here = at_row[:, lo:hi]
            total = jnp.zeros((wide, hi - lo), F32)
            for r in range(grid_rows):
                total = total + jnp.where(row_here == r, lines[r * wide : (r + 1) * wide], 0.0)
            out_ref[2 * s] = total[:, :group]
            out_ref[2 * s + 1] = total[:, group:]

    return kernel_call(
        body,
        shape(bins, wide, group),
        4,
        in_specs=[VMEM_SPEC] * 5 + [ANY_SPEC],
        out_specs=VMEM_SPEC,
        scratch_shapes=[pltpu.VMEM((grid_rows * wide, 2 * grid_cols), BF16)],
    )(grid, above, below, cell, edge_codes, token)


def numer_part(counts, loadings, me, genes_n, half, send_ids, token):
    rows, genes = counts.shape
    first_call = loadings.dtype == F32
    width_all = loadings.shape[0] if first_call else loadings.shape[1]
    width = width_all // genes_n
    half_rows = rows // 2
    steps = half_rows // STEP
    side = genes // 2
    keep_ids = [k for k in range(genes_n) if k not in send_ids]
    total_cols = half_rows + first_call * width_all

    def body(me_ref, left_ref, right_ref, *refs):
        at = pl.program_id(0)
        firsts = [pl.multiple_of((k ^ me_ref[0]) * width, width) for k in range(genes_n)]
        if first_call:
            load_ref, _, send_ref, keep_ref, load_t, load_bf, load_f, turned, sems = refs

            @pl.when(at == 0)
            def _():
                reads = [
                    pltpu.make_async_copy(
                        load_ref.at[pl.ds(first, width), :],
                        load_f.at[pl.ds(k * width, width), :],
                        sems.at[k],
                    )
                    for k, first in enumerate(firsts)
                ]
                for copy in reads:
                    copy.start()
                for k, copy in enumerate(reads):
                    copy.wait()
                    here = slice(k * width, (k + 1) * width)
                    load_bf[here, :] = load_f[here, :].astype(BF16)
                load_t[...] = load_bf[...].T

        else:
            load_t, _, send_ref, keep_ref = refs

        def put(part, cols):
            for i, k in enumerate(send_ids):
                send_ref[i, :, cols] = part[k * width : (k + 1) * width]
            for i, k in enumerate(keep_ids):
                keep_ref[i, :, cols] = part[k * width : (k + 1) * width]

        part = dot(left_ref[...], load_t[:side, :], PLAIN)
        part = part + dot(right_ref[...], load_t[side:, :], PLAIN)
        put(part.T, pl.ds(pl.multiple_of(at * STEP, STEP), STEP))

        if first_call:

            @pl.when(at == 0)
            def _():
                local = dot(load_bf[...], load_t[...], PLAIN)
                for k, first in enumerate(firsts):
                    turned[pl.ds(first, width), :] = local[k * width : (k + 1) * width]
                put(turned[...].T, slice(half_rows, total_cols))

    out = shape(genes_n // 2, width, total_cols)
    out_spec = pl.BlockSpec((genes_n // 2, width, total_cols), lambda i, m: (0, 0, 0))
    outs, out_specs, scratch = (out, out), (out_spec, out_spec), []
    if first_call:
        outs += (shape(genes, width_all, dtype=BF16),)
        out_specs += (pl.BlockSpec((genes, width_all), lambda i, m: (0, 0)),)
        scratch = [
            pltpu.VMEM((width_all, genes), BF16),
            pltpu.VMEM((width_all, genes), F32),
            pltpu.VMEM((width_all, width_all), F32),
            pltpu.SemaphoreType.DMA((genes_n,)),
        ]
        load_spec = ANY_SPEC
    else:
        load_spec = pl.BlockSpec((genes, width_all), lambda i, m: (0, 0))
    grid_spec = pltpu.PrefetchScalarGridSpec(
        num_scalar_prefetch=1,
        grid=(steps,),
        in_specs=[
            pl.BlockSpec((STEP, side), lambda i, m: (i + half * steps, 0)),
            pl.BlockSpec((STEP, side), lambda i, m: (i + half * steps, 1)),
            load_spec,
            ANY_SPEC,
        ],
        out_specs=out_specs,
        scratch_shapes=scratch,
    )
    return kernel_call(body, outs, 7, limit=36, grid_spec=grid_spec)(me, counts, counts, loadings, token)


def swap(block, axis, bit):
    return lax.ppermute(block, axis, [(i, i ^ bit) for i in range(lax.axis_size(axis))])


def picked_sum(arrays, ids, token):
    _, width, cols = arrays[0].shape
    first, step = ids[0], (ids[1] - ids[0] if len(ids) > 1 else 1)

    def body(*refs):
        total = refs[0][...]
        for ref in refs[1:-2]:
            total = total + ref[...]
        refs[-1][...] = total

    return kernel_call(
        body,
        shape(len(ids), width, cols),
        0.02,
        grid=(len(ids),),
        in_specs=[pl.BlockSpec((1, width, cols), lambda i: (first + step * i, 0, 0))] * len(arrays)
        + [ANY_SPEC],
        out_specs=pl.BlockSpec((1, width, cols), lambda i: (i, 0, 0)),
    )(*arrays, token)


def plain_terms(first, second, factors, token):
    rows, width_all = factors.shape
    width = first[0].shape[1]
    half_rows = rows // 2
    n = len(first)

    def body(*refs):
        fac_ref, _, numer_ref, plain_ref, gram = refs[2 * n :]

        def total(part, cols):
            out = part[0][0, :, cols]
            for ref in part[1:]:
                out = out + ref[0, :, cols]
            return out

        @pl.when(pl.program_id(0) == 0)
        def _():
            gram[...] = total(refs[n : 2 * n], slice(half_rows, half_rows + width_all))
            numer_ref[...] = total(refs[:n], slice(0, half_rows))

        @pl.when(pl.program_id(0) == 1)
        def _():
            numer_ref[...] = total(refs[n : 2 * n], slice(0, half_rows))

        plain_ref[...] = dot(fac_ref[...], gram[...], MINOR, lax.Precision.HIGHEST).T

    out_spec = pl.BlockSpec((width, half_rows), lambda i: (0, i))
    arrays = list(first) + list(second)
    return kernel_call(
        body,
        (pltpu.HBM((width, rows), F32),) * 2,
        4,
        limit=24,
        grid=(2,),
        in_specs=[pl.BlockSpec((1,) + x.shape[1:], lambda i: (0, 0, 0)) for x in arrays]
        + [pl.BlockSpec((half_rows, width_all), lambda i: (i, 0)), ANY_SPEC],
        out_specs=(out_spec, out_spec),
        scratch_shapes=[pltpu.VMEM((width, width_all), F32)],
    )(*arrays, factors, token)


def new_factors(payload, back, numer, plain):
    bins, wide, group = payload.shape
    width = wide - EXTRA

    def body(pay_ref, back_ref, numer_ref, plain_ref, out_ref):
        pay = jnp.concatenate([pay_ref[0], pay_ref[1]], axis=1)
        got = jnp.concatenate([back_ref[0], back_ref[1]], axis=1)
        fac, smooth, degree = pay[:width], got[:width], got[width : width + 1]
        out_ref[...] = (
            fac * (numer_ref[...] + PENALTY * smooth) / (plain_ref[...] + PENALTY * degree * fac)
        )

    pair = pl.BlockSpec((2, wide, group), lambda i: (i, 0, 0))
    cols = pl.BlockSpec((width, 2 * group), lambda i: (0, i))
    return kernel_call(
        body,
        shape(width, bins * group),
        0.02,
        grid=(bins // 2,),
        in_specs=[pair, pair, cols, cols],
        out_specs=cols,
    )(payload, back, numer, plain)


def sent_on(blocks, token):
    n = len(blocks)

    def body(*refs):
        for src, dst in zip(refs[:n], refs[n + 1 :]):
            dst[...] = src[...]

    return kernel_call(
        body,
        tuple(shape(*b.shape) for b in blocks),
        0.02,
        limit=1,
        in_specs=[VMEM_SPEC] * n + [ANY_SPEC],
        out_specs=(VMEM_SPEC,) * n,
    )(*blocks, token)


def turned_back(blocks, ids, width, me, token):
    rows = blocks[0].shape[1]
    width_all = len(ids) * width
    step = 384
    steps = rows // step

    def body(me_ref, *refs):
        out_ref, _, block = refs[-3:]
        for ref, k in zip(refs, ids):
            block[pl.ds(pl.multiple_of((k ^ me_ref[0]) * width, width), width), :] = ref[...]
        out_ref[...] = block[...].T

    grid_spec = pltpu.PrefetchScalarGridSpec(
        num_scalar_prefetch=1,
        grid=(steps,),
        in_specs=[pl.BlockSpec((width, step), lambda i, m: (0, i))] * len(ids) + [ANY_SPEC],
        out_specs=(pl.BlockSpec((step, width_all), lambda i, m: (i, 0)), VMEM_SPEC),
        scratch_shapes=[pltpu.VMEM((width_all, step), F32)],
    )
    outs = (pltpu.HBM((rows, width_all), F32), shape(8, 128))
    return kernel_call(body, outs, 0.02, limit=8, grid_spec=grid_spec)(me, *blocks, token)


def put_rounded(fac, refs, width):
    for j, ref in enumerate(refs):
        fac[j * width : (j + 1) * width, :] = ref[...].astype(BF16)


def near_products(new, fac, width_all):
    near = dot(new, fac, MINOR)
    if near.shape[1] < width_all:
        near = jnp.concatenate([near, jnp.zeros((near.shape[0], width_all - near.shape[1]), F32)], axis=1)
    return near


def first_cross(block, counts, width_all, token):
    width, rows = block.shape
    genes = counts.shape[1]
    cols = genes // HALVES
    step = STEP
    steps = rows // step

    def body(counts_ref, block_ref, _, *refs):
        outs, held, (fac, sems) = refs[:HALVES], refs[HALVES : HALVES + steps], refs[HALVES + steps :]
        copies = [
            pltpu.make_async_copy(
                counts_ref.at[pl.ds(i * step, step), :], held[i], sems.at[i]
            )
            for i in range(steps)
        ]
        for copy in copies:
            copy.start()
        put_rounded(fac, [block_ref], width)
        near = near_products(fac[...], fac[...], width_all)
        for out in outs:
            out[:, cols:] = near
        for i, copy in enumerate(copies):
            copy.wait()
            at = slice(i * step, (i + 1) * step)
            for h, out in enumerate(outs):
                part = dot(fac[:, at], held[i][:, h * cols : (h + 1) * cols], PLAIN)
                out[:, :cols] = part if i == 0 else out[:, :cols] + part

    return kernel_call(
        body,
        (shape(width, cols + width_all),) * HALVES + (pltpu.VMEM((step, genes), BF16),) * steps,
        0.02,
        limit=8,
        in_specs=[ANY_SPEC, VMEM_SPEC, ANY_SPEC],
        out_specs=(VMEM_SPEC,) * (HALVES + steps),
        scratch_shapes=[pltpu.VMEM((width, rows), BF16), pltpu.SemaphoreType.DMA((steps,))],
    )(counts, block, token)


def cross_part(blocks, n_old, held, half, width_all, tokens):
    width, rows = blocks[0].shape
    cols = held[0].shape[1] // HALVES
    steps = 3
    step = cols // steps
    n = len(blocks) - n_old

    def body(*refs):
        pieces, refs = refs[: len(held)], refs[len(held) :]
        outs, fac = refs[-1 - n : -1], refs[-1]
        put_rounded(fac, refs[: len(blocks)], width)
        new = fac[n_old * width :, :]

        def put(part, where):
            for j, out in enumerate(outs):
                out[:, where] = part[j * width : (j + 1) * width]

        for i in range(steps):
            at = slice(half * cols + i * step, half * cols + (i + 1) * step)
            part = None
            for j, piece in enumerate(pieces):
                here = slice(j * piece.shape[0], (j + 1) * piece.shape[0])
                more = dot(new[:, here], piece[:, at], PLAIN)
                part = more if part is None else part + more
            put(part, slice(i * step, (i + 1) * step))
        put(near_products(new, fac[...], width_all), slice(cols, cols + width_all))

    return kernel_call(
        body,
        (shape(width, cols + width_all),) * n,
        0.02,
        limit=8,
        in_specs=[VMEM_SPEC] * (len(held) + len(blocks)) + [ANY_SPEC] * len(tokens),
        out_specs=(VMEM_SPEC,) * n,
        scratch_shapes=[pltpu.VMEM((len(blocks) * width, rows), BF16)],
    )(*held, *blocks, *tokens)


def tiny_token(arrays):
    def body(*refs):
        refs[-1][...] = jnp.zeros(refs[-1].shape, F32)

    return kernel_call(
        body, shape(8, 128), 0.02, limit=1, in_specs=[ANY_SPEC] * len(arrays), out_specs=VMEM_SPEC
    )(*arrays)


def both_cores(parts, came, token):
    n = len(parts)

    def body(*refs):
        for a, b, out in zip(refs[:n], refs[n : 2 * n], refs[2 * n + 1 :]):
            out[...] = a[...] + b[...]

    return kernel_call(
        body,
        tuple(shape(*part.shape) for part in parts),
        0.02,
        limit=1,
        in_specs=[VMEM_SPEC] * (2 * n) + [ANY_SPEC],
        out_specs=(VMEM_SPEC,) * n,
    )(*parts, *came, token)


def line_slot(flags, t, chunks, own, come, token):
    line = lax.axis_size("bin") // 2
    places = [q for q in range(line - 1) if 0 <= t - q < chunks]
    hops = [(2 * q, 2 * q + 2) for q in places]
    hops += [(2 * (line - 1 - q) + 1, 2 * (line - 2 - q) + 1) for q in places]
    if t == 0:
        return lax.ppermute(own[0], "bin", hops), token
    arrays = [own[t - q] for q in places]

    def body(flag_ref, come_ref, _, *refs):
        for i, q in enumerate(places):

            @pl.when(flag_ref[2] == q)
            def _():
                value = refs[i][...]
                refs[-1][...] = value if q == 0 else value + come_ref[...]

    send = kernel_call(
        body,
        shape(*come.shape),
        0.02,
        limit=1,
        in_specs=[SMEM_SPEC, VMEM_SPEC, ANY_SPEC] + [VMEM_SPEC] * len(arrays),
        out_specs=VMEM_SPEC,
    )(flags, come, token, *arrays)
    return lax.ppermute(send, "bin", hops), send


def line_end(flags, come, token):
    def body(flag_ref, _, *refs):
        out = refs[-1]

        @pl.when(flag_ref[2] == 0)
        def _():
            out[...] = jnp.zeros(out.shape, F32)

        for d in range(len(come)):

            @pl.when(flag_ref[2] == d + 1)
            def _():
                out[...] = refs[d][...]

    end = kernel_call(
        body,
        shape(*come[0].shape),
        0.02,
        limit=1,
        in_specs=[SMEM_SPEC, ANY_SPEC] + [VMEM_SPEC] * len(come),
        out_specs=VMEM_SPEC,
    )(flags, token, *come)
    return end, swap(end, "bin", 1)


def shares(loadings, sums, ids, cols, me, token):
    width_all, genes = loadings.shape
    width = width_all // len(ids)
    steps = 6
    step = genes // steps
    arrays = [x for terms in sums for x in terms]

    def body(me_ref, load_ref, *refs):
        out_ref, tiny, load, gram = refs[-4:]
        firsts = [pl.multiple_of((k ^ me_ref[0]) * width, width) for k in ids]

        @pl.when(pl.program_id(0) == 0)
        def _():
            behind = slice(cols, cols + width_all)
            for j in range(len(sums)):
                own, end, other = refs[3 * j : 3 * j + 3]
                gram[j * width : (j + 1) * width, :] = own[:, behind] + (end[:, behind] + other[:, behind])
            low = gram[...]
            row = lax.broadcasted_iota(jnp.int32, low.shape, 0) // width
            col = lax.broadcasted_iota(jnp.int32, low.shape, 1) // width
            gram[...] = jnp.where(col <= row, low, low.T)

        for j, first in enumerate(firsts):
            load[j * width : (j + 1) * width, :] = load_ref[pl.ds(first, width), :]
        value = load[...]
        value = value / dot(gram[...], value, PLAIN, lax.Precision.HIGHEST)
        for j, first in enumerate(firsts):
            out_ref[pl.ds(first, width), :] = value[j * width : (j + 1) * width]

    block = pl.BlockSpec((width_all, step), lambda i, f: (0, i))
    return kernel_call(
        body,
        (shape(width_all, genes), shape(8, 128)),
        0.02,
        limit=12,
        grid_spec=pltpu.PrefetchScalarGridSpec(
            num_scalar_prefetch=1,
            grid=(steps,),
            in_specs=[block] + [VMEM_SPEC] * len(arrays) + [ANY_SPEC],
            out_specs=(block, VMEM_SPEC),
            scratch_shapes=[
                pltpu.VMEM((width_all, step), F32),
                pltpu.VMEM((width_all, width_all), F32),
            ],
        ),
    )(me, loadings, *arrays, token)


def new_loadings(share, parts, k, width, me, before, token):
    width_all, genes = share.shape
    halves = sorted(parts)
    cols = genes // HALVES
    arrays = [x for h in halves for x in parts[h]]

    def body(me_ref, share_ref, _, *refs):
        out_ref = refs[-2]
        at = pl.ds(pl.multiple_of((k ^ me_ref[0]) * width, width), width)
        for i, h in enumerate(halves):
            own, end, other = refs[3 * i : 3 * i + 3]
            here = slice(h * cols, (h + 1) * cols)
            total = own[:, :cols] + (end[:, :cols] + other[:, :cols])
            out_ref[:, i * cols : (i + 1) * cols] = share_ref[at, here] * total

    operands = [me, share, token] + arrays
    specs = [VMEM_SPEC, ANY_SPEC] + [VMEM_SPEC] * len(arrays)
    aliases = {}
    if before is not None:
        operands.append(before)
        specs.append(ANY_SPEC)
        aliases = {len(operands) - 1: 0}
    column = 0 if len(halves) == HALVES else halves[0]
    return kernel_call(
        body,
        (pltpu.HBM((width_all, genes), F32), shape(8, 128)),
        0.02,
        limit=6,
        grid_spec=pltpu.PrefetchScalarGridSpec(
            num_scalar_prefetch=1,
            grid=(1,),
            in_specs=specs,
            out_specs=(
                pl.BlockSpec((width, len(halves) * cols), lambda i, m: (k ^ m[0], column)),
                VMEM_SPEC,
            ),
        ),
        input_output_aliases=aliases,
    )(*operands)


def on_device(counts, factors, loadings, position, edge_codes):
    bins, genes_n = lax.axis_size("bin"), lax.axis_size("gene")
    line = bins // 2
    me, bin_me = lax.axis_index("gene"), lax.axis_index("bin")
    rows, width_all = factors.shape
    width = width_all // genes_n
    scalar = lambda x: jnp.asarray(x, jnp.int32).reshape(1)
    me1, bin1 = scalar(me), scalar(bin_me)
    core, chip = bin1 & 1, bin1 >> 1
    flags = jnp.concatenate([me1, core, jnp.where(core == 0, chip, line - 1 - chip)])
    bits = [1 << b for b in range(genes_n.bit_length() - 1)]

    counts = pltpu.with_memory_space_constraint(counts, pltpu.HBM)
    payload = pack(factors, position, me1, width, bins)
    got = lax.all_to_all(payload, "bin", split_axis=0, concat_axis=0, tiled=True)
    in_hbm = lambda x: pltpu.with_memory_space_constraint(x, pltpu.HBM)

    orders = (bits, bits[::-1])
    token, load = payload, pltpu.with_memory_space_constraint(loadings, pltpu.HBM)
    parts, keeps = [None, None], [None, None]
    for half in (1, 0):
        bit = orders[half][0]
        send_ids = [k for k in range(genes_n) if k & bit]
        keeps[half] = [k for k in range(genes_n) if not k & bit]
        send, keep, *made = numer_part(counts, load, me1, genes_n, half, send_ids, token)
        load = made[0] if made else load
        token = keep
        parts[half] = [keep, swap(send, "gene", bit)]

    def scatter_more(half, bit, token):
        out_ids = [i for i, k in enumerate(keeps[half]) if k & bit]
        in_ids = [i for i, k in enumerate(keeps[half]) if not k & bit]
        keeps[half] = [keeps[half][i] for i in in_ids]
        parts[half] = [in_hbm(x) for x in parts[half]]
        send = picked_sum(parts[half], out_ids, token)
        if len(in_ids) > 1:
            parts[half] = [picked_sum(parts[half], in_ids, send)]
        parts[half] = parts[half] + [swap(send, "gene", bit)]
        return send

    grid, first, last, cell = to_grid(got, edge_codes, bin1, token)
    above = lax.ppermute(last, "bin", [(i, i + 1) for i in range(bins - 1)])
    below = lax.ppermute(first, "bin", [(i + 1, i) for i in range(bins - 1)])
    token = grid
    for i in range(1, len(bits)):
        for half in (1, 0):
            token = scatter_more(half, orders[half][i], token)
    smooth = from_grid(grid, above, below, cell, edge_codes, bins, token)
    back = lax.all_to_all(smooth, "bin", split_axis=0, concat_axis=0, tiled=True)
    numer, plain = plain_terms(*[[in_hbm(x) for x in p] for p in parts], in_hbm(factors), smooth)
    own_block = new_factors(*[in_hbm(x) for x in (payload, back, numer, plain)])

    ids = sorted(range(genes_n), key=lambda k: (bin(k).count("1"), k))
    groups = [[k for k in ids if bin(k).count("1") == n] for n in range(len(bits) + 1)]
    chunks = len(ids)
    blocks = {0: own_block}
    for k in bits:
        blocks[k] = swap(own_block, "gene", k)

    def come_on(group, token):
        outs = sent_on([blocks[k & (k - 1)] for k in group], token)
        for k, out in zip(group, outs):
            blocks[k] = swap(out, "gene", k & -k)
        return outs[-1]

    pending = [[None] * len(groups) for _ in range(HALVES)]
    own = [{} for _ in range(HALVES)]
    come = [[] for _ in range(HALVES)]
    ends = [{} for _ in range(HALVES)]

    def product(g, half, *tokens):
        upto = ids.index(groups[g][-1]) + 1
        n_old = upto - len(groups[g])
        parts = cross_part([blocks[k] for k in ids[:upto]], n_old, held, half, width_all, tokens)
        pending[half][g] = (parts, [swap(part, "bin", 1) for part in parts])
        return parts[-1]

    def own_chunks(g, half, token):
        arrays = both_cores(*pending[half][g], token)
        for k, array in zip(groups[g], arrays):
            own[half][ids.index(k)] = array
        return arrays[-1]

    def slot(half, t, token):
        before = come[half][-1] if come[half] else None
        got, token = line_slot(flags, t, chunks, own[half], before, token)
        come[half].append(got)
        return token

    def end(c, half, token):
        ends[half][c] = line_end(flags, come[half][c : c + line - 1], token)
        return ends[half][c][0]

    def final(c, before, token, halves=range(HALVES)):
        sums = {h: (own[h][c],) + ends[h][c] for h in halves}
        return new_loadings(share, sums, ids[c], width, me1, before, token)

    def both(step, *args):
        nonlocal token
        for half in range(HALVES):
            token = step(*args, half, token)

    def awaited(arrays, token):
        return tiny_token(list(arrays) + [token])

    made = first_cross(own_block, counts, width_all, own_block)
    parts, held = made[:HALVES], made[HALVES:]
    for half in range(HALVES):
        pending[half][0] = ((parts[half],), [swap(parts[half], "bin", 1)])
    token = awaited([blocks[k] for k in bits], parts[-1])
    if len(groups) > 2:
        token = come_on(groups[2], token)
    for half in range(HALVES):
        token = own_chunks(0, half, token)
        token = slot(half, 0, token)
    both(product, 1)
    firsts = {ids.index(group[0]): g for g, group in enumerate(groups)}
    last_slot = chunks + line - 3
    for t in range(1, last_slot + 1):
        if t in firsts and firsts[t] + 1 < len(groups):
            token = awaited([blocks[k] for k in groups[firsts[t] + 1]], token)
            token = awaited([come[half][-1] for half in range(HALVES)], token)
        for half in range(HALVES):
            if t in firsts:
                token = own_chunks(firsts[t], half, token)
            token = slot(half, t, token)
        g = firsts.get(t, len(groups)) + 1
        if g < len(groups):
            both(product, g)
            if g + 1 < len(groups):
                token = come_on(groups[g + 1], token)
        if t == chunks - 1:
            factors_new, token = turned_back([blocks[k] for k in ids], ids, width, me1, token)
        c = t - (line - 1)
        if c - 1 in ends[0]:
            token = awaited([ends[half][c - 1][1] for half in range(HALVES)], token)
        if 0 <= c < chunks:
            both(end, c)
    rest = [c for c in range(chunks) if c not in ends[0]]
    for c in rest:
        token = end(c, 0, token)
    sums = [(own[0][c],) + ends[0][c] for c in range(chunks)]
    loadings_new = None
    share, token = shares(loadings, sums, ids, counts.shape[1] // HALVES, me1, token)
    for c in rest:
        token = end(c, 1, token)
    for c in range(chunks - 1):
        loadings_new, token = final(c, loadings_new, token)
    for half in range(HALVES):
        loadings_new, token = final(chunks - 1, loadings_new, token, [half])
    return factors_new, loadings_new


def solution(mesh):
    placed = (P("bin", "gene"), P("bin", None), P(None, "gene"), P("bin"), P("bin", None))
    return jax.shard_map(
        on_device,
        mesh=mesh,
        in_specs=placed,
        out_specs=(P("bin", None), P(None, "gene")),
        check_vma=False,
    )
```

```python
import jax
import jax.numpy as jnp
from jax import lax
from jax.experimental import pallas as pl
from jax.experimental.pallas import tpu as pltpu
from jax.sharding import PartitionSpec as P

K = 256
G = 18432
PENALTY = float(G * K) / 64.0
EXTRA = 8
HALVES = 2
STEP = 512
READS = 2
MIB = 1024 * 1024
MINOR = (((1,), (1,)), ((), ()))
PLAIN = (((1,), (0,)), ((), ()))
F32 = jnp.float32
BF16 = jnp.bfloat16
ANY_SPEC = pl.BlockSpec(memory_space=pl.ANY)
VMEM_SPEC = pl.BlockSpec(memory_space=pltpu.VMEM)
SMEM_SPEC = pl.BlockSpec(memory_space=pltpu.SMEM)


def dot(a, b, dims, precision=None):
    return lax.dot_general(a, b, dims, precision=precision, preferred_element_type=F32)


def kernel_call(body, out_shape, us, limit=10, **kw):
    return pl.pallas_call(
        body,
        out_shape=out_shape,
        compiler_params=pltpu.CompilerParams(vmem_limit_bytes=limit * MIB),
        cost_estimate=pl.CostEstimate(flops=0, bytes_accessed=int(us * 3.69e6), transcendentals=0),
        **kw,
    )


def shape(*dims, dtype=F32):
    return jax.ShapeDtypeStruct(dims, dtype)


def pack(factors, position, me, width, bins):
    rows, width_all = factors.shape
    group = rows // bins
    lanes = 128 if width_all % 128 == 0 and 128 % width == 0 else width_all

    def body(me_ref, fac_ref, pos_ref, out_ref, turned):
        turned[...] = fac_ref[...].T
        first = pl.multiple_of(lax.rem(me_ref[0] * width, lanes), width)
        out_ref[0, :width, :] = turned[pl.ds(first, width), :]
        out_ref[0, width:, :] = jnp.broadcast_to(pos_ref[0], (EXTRA, group))

    grid_spec = pltpu.PrefetchScalarGridSpec(
        num_scalar_prefetch=1,
        grid=(bins,),
        in_specs=[
            pl.BlockSpec((group, lanes), lambda t, m: (t, m[0] * width // lanes)),
            pl.BlockSpec((1, 1, group), lambda t, m: (t, 0, 0)),
        ],
        out_specs=pl.BlockSpec((1, width + EXTRA, group), lambda t, m: (t, 0, 0)),
        scratch_shapes=[pltpu.VMEM((lanes, group), F32)],
    )
    return kernel_call(
        body, shape(bins, width + EXTRA, group), 3, grid_spec=grid_spec
    )(me, factors, position.astype(F32).reshape(bins, 1, group))


def to_grid(got, edge_codes, bin_me, token):
    bins, wide, group = got.shape
    width = wide - EXTRA
    grid_rows, grid_cols = edge_codes.shape
    rows = bins * group
    per = 4

    def body(me_ref, got_ref, code_ref, _, grid_ref, first_ref, last_ref, cell_ref, masked):
        block = jnp.concatenate([got_ref[s] for s in range(bins)], axis=1)
        cell = block[width : width + 1].astype(jnp.int32) - me_ref[0] * rows
        cell_ref[...] = cell
        at_row, at_col = cell // grid_cols, cell % grid_cols
        col_hot = jnp.where(
            lax.broadcasted_iota(jnp.int32, (grid_cols, rows), 0) == at_col, 1.0, 0.0
        ).astype(BF16)
        values = block[:width]
        high = values.astype(BF16)
        both = jnp.concatenate([high, (values - high.astype(F32)).astype(BF16)], axis=0)
        scale = code_ref[...].astype(F32) / 8.0
        for r in range(grid_rows):
            at = r % per * 2 * width
            if at == 0:
                for i in range(per):
                    mask = jnp.where(at_row == r + i, 1.0, 0.0).astype(BF16)
                    masked[i * 2 * width : (i + 1) * 2 * width, :] = both * mask
                placed = dot(masked[...], col_hot, MINOR)
            line = placed[at : at + width] + placed[at + width : at + 2 * width]
            row_scale = scale[r : r + 1]
            weighted = jnp.concatenate(
                [line * row_scale, jnp.broadcast_to(row_scale, (EXTRA, grid_cols))], axis=0
            )
            grid_ref[r] = weighted
            if r == 0:
                first_ref[...] = weighted
            if r == grid_rows - 1:
                last_ref[...] = weighted

    return kernel_call(
        body,
        (
            shape(grid_rows, wide, grid_cols),
            shape(wide, grid_cols),
            shape(wide, grid_cols),
            shape(1, rows, dtype=jnp.int32),
        ),
        3,
        limit=12,
        in_specs=[SMEM_SPEC, VMEM_SPEC, VMEM_SPEC, ANY_SPEC],
        out_specs=(VMEM_SPEC,) * 4,
        scratch_shapes=[pltpu.VMEM((per * 2 * width, rows), BF16)],
    )(bin_me, got, edge_codes, token)


def from_grid(grid, above, below, cell, edge_codes, bins, token):
    grid_rows, wide, grid_cols = grid.shape
    rows = cell.shape[1]
    group = rows // bins

    def body(grid_ref, above_ref, below_ref, cell_ref, code_ref, _, out_ref, halves):
        scale = code_ref[...].astype(F32) / 8.0
        lane = lax.broadcasted_iota(jnp.int32, (wide, grid_cols), 1)
        for r in range(grid_rows):
            here = grid_ref[r]
            upper = above_ref[...] if r == 0 else grid_ref[r - 1]
            lower = below_ref[...] if r == grid_rows - 1 else grid_ref[r + 1]
            left = jnp.where(lane == 0, 0.0, pltpu.roll(here, 1, 1))
            right = jnp.where(lane == grid_cols - 1, 0.0, pltpu.roll(here, grid_cols - 1, 1))
            value = scale[r : r + 1] * (left + right + 0.5 * (upper + lower))
            high = value.astype(BF16)
            halves[r * wide : (r + 1) * wide, :grid_cols] = high
            halves[r * wide : (r + 1) * wide, grid_cols:] = (value - high.astype(F32)).astype(BF16)
        cell = cell_ref[...]
        at_row, at_col = cell // grid_cols, cell % grid_cols
        for s in range(bins // 2):
            lo, hi = 2 * s * group, (2 * s + 2) * group
            hot = jnp.where(
                lax.broadcasted_iota(jnp.int32, (grid_cols, hi - lo), 0) == at_col[:, lo:hi], 1.0, 0.0
            ).astype(BF16)
            lines = dot(halves[...], jnp.concatenate([hot, hot], axis=0), PLAIN)
            row_here = at_row[:, lo:hi]
            total = jnp.zeros((wide, hi - lo), F32)
            for r in range(grid_rows):
                total = total + jnp.where(row_here == r, lines[r * wide : (r + 1) * wide], 0.0)
            out_ref[2 * s] = total[:, :group]
            out_ref[2 * s + 1] = total[:, group:]

    return kernel_call(
        body,
        shape(bins, wide, group),
        4,
        in_specs=[VMEM_SPEC] * 5 + [ANY_SPEC],
        out_specs=VMEM_SPEC,
        scratch_shapes=[pltpu.VMEM((grid_rows * wide, 2 * grid_cols), BF16)],
    )(grid, above, below, cell, edge_codes, token)


def numer_part(counts, loadings, me, genes_n, half, send_ids, token):
    rows, genes = counts.shape
    first_call = loadings.dtype == F32
    width_all = loadings.shape[0] if first_call else loadings.shape[1]
    width = width_all // genes_n
    half_rows = rows // 2
    piece = STEP // 2
    pieces = half_rows // piece
    keep_ids = [k for k in range(genes_n) if k not in send_ids]
    total_cols = half_rows + first_call * width_all

    def body(me_ref, counts_ref, *refs):
        firsts = [pl.multiple_of((k ^ me_ref[0]) * width, width) for k in range(genes_n)]
        if first_call:
            load_ref, _, send_ref, keep_ref, load_t, held, sems, load_bf, load_f, turned = refs
        else:
            load_t, _, send_ref, keep_ref, held, sems = refs
        copies = [
            pltpu.make_async_copy(
                counts_ref.at[pl.ds(half * half_rows + i * piece, piece), :],
                held.at[pl.ds(i * piece, piece), :],
                sems.at[i],
            )
            for i in range(pieces)
        ]

        def put(part, cols):
            for i, k in enumerate(send_ids):
                send_ref[i, :, cols] = part[k * width : (k + 1) * width]
            for i, k in enumerate(keep_ids):
                keep_ref[i, :, cols] = part[k * width : (k + 1) * width]

        if first_call:
            reads = [
                pltpu.make_async_copy(
                    load_ref.at[pl.ds(first, width), :],
                    load_f.at[pl.ds(k * width, width), :],
                    sems.at[pieces + k],
                )
                for k, first in enumerate(firsts)
            ]
            for copy in reads + copies:
                copy.start()
            for k, copy in enumerate(reads):
                copy.wait()
                here = slice(k * width, (k + 1) * width)
                load_bf[here, :] = load_f[here, :].astype(BF16)
            load_t[...] = load_bf[...].T
            local = dot(load_bf[...], load_t[...], PLAIN)
            for k, first in enumerate(firsts):
                turned[pl.ds(first, width), :] = local[k * width : (k + 1) * width]
            put(turned[...].T, slice(half_rows, total_cols))
        else:
            for copy in copies:
                copy.start()
        for i in range(0, pieces, 2):
            copies[i].wait()
            copies[i + 1].wait()
            at = slice(i * piece, (i + 2) * piece)
            put(dot(held[at, :], load_t[...], PLAIN).T, at)

    outs = (shape(genes_n // 2, width, total_cols),) * 2
    scratch = [pltpu.VMEM((half_rows, genes), BF16), pltpu.SemaphoreType.DMA((pieces + genes_n,))]
    if first_call:
        outs += (shape(genes, width_all, dtype=BF16),)
        scratch += [
            pltpu.VMEM((width_all, genes), BF16),
            pltpu.VMEM((width_all, genes), F32),
            pltpu.VMEM((width_all, width_all), F32),
        ]
    return kernel_call(
        body,
        outs,
        7,
        limit=36,
        in_specs=[SMEM_SPEC, ANY_SPEC, ANY_SPEC if first_call else VMEM_SPEC, ANY_SPEC],
        out_specs=(VMEM_SPEC,) * len(outs),
        scratch_shapes=scratch,
    )(me, counts, loadings, token)


def swap(block, axis, bit):
    return lax.ppermute(block, axis, [(i, i ^ bit) for i in range(lax.axis_size(axis))])


def picked_sum(arrays, ids, token):
    _, width, cols = arrays[0].shape
    first, step = ids[0], (ids[1] - ids[0] if len(ids) > 1 else 1)

    def body(*refs):
        total = refs[0][...]
        for ref in refs[1:-2]:
            total = total + ref[...]
        refs[-1][...] = total

    return kernel_call(
        body,
        shape(len(ids), width, cols),
        0.02,
        grid=(len(ids),),
        in_specs=[pl.BlockSpec((1, width, cols), lambda i: (first + step * i, 0, 0))] * len(arrays)
        + [ANY_SPEC],
        out_specs=pl.BlockSpec((1, width, cols), lambda i: (i, 0, 0)),
    )(*arrays, token)


def plain_terms(first, second, factors, token):
    rows, width_all = factors.shape
    width = first[0].shape[1]
    half_rows = rows // 2
    n = len(first)

    def body(*refs):
        fac_ref, _, numer_ref, plain_ref, gram = refs[2 * n :]

        def total(part, cols):
            out = part[0][0, :, cols]
            for ref in part[1:]:
                out = out + ref[0, :, cols]
            return out

        @pl.when(pl.program_id(0) == 0)
        def _():
            gram[...] = total(refs[n : 2 * n], slice(half_rows, half_rows + width_all))
            numer_ref[...] = total(refs[:n], slice(0, half_rows))

        @pl.when(pl.program_id(0) == 1)
        def _():
            numer_ref[...] = total(refs[n : 2 * n], slice(0, half_rows))

        plain_ref[...] = dot(fac_ref[...], gram[...], MINOR, lax.Precision.HIGHEST).T

    out_spec = pl.BlockSpec((width, half_rows), lambda i: (0, i))
    arrays = list(first) + list(second)
    return kernel_call(
        body,
        (pltpu.HBM((width, rows), F32),) * 2,
        4,
        limit=24,
        grid=(2,),
        in_specs=[pl.BlockSpec((1,) + x.shape[1:], lambda i: (0, 0, 0)) for x in arrays]
        + [pl.BlockSpec((half_rows, width_all), lambda i: (i, 0)), ANY_SPEC],
        out_specs=(out_spec, out_spec),
        scratch_shapes=[pltpu.VMEM((width, width_all), F32)],
    )(*arrays, factors, token)


def new_factors(payload, back, numer, plain):
    bins, wide, group = payload.shape
    width = wide - EXTRA

    def body(pay_ref, back_ref, numer_ref, plain_ref, out_ref):
        pay = jnp.concatenate([pay_ref[0], pay_ref[1]], axis=1)
        got = jnp.concatenate([back_ref[0], back_ref[1]], axis=1)
        fac, smooth, degree = pay[:width], got[:width], got[width : width + 1]
        out_ref[...] = (
            fac * (numer_ref[...] + PENALTY * smooth) / (plain_ref[...] + PENALTY * degree * fac)
        )

    pair = pl.BlockSpec((2, wide, group), lambda i: (i, 0, 0))
    cols = pl.BlockSpec((width, 2 * group), lambda i: (0, i))
    return kernel_call(
        body,
        shape(width, bins * group),
        0.02,
        grid=(bins // 2,),
        in_specs=[pair, pair, cols, cols],
        out_specs=cols,
    )(payload, back, numer, plain)


def sent_on(sources, token):
    n = len(sources)
    width, rows = sources[0][0].shape
    half_rows = rows // 2

    def body(*refs):
        for (_, half), src, dst in zip(sources, refs[:n], refs[n + 1 :]):
            dst[...] = src[:, half * half_rows : (half + 1) * half_rows]

    return kernel_call(
        body,
        (shape(width, half_rows),) * n,
        0.02,
        limit=1,
        in_specs=[VMEM_SPEC] * n + [ANY_SPEC],
        out_specs=(VMEM_SPEC,) * n,
    )(*[block for block, _ in sources], token)


def joined(halves, token):
    n = len(halves)
    width, half_rows = halves[0][0].shape

    def body(*refs):
        for i in range(n):
            for j in range(2):
                refs[2 * n + 1 + i][:, j * half_rows : (j + 1) * half_rows] = refs[2 * i + j][...]

    return kernel_call(
        body,
        (shape(width, 2 * half_rows),) * n,
        0.02,
        limit=1,
        in_specs=[VMEM_SPEC] * (2 * n) + [ANY_SPEC],
        out_specs=(VMEM_SPEC,) * n,
    )(*[x for pair in halves for x in pair], token)


def turned_back(blocks, ids, width, me, token):
    rows = blocks[0].shape[1]
    width_all = len(ids) * width
    step = 384
    steps = rows // step

    def body(me_ref, *refs):
        out_ref, _, block = refs[-3:]
        for ref, k in zip(refs, ids):
            block[pl.ds(pl.multiple_of((k ^ me_ref[0]) * width, width), width), :] = ref[...]
        out_ref[...] = block[...].T

    grid_spec = pltpu.PrefetchScalarGridSpec(
        num_scalar_prefetch=1,
        grid=(steps,),
        in_specs=[pl.BlockSpec((width, step), lambda i, m: (0, i))] * len(ids) + [ANY_SPEC],
        out_specs=(pl.BlockSpec((step, width_all), lambda i, m: (i, 0)), VMEM_SPEC),
        scratch_shapes=[pltpu.VMEM((width_all, step), F32)],
    )
    outs = (pltpu.HBM((rows, width_all), F32), shape(8, 128))
    return kernel_call(body, outs, 0.02, limit=8, grid_spec=grid_spec)(me, *blocks, token)


def put_rounded(fac, refs, width):
    for j, ref in enumerate(refs):
        fac[j * width : (j + 1) * width, :] = ref[...].astype(BF16)


def near_products(new, fac, width_all):
    near = dot(new, fac, MINOR)
    if near.shape[1] < width_all:
        near = jnp.concatenate([near, jnp.zeros((near.shape[0], width_all - near.shape[1]), F32)], axis=1)
    return near


def first_cross(block, counts, width_all, token):
    width, rows = block.shape
    genes = counts.shape[1]
    cols = genes // HALVES
    step = STEP
    steps = rows // step

    def body(counts_ref, block_ref, _, *refs):
        outs, held, (fac, sems) = refs[:HALVES], refs[HALVES : HALVES + steps], refs[HALVES + steps :]
        copies = [
            pltpu.make_async_copy(
                counts_ref.at[pl.ds(i * step, step), :], held[i], sems.at[i]
            )
            for i in range(steps)
        ]
        for copy in copies:
            copy.start()
        put_rounded(fac, [block_ref], width)
        near = near_products(fac[...], fac[...], width_all)
        for out in outs:
            out[:, cols:] = near
        for i, copy in enumerate(copies):
            copy.wait()
            at = slice(i * step, (i + 1) * step)
            for h, out in enumerate(outs):
                part = dot(fac[:, at], held[i][:, h * cols : (h + 1) * cols], PLAIN)
                out[:, :cols] = part if i == 0 else out[:, :cols] + part

    return kernel_call(
        body,
        (shape(width, cols + width_all),) * HALVES + (pltpu.VMEM((step, genes), BF16),) * steps,
        0.02,
        limit=8,
        in_specs=[ANY_SPEC, VMEM_SPEC, ANY_SPEC],
        out_specs=(VMEM_SPEC,) * (HALVES + steps),
        scratch_shapes=[pltpu.VMEM((width, rows), BF16), pltpu.SemaphoreType.DMA((steps,))],
    )(counts, block, token)


def cross_part(blocks, n_old, held, half, width_all, tokens):
    width, rows = blocks[0].shape
    cols = held[0].shape[1] // HALVES
    steps = 3
    step = cols // steps
    n = len(blocks) - n_old

    def body(*refs):
        pieces, refs = refs[: len(held)], refs[len(held) :]
        outs, fac = refs[-1 - n : -1], refs[-1]
        put_rounded(fac, refs[: len(blocks)], width)
        new = fac[n_old * width :, :]

        def put(part, where):
            for j, out in enumerate(outs):
                out[:, where] = part[j * width : (j + 1) * width]

        for i in range(steps):
            at = slice(half * cols + i * step, half * cols + (i + 1) * step)
            part = None
            for j, piece in enumerate(pieces):
                here = slice(j * piece.shape[0], (j + 1) * piece.shape[0])
                more = dot(new[:, here], piece[:, at], PLAIN)
                part = more if part is None else part + more
            put(part, slice(i * step, (i + 1) * step))
        put(near_products(new, fac[...], width_all), slice(cols, cols + width_all))

    return kernel_call(
        body,
        (shape(width, cols + width_all),) * n,
        0.02,
        limit=8,
        in_specs=[VMEM_SPEC] * (len(held) + len(blocks)) + [ANY_SPEC] * len(tokens),
        out_specs=(VMEM_SPEC,) * n,
        scratch_shapes=[pltpu.VMEM((len(blocks) * width, rows), BF16)],
    )(*held, *blocks, *tokens)


def tiny_token(arrays):
    def body(*refs):
        refs[-1][...] = jnp.zeros(refs[-1].shape, F32)

    return kernel_call(
        body, shape(8, 128), 0.02, limit=1, in_specs=[ANY_SPEC] * len(arrays), out_specs=VMEM_SPEC
    )(*arrays)


def both_cores(parts, came, token):
    n = len(parts)

    def body(*refs):
        for a, b, out in zip(refs[:n], refs[n : 2 * n], refs[2 * n + 1 :]):
            out[...] = a[...] + b[...]

    return kernel_call(
        body,
        tuple(shape(*part.shape) for part in parts),
        0.02,
        limit=1,
        in_specs=[VMEM_SPEC] * (2 * n) + [ANY_SPEC],
        out_specs=(VMEM_SPEC,) * n,
    )(*parts, *came, token)


def line_slot(flags, t, chunks, own, come, token):
    line = lax.axis_size("bin") // 2
    places = [q for q in range(line - 1) if 0 <= t - q < chunks]
    hops = [(2 * q, 2 * q + 2) for q in places]
    hops += [(2 * (line - 1 - q) + 1, 2 * (line - 2 - q) + 1) for q in places]
    if t == 0:
        return lax.ppermute(own[0], "bin", hops), token
    arrays = [own[t - q] for q in places]

    def body(flag_ref, come_ref, _, *refs):
        for i, q in enumerate(places):

            @pl.when(flag_ref[2] == q)
            def _():
                value = refs[i][...]
                refs[-1][...] = value if q == 0 else value + come_ref[...]

    send = kernel_call(
        body,
        shape(*come.shape),
        0.02,
        limit=1,
        in_specs=[SMEM_SPEC, VMEM_SPEC, ANY_SPEC] + [VMEM_SPEC] * len(arrays),
        out_specs=VMEM_SPEC,
    )(flags, come, token, *arrays)
    return lax.ppermute(send, "bin", hops), send


def line_end(flags, come, token):
    def body(flag_ref, _, *refs):
        out = refs[-1]

        @pl.when(flag_ref[2] == 0)
        def _():
            out[...] = jnp.zeros(out.shape, F32)

        for d in range(len(come)):

            @pl.when(flag_ref[2] == d + 1)
            def _():
                out[...] = refs[d][...]

    end = kernel_call(
        body,
        shape(*come[0].shape),
        0.02,
        limit=1,
        in_specs=[SMEM_SPEC, ANY_SPEC] + [VMEM_SPEC] * len(come),
        out_specs=VMEM_SPEC,
    )(flags, token, *come)
    return end, swap(end, "bin", 1)


def split(x):
    high = x.astype(BF16)
    return high, (x - high.astype(F32)).astype(BF16)


def shares(loadings, sums, ids, cols, me, token):
    width_all, genes = loadings.shape
    width = width_all // len(ids)
    steps = 6
    step = genes // steps
    arrays = [x for terms in sums for x in terms]

    def body(me_ref, load_ref, *refs):
        out_ref, tiny, load, gram = refs[-4:]
        firsts = [pl.multiple_of((k ^ me_ref[0]) * width, width) for k in ids]

        @pl.when(pl.program_id(0) == 0)
        def _():
            behind = slice(cols, cols + width_all)
            for j in range(len(sums)):
                own, end, other = refs[3 * j : 3 * j + 3]
                gram[j * width : (j + 1) * width, :] = own[:, behind] + (end[:, behind] + other[:, behind])
            low = gram[...]
            row = lax.broadcasted_iota(jnp.int32, low.shape, 0) // width
            col = lax.broadcasted_iota(jnp.int32, low.shape, 1) // width
            gram[...] = jnp.where(col <= row, low, low.T)

        for j, first in enumerate(firsts):
            load[j * width : (j + 1) * width, :] = load_ref[pl.ds(first, width), :]
        value = load[...]
        (gram_hi, gram_lo), (hi, lo) = split(gram[...]), split(value)
        value = value / (dot(gram_hi, hi, PLAIN) + (dot(gram_hi, lo, PLAIN) + dot(gram_lo, hi, PLAIN)))
        for j, first in enumerate(firsts):
            out_ref[pl.ds(first, width), :] = value[j * width : (j + 1) * width]

    block = pl.BlockSpec((width_all, step), lambda i, f: (0, i))
    return kernel_call(
        body,
        (shape(width_all, genes), shape(8, 128)),
        0.02,
        limit=12,
        grid_spec=pltpu.PrefetchScalarGridSpec(
            num_scalar_prefetch=1,
            grid=(steps,),
            in_specs=[block] + [VMEM_SPEC] * len(arrays) + [ANY_SPEC],
            out_specs=(block, VMEM_SPEC),
            scratch_shapes=[
                pltpu.VMEM((width_all, step), F32),
                pltpu.VMEM((width_all, width_all), F32),
            ],
        ),
    )(me, loadings, *arrays, token)


def new_loadings(share, parts, k, width, me, before, token):
    width_all, genes = share.shape
    halves = sorted(parts)
    cols = genes // HALVES
    arrays = [x for h in halves for x in parts[h]]

    def body(me_ref, share_ref, _, *refs):
        out_ref = refs[-2]
        at = pl.ds(pl.multiple_of((k ^ me_ref[0]) * width, width), width)
        for i, h in enumerate(halves):
            own, end, other = refs[3 * i : 3 * i + 3]
            here = slice(h * cols, (h + 1) * cols)
            total = own[:, :cols] + (end[:, :cols] + other[:, :cols])
            out_ref[:, i * cols : (i + 1) * cols] = share_ref[at, here] * total

    operands = [me, share, token] + arrays
    specs = [VMEM_SPEC, ANY_SPEC] + [VMEM_SPEC] * len(arrays)
    aliases = {}
    if before is not None:
        operands.append(before)
        specs.append(ANY_SPEC)
        aliases = {len(operands) - 1: 0}
    column = 0 if len(halves) == HALVES else halves[0]
    return kernel_call(
        body,
        (pltpu.HBM((width_all, genes), F32), shape(8, 128)),
        0.02,
        limit=6,
        grid_spec=pltpu.PrefetchScalarGridSpec(
            num_scalar_prefetch=1,
            grid=(1,),
            in_specs=specs,
            out_specs=(
                pl.BlockSpec((width, len(halves) * cols), lambda i, m: (k ^ m[0], column)),
                VMEM_SPEC,
            ),
        ),
        input_output_aliases=aliases,
    )(*operands)


def on_device(counts, factors, loadings, position, edge_codes):
    bins, genes_n = lax.axis_size("bin"), lax.axis_size("gene")
    line = bins // 2
    me, bin_me = lax.axis_index("gene"), lax.axis_index("bin")
    rows, width_all = factors.shape
    width = width_all // genes_n
    scalar = lambda x: jnp.asarray(x, jnp.int32).reshape(1)
    me1, bin1 = scalar(me), scalar(bin_me)
    core, chip = bin1 & 1, bin1 >> 1
    flags = jnp.concatenate([me1, core, jnp.where(core == 0, chip, line - 1 - chip)])
    bits = [1 << b for b in range(genes_n.bit_length() - 1)]

    counts = pltpu.with_memory_space_constraint(counts, pltpu.HBM)
    payload = pack(factors, position, me1, width, bins)
    got = lax.all_to_all(payload, "bin", split_axis=0, concat_axis=0, tiled=True)
    in_hbm = lambda x: pltpu.with_memory_space_constraint(x, pltpu.HBM)

    orders = (bits, bits[::-1])
    token, load = payload, pltpu.with_memory_space_constraint(loadings, pltpu.HBM)
    parts, keeps = [None, None], [None, None]
    for half in (1, 0):
        bit = orders[half][0]
        send_ids = [k for k in range(genes_n) if k & bit]
        keeps[half] = [k for k in range(genes_n) if not k & bit]
        send, keep, *made = numer_part(counts, load, me1, genes_n, half, send_ids, token)
        load = made[0] if made else load
        token = keep
        parts[half] = [keep, swap(send, "gene", bit)]

    def scatter_more(half, bit, token):
        out_ids = [i for i, k in enumerate(keeps[half]) if k & bit]
        in_ids = [i for i, k in enumerate(keeps[half]) if not k & bit]
        keeps[half] = [keeps[half][i] for i in in_ids]
        parts[half] = [in_hbm(x) for x in parts[half]]
        send = picked_sum(parts[half], out_ids, token)
        if len(in_ids) > 1:
            parts[half] = [picked_sum(parts[half], in_ids, send)]
        parts[half] = parts[half] + [swap(send, "gene", bit)]
        return send

    grid, first, last, cell = to_grid(got, edge_codes, bin1, token)
    above = lax.ppermute(last, "bin", [(i, i + 1) for i in range(bins - 1)])
    below = lax.ppermute(first, "bin", [(i + 1, i) for i in range(bins - 1)])
    token = grid
    for i in range(1, len(bits)):
        for half in (1, 0):
            token = scatter_more(half, orders[half][i], token)
    smooth = from_grid(grid, above, below, cell, edge_codes, bins, token)
    back = lax.all_to_all(smooth, "bin", split_axis=0, concat_axis=0, tiled=True)
    numer, plain = plain_terms(*[[in_hbm(x) for x in p] for p in parts], in_hbm(factors), smooth)
    own_block = new_factors(*[in_hbm(x) for x in (payload, back, numer, plain)])

    ids = sorted(range(genes_n), key=lambda k: (bin(k).count("1"), k))
    groups = [[k for k in ids if bin(k).count("1") == n] for n in range(len(bits) + 1)]
    chunks = len(ids)
    blocks = {0: own_block}
    for k in bits:
        blocks[k] = swap(own_block, "gene", k)

    coming = {}

    def come_on(group, token):
        axes = [(k & -k, 1 << (k.bit_length() - 1)) for k in group]
        sources = [(blocks[k ^ bit], j) for k, pair in zip(group, axes) for j, bit in enumerate(pair)]
        outs = sent_on(sources, token)
        for i, (k, pair) in enumerate(zip(group, axes)):
            coming[k] = [swap(outs[2 * i + j], "gene", bit) for j, bit in enumerate(pair)]
        return outs[-1]

    pending = [[None] * len(groups) for _ in range(HALVES)]
    own = [{} for _ in range(HALVES)]
    come = [[] for _ in range(HALVES)]
    ends = [{} for _ in range(HALVES)]

    def product(g, half, *tokens):
        upto = ids.index(groups[g][-1]) + 1
        n_old = upto - len(groups[g])
        parts = cross_part([blocks[k] for k in ids[:upto]], n_old, held, half, width_all, tokens)
        pending[half][g] = (parts, [swap(part, "bin", 1) for part in parts])
        return parts[-1]

    def own_chunks(g, half, token):
        arrays = both_cores(*pending[half][g], token)
        for k, array in zip(groups[g], arrays):
            own[half][ids.index(k)] = array
        return arrays[-1]

    def slot(half, t, token):
        before = come[half][-1] if come[half] else None
        got, token = line_slot(flags, t, chunks, own[half], before, token)
        come[half].append(got)
        return token

    def end(c, half, token):
        ends[half][c] = line_end(flags, come[half][c : c + line - 1], token)
        return ends[half][c][0]

    def final(c, before, token, halves=range(HALVES)):
        sums = {h: (own[h][c],) + ends[h][c] for h in halves}
        return new_loadings(share, sums, ids[c], width, me1, before, token)

    def both(step, *args):
        nonlocal token
        for half in range(HALVES):
            token = step(*args, half, token)

    def awaited(arrays, token):
        return tiny_token(list(arrays) + [token])

    made = first_cross(own_block, counts, width_all, own_block)
    parts, held = made[:HALVES], made[HALVES:]
    for half in range(HALVES):
        pending[half][0] = ((parts[half],), [swap(parts[half], "bin", 1)])
    token = awaited([blocks[k] for k in bits], parts[-1])
    if len(groups) > 2:
        token = come_on(groups[2], token)
    for half in range(HALVES):
        token = own_chunks(0, half, token)
        token = slot(half, 0, token)
    both(product, 1)
    firsts = {ids.index(group[0]): g for g, group in enumerate(groups)}
    last_slot = chunks + line - 3
    for t in range(1, last_slot + 1):
        if t in firsts and firsts[t] + 1 < len(groups):
            later = groups[firsts[t] + 1]
            for k, block in zip(later, joined([coming[k] for k in later], token)):
                blocks[k] = token = block
            token = awaited([come[half][-1] for half in range(HALVES)], token)
        for half in range(HALVES):
            if t in firsts:
                token = own_chunks(firsts[t], half, token)
            token = slot(half, t, token)
        g = firsts.get(t, len(groups)) + 1
        if g < len(groups):
            both(product, g)
            if g + 1 < len(groups):
                token = come_on(groups[g + 1], token)
        if t == chunks - 1:
            factors_new, token = turned_back([blocks[k] for k in ids], ids, width, me1, token)
        c = t - (line - 1)
        if c - 1 in ends[0]:
            token = awaited([ends[half][c - 1][1] for half in range(HALVES)], token)
        if 0 <= c < chunks:
            both(end, c)
    rest = [c for c in range(chunks) if c not in ends[0]]
    for c in rest:
        both(end, c)
    sums = [(own[0][c],) + ends[0][c] for c in range(chunks)]
    loadings_new = None
    share, token = shares(loadings, sums, ids, counts.shape[1] // HALVES, me1, token)
    for c in range(chunks - 1):
        loadings_new, token = final(c, loadings_new, token)
    for half in range(HALVES):
        loadings_new, token = final(chunks - 1, loadings_new, token, [half])
    return factors_new, loadings_new


def solution(mesh):
    placed = (P("bin", "gene"), P("bin", None), P(None, "gene"), P("bin"), P("bin", None))
    return jax.shard_map(
        on_device,
        mesh=mesh,
        in_specs=placed,
        out_specs=(P("bin", None), P(None, "gene")),
        check_vma=False,
    )
```

```python
import jax
import jax.numpy as jnp
from jax import lax
from jax.experimental import pallas as pl
from jax.experimental.pallas import tpu as pltpu
from jax.sharding import PartitionSpec as P

K = 256
G = 18432
PENALTY = float(G * K) / 64.0
EXTRA = 8
HALVES = 2
STEP = 512
READS = 2
MIB = 1024 * 1024
MINOR = (((1,), (1,)), ((), ()))
PLAIN = (((1,), (0,)), ((), ()))
F32 = jnp.float32
BF16 = jnp.bfloat16
ANY_SPEC = pl.BlockSpec(memory_space=pl.ANY)
VMEM_SPEC = pl.BlockSpec(memory_space=pltpu.VMEM)
SMEM_SPEC = pl.BlockSpec(memory_space=pltpu.SMEM)


def dot(a, b, dims, precision=None):
    return lax.dot_general(a, b, dims, precision=precision, preferred_element_type=F32)


def kernel_call(body, out_shape, us, limit=10, **kw):
    return pl.pallas_call(
        body,
        out_shape=out_shape,
        compiler_params=pltpu.CompilerParams(vmem_limit_bytes=limit * MIB),
        cost_estimate=pl.CostEstimate(flops=0, bytes_accessed=int(us * 3.69e6), transcendentals=0),
        **kw,
    )


def shape(*dims, dtype=F32):
    return jax.ShapeDtypeStruct(dims, dtype)


def pack(factors, position, me, width, bins):
    rows, width_all = factors.shape
    group = rows // bins
    lanes = 128 if width_all % 128 == 0 and 128 % width == 0 else width_all

    def body(me_ref, fac_ref, pos_ref, out_ref, turned):
        turned[...] = fac_ref[...].T
        first = pl.multiple_of(lax.rem(me_ref[0] * width, lanes), width)
        out_ref[0, :width, :] = turned[pl.ds(first, width), :]
        out_ref[0, width:, :] = jnp.broadcast_to(pos_ref[0], (EXTRA, group))

    grid_spec = pltpu.PrefetchScalarGridSpec(
        num_scalar_prefetch=1,
        grid=(bins,),
        in_specs=[
            pl.BlockSpec((group, lanes), lambda t, m: (t, m[0] * width // lanes)),
            pl.BlockSpec((1, 1, group), lambda t, m: (t, 0, 0)),
        ],
        out_specs=pl.BlockSpec((1, width + EXTRA, group), lambda t, m: (t, 0, 0)),
        scratch_shapes=[pltpu.VMEM((lanes, group), F32)],
    )
    return kernel_call(
        body, shape(bins, width + EXTRA, group), 3, grid_spec=grid_spec
    )(me, factors, position.astype(F32).reshape(bins, 1, group))


def to_grid(got, edge_codes, bin_me, token):
    bins, wide, group = got.shape
    width = wide - EXTRA
    grid_rows, grid_cols = edge_codes.shape
    rows = bins * group
    per = 4

    def body(me_ref, got_ref, code_ref, _, grid_ref, first_ref, last_ref, cell_ref, masked):
        block = jnp.concatenate([got_ref[s] for s in range(bins)], axis=1)
        cell = block[width : width + 1].astype(jnp.int32) - me_ref[0] * rows
        cell_ref[...] = cell
        at_row, at_col = cell // grid_cols, cell % grid_cols
        col_hot = jnp.where(
            lax.broadcasted_iota(jnp.int32, (grid_cols, rows), 0) == at_col, 1.0, 0.0
        ).astype(BF16)
        values = block[:width]
        high = values.astype(BF16)
        both = jnp.concatenate([high, (values - high.astype(F32)).astype(BF16)], axis=0)
        scale = code_ref[...].astype(F32) / 8.0
        for r in range(grid_rows):
            at = r % per * 2 * width
            if at == 0:
                for i in range(per):
                    mask = jnp.where(at_row == r + i, 1.0, 0.0).astype(BF16)
                    masked[i * 2 * width : (i + 1) * 2 * width, :] = both * mask
                placed = dot(masked[...], col_hot, MINOR)
            line = placed[at : at + width] + placed[at + width : at + 2 * width]
            row_scale = scale[r : r + 1]
            weighted = jnp.concatenate(
                [line * row_scale, jnp.broadcast_to(row_scale, (EXTRA, grid_cols))], axis=0
            )
            grid_ref[r] = weighted
            if r == 0:
                first_ref[...] = weighted
            if r == grid_rows - 1:
                last_ref[...] = weighted

    return kernel_call(
        body,
        (
            shape(grid_rows, wide, grid_cols),
            shape(wide, grid_cols),
            shape(wide, grid_cols),
            shape(1, rows, dtype=jnp.int32),
        ),
        3,
        limit=12,
        in_specs=[SMEM_SPEC, VMEM_SPEC, VMEM_SPEC, ANY_SPEC],
        out_specs=(VMEM_SPEC,) * 4,
        scratch_shapes=[pltpu.VMEM((per * 2 * width, rows), BF16)],
    )(bin_me, got, edge_codes, token)


def from_grid(grid, above, below, cell, edge_codes, bins, token):
    grid_rows, wide, grid_cols = grid.shape
    rows = cell.shape[1]
    group = rows // bins

    def body(grid_ref, above_ref, below_ref, cell_ref, code_ref, _, out_ref, halves):
        scale = code_ref[...].astype(F32) / 8.0
        lane = lax.broadcasted_iota(jnp.int32, (wide, grid_cols), 1)
        for r in range(grid_rows):
            here = grid_ref[r]
            upper = above_ref[...] if r == 0 else grid_ref[r - 1]
            lower = below_ref[...] if r == grid_rows - 1 else grid_ref[r + 1]
            left = jnp.where(lane == 0, 0.0, pltpu.roll(here, 1, 1))
            right = jnp.where(lane == grid_cols - 1, 0.0, pltpu.roll(here, grid_cols - 1, 1))
            value = scale[r : r + 1] * (left + right + 0.5 * (upper + lower))
            high = value.astype(BF16)
            halves[r * wide : (r + 1) * wide, :grid_cols] = high
            halves[r * wide : (r + 1) * wide, grid_cols:] = (value - high.astype(F32)).astype(BF16)
        cell = cell_ref[...]
        at_row, at_col = cell // grid_cols, cell % grid_cols
        for s in range(bins // 2):
            lo, hi = 2 * s * group, (2 * s + 2) * group
            hot = jnp.where(
                lax.broadcasted_iota(jnp.int32, (grid_cols, hi - lo), 0) == at_col[:, lo:hi], 1.0, 0.0
            ).astype(BF16)
            lines = dot(halves[...], jnp.concatenate([hot, hot], axis=0), PLAIN)
            row_here = at_row[:, lo:hi]
            total = jnp.zeros((wide, hi - lo), F32)
            for r in range(grid_rows):
                total = total + jnp.where(row_here == r, lines[r * wide : (r + 1) * wide], 0.0)
            out_ref[2 * s] = total[:, :group]
            out_ref[2 * s + 1] = total[:, group:]

    return kernel_call(
        body,
        shape(bins, wide, group),
        4,
        in_specs=[VMEM_SPEC] * 5 + [ANY_SPEC],
        out_specs=VMEM_SPEC,
        scratch_shapes=[pltpu.VMEM((grid_rows * wide, 2 * grid_cols), BF16)],
    )(grid, above, below, cell, edge_codes, token)


def numer_part(counts, loadings, gram, me, genes_n, part, send_ids, token):
    rows, genes = counts.shape
    first_call = loadings.dtype == F32
    width_all = loadings.shape[0] if first_call else loadings.shape[1]
    width = width_all // genes_n
    start, some_rows = part
    piece = STEP // 2
    pieces = some_rows // piece
    keep_ids = [k for k in range(genes_n) if k not in send_ids]
    total_cols = some_rows + (not first_call) * width_all

    def body(me_ref, counts_ref, *refs):
        firsts = [pl.multiple_of((k ^ me_ref[0]) * width, width) for k in range(genes_n)]
        if first_call:
            load_ref, _, send_ref, keep_ref, load_t, gram_ref, held, sems, load_bf, load_f = refs
        else:
            load_t, gram_ref, _, send_ref, keep_ref, held, sems = refs
        copies = [
            pltpu.make_async_copy(
                counts_ref.at[pl.ds(start + i * piece, piece), :],
                held.at[pl.ds(i * piece, piece), :],
                sems.at[i],
            )
            for i in range(pieces)
        ]

        def put(part, cols):
            for i, k in enumerate(send_ids):
                send_ref[i, :, cols] = part[k * width : (k + 1) * width]
            for i, k in enumerate(keep_ids):
                keep_ref[i, :, cols] = part[k * width : (k + 1) * width]

        if first_call:
            reads = [
                pltpu.make_async_copy(
                    load_ref.at[pl.ds(first, width), :],
                    load_f.at[pl.ds(k * width, width), :],
                    sems.at[pieces + k],
                )
                for k, first in enumerate(firsts)
            ]
            for copy in reads + copies:
                copy.start()
            for k, copy in enumerate(reads):
                copy.wait()
                here = slice(k * width, (k + 1) * width)
                load_bf[here, :] = load_f[here, :].astype(BF16)
            load_t[...] = load_bf[...].T
            local = dot(load_bf[...], load_t[...], PLAIN)
            for k, first in enumerate(firsts):
                gram_ref[pl.ds(first, width), :] = local[k * width : (k + 1) * width]
        else:
            for copy in copies:
                copy.start()
            put(gram_ref[...].T, slice(some_rows, total_cols))
        for i in range(0, pieces, 2):
            copies[i].wait()
            copies[i + 1].wait()
            at = slice(i * piece, (i + 2) * piece)
            put(dot(held[at, :], load_t[...], PLAIN).T, at)

    outs = (shape(genes_n // 2, width, total_cols),) * 2
    scratch = [pltpu.VMEM((some_rows, genes), BF16), pltpu.SemaphoreType.DMA((pieces + genes_n,))]
    if first_call:
        outs += (shape(genes, width_all, dtype=BF16), shape(width_all, width_all))
        scratch += [
            pltpu.VMEM((width_all, genes), BF16),
            pltpu.VMEM((width_all, genes), F32),
        ]
    loads = [loadings] if first_call else [loadings, gram]
    return kernel_call(
        body,
        outs,
        7,
        limit=40,
        in_specs=[SMEM_SPEC, ANY_SPEC]
        + [ANY_SPEC if first_call else VMEM_SPEC] * len(loads)
        + [ANY_SPEC],
        out_specs=(VMEM_SPEC,) * len(outs),
        scratch_shapes=scratch,
    )(me, counts, *loads, token)


def swap(block, axis, bit):
    return lax.ppermute(block, axis, [(i, i ^ bit) for i in range(lax.axis_size(axis))])


def picked_sum(arrays, ids, token):
    _, width, cols = arrays[0].shape
    first, step = ids[0], (ids[1] - ids[0] if len(ids) > 1 else 1)

    def body(*refs):
        total = refs[0][...]
        for ref in refs[1:-2]:
            total = total + ref[...]
        refs[-1][...] = total

    return kernel_call(
        body,
        shape(len(ids), width, cols),
        0.02,
        grid=(len(ids),),
        in_specs=[pl.BlockSpec((1, width, cols), lambda i: (first + step * i, 0, 0))] * len(arrays)
        + [ANY_SPEC],
        out_specs=pl.BlockSpec((1, width, cols), lambda i: (i, 0, 0)),
    )(*arrays, token)


def plain_terms(first, second, factors, token):
    rows, width_all = factors.shape
    width = first[0].shape[1]
    third = rows // 3
    n = len(first)

    def body(*refs):
        fac_ref, _, numer_ref, plain_ref, gram = refs[2 * n :]

        def total(part, cols):
            out = part[0][0, :, cols]
            for ref in part[1:]:
                out = out + ref[0, :, cols]
            return out

        @pl.when(pl.program_id(0) == 0)
        def _():
            gram[...] = total(refs[:n], slice(third, third + width_all))
            numer_ref[...] = total(refs[:n], slice(0, third))

        for i in (1, 2):

            @pl.when(pl.program_id(0) == i)
            def _():
                numer_ref[...] = total(refs[n : 2 * n], slice((i - 1) * third, i * third))

        plain_ref[...] = dot(fac_ref[...], gram[...], MINOR, lax.Precision.HIGHEST).T

    out_spec = pl.BlockSpec((width, third), lambda i: (0, i))
    arrays = list(first) + list(second)
    return kernel_call(
        body,
        (pltpu.HBM((width, rows), F32),) * 2,
        4,
        limit=24,
        grid=(3,),
        in_specs=[pl.BlockSpec((1,) + x.shape[1:], lambda i: (0, 0, 0)) for x in arrays]
        + [pl.BlockSpec((third, width_all), lambda i: (i, 0)), ANY_SPEC],
        out_specs=(out_spec, out_spec),
        scratch_shapes=[pltpu.VMEM((width, width_all), F32)],
    )(*arrays, factors, token)


def new_factors(payload, back, numer, plain):
    bins, wide, group = payload.shape
    width = wide - EXTRA

    def body(pay_ref, back_ref, numer_ref, plain_ref, out_ref):
        pay = jnp.concatenate([pay_ref[0], pay_ref[1]], axis=1)
        got = jnp.concatenate([back_ref[0], back_ref[1]], axis=1)
        fac, smooth, degree = pay[:width], got[:width], got[width : width + 1]
        out_ref[...] = (
            fac * (numer_ref[...] + PENALTY * smooth) / (plain_ref[...] + PENALTY * degree * fac)
        )

    pair = pl.BlockSpec((2, wide, group), lambda i: (i, 0, 0))
    cols = pl.BlockSpec((width, 2 * group), lambda i: (0, i))
    return kernel_call(
        body,
        shape(width, bins * group),
        0.02,
        grid=(bins // 2,),
        in_specs=[pair, pair, cols, cols],
        out_specs=cols,
    )(payload, back, numer, plain)


def sent_on(sources, token):
    n = len(sources)
    width, rows = sources[0][0].shape
    half_rows = rows // 2

    def body(*refs):
        for (_, half), src, dst in zip(sources, refs[:n], refs[n + 1 :]):
            dst[...] = src[:, half * half_rows : (half + 1) * half_rows]

    return kernel_call(
        body,
        (shape(width, half_rows),) * n,
        0.02,
        limit=1,
        in_specs=[VMEM_SPEC] * n + [ANY_SPEC],
        out_specs=(VMEM_SPEC,) * n,
    )(*[block for block, _ in sources], token)


def joined(halves, token):
    n = len(halves)
    width, half_rows = halves[0][0].shape

    def body(*refs):
        for i in range(n):
            for j in range(2):
                refs[2 * n + 1 + i][:, j * half_rows : (j + 1) * half_rows] = refs[2 * i + j][...]

    return kernel_call(
        body,
        (shape(width, 2 * half_rows),) * n,
        0.02,
        limit=1,
        in_specs=[VMEM_SPEC] * (2 * n) + [ANY_SPEC],
        out_specs=(VMEM_SPEC,) * n,
    )(*[x for pair in halves for x in pair], token)


def turned_back(blocks, ids, width, me, token):
    rows = blocks[0].shape[1]
    width_all = len(ids) * width
    step = 384
    steps = rows // step

    def body(me_ref, *refs):
        out_ref, _, block = refs[-3:]
        for ref, k in zip(refs, ids):
            block[pl.ds(pl.multiple_of((k ^ me_ref[0]) * width, width), width), :] = ref[...]
        out_ref[...] = block[...].T

    grid_spec = pltpu.PrefetchScalarGridSpec(
        num_scalar_prefetch=1,
        grid=(steps,),
        in_specs=[pl.BlockSpec((width, step), lambda i, m: (0, i))] * len(ids) + [ANY_SPEC],
        out_specs=(pl.BlockSpec((step, width_all), lambda i, m: (i, 0)), VMEM_SPEC),
        scratch_shapes=[pltpu.VMEM((width_all, step), F32)],
    )
    outs = (pltpu.HBM((rows, width_all), F32), shape(8, 128))
    return kernel_call(body, outs, 0.02, limit=8, grid_spec=grid_spec)(me, *blocks, token)


def put_rounded(fac, refs, width):
    for j, ref in enumerate(refs):
        fac[j * width : (j + 1) * width, :] = ref[...].astype(BF16)


def near_products(new, fac, width_all):
    near = dot(new, fac, MINOR)
    if near.shape[1] < width_all:
        near = jnp.concatenate([near, jnp.zeros((near.shape[0], width_all - near.shape[1]), F32)], axis=1)
    return near


def first_cross(block, counts, width_all, token):
    width, rows = block.shape
    genes = counts.shape[1]
    cols, extra = genes // HALVES, width_all // HALVES
    step = STEP
    steps = rows // step

    def body(counts_ref, block_ref, _, *refs):
        outs, held, (fac, sems) = refs[:HALVES], refs[HALVES : HALVES + steps], refs[HALVES + steps :]
        copies = [
            pltpu.make_async_copy(
                counts_ref.at[pl.ds(i * step, step), :], held[i], sems.at[i]
            )
            for i in range(steps)
        ]
        for copy in copies:
            copy.start()
        put_rounded(fac, [block_ref], width)
        near = near_products(fac[...], fac[...], width_all)
        for h, out in enumerate(outs):
            out[:, cols:] = near[:, h * extra : (h + 1) * extra]
        for i, copy in enumerate(copies):
            copy.wait()
            at = slice(i * step, (i + 1) * step)
            for h, out in enumerate(outs):
                part = dot(fac[:, at], held[i][:, h * cols : (h + 1) * cols], PLAIN)
                out[:, :cols] = part if i == 0 else out[:, :cols] + part

    return kernel_call(
        body,
        (shape(width, cols + extra),) * HALVES + (pltpu.VMEM((step, genes), BF16),) * steps,
        0.02,
        limit=8,
        in_specs=[ANY_SPEC, VMEM_SPEC, ANY_SPEC],
        out_specs=(VMEM_SPEC,) * (HALVES + steps),
        scratch_shapes=[pltpu.VMEM((width, rows), BF16), pltpu.SemaphoreType.DMA((steps,))],
    )(counts, block, token)


def cross_part(blocks, n_old, held, half, width_all, tokens):
    width, rows = blocks[0].shape
    cols, extra = held[0].shape[1] // HALVES, width_all // HALVES
    steps = 3
    step = cols // steps
    n = len(blocks) - n_old

    def body(*refs):
        pieces, refs = refs[: len(held)], refs[len(held) :]
        outs, fac = refs[-1 - n : -1], refs[-1]
        put_rounded(fac, refs[: len(blocks)], width)
        new = fac[n_old * width :, :]

        def put(part, where):
            for j, out in enumerate(outs):
                out[:, where] = part[j * width : (j + 1) * width]

        for i in range(steps):
            at = slice(half * cols + i * step, half * cols + (i + 1) * step)
            part = None
            for j, piece in enumerate(pieces):
                here = slice(j * piece.shape[0], (j + 1) * piece.shape[0])
                more = dot(new[:, here], piece[:, at], PLAIN)
                part = more if part is None else part + more
            put(part, slice(i * step, (i + 1) * step))
        near = near_products(new, fac[...], width_all)
        put(near[:, half * extra : (half + 1) * extra], slice(cols, cols + extra))

    return kernel_call(
        body,
        (shape(width, cols + extra),) * n,
        0.02,
        limit=8,
        in_specs=[VMEM_SPEC] * (len(held) + len(blocks)) + [ANY_SPEC] * len(tokens),
        out_specs=(VMEM_SPEC,) * n,
        scratch_shapes=[pltpu.VMEM((len(blocks) * width, rows), BF16)],
    )(*held, *blocks, *tokens)


def tiny_token(arrays):
    def body(*refs):
        refs[-1][...] = jnp.zeros(refs[-1].shape, F32)

    return kernel_call(
        body, shape(8, 128), 0.02, limit=1, in_specs=[ANY_SPEC] * len(arrays), out_specs=VMEM_SPEC
    )(*arrays)


def both_cores(parts, came, token):
    n = len(parts)

    def body(*refs):
        for a, b, out in zip(refs[:n], refs[n : 2 * n], refs[2 * n + 1 :]):
            out[...] = a[...] + b[...]

    return kernel_call(
        body,
        tuple(shape(*part.shape) for part in parts),
        0.02,
        limit=1,
        in_specs=[VMEM_SPEC] * (2 * n) + [ANY_SPEC],
        out_specs=(VMEM_SPEC,) * n,
    )(*parts, *came, token)


def line_slot(flags, t, chunks, own, come, token):
    line = lax.axis_size("bin") // 2
    places = [q for q in range(line - 1) if 0 <= t - q < chunks]
    hops = [(2 * q, 2 * q + 2) for q in places]
    hops += [(2 * (line - 1 - q) + 1, 2 * (line - 2 - q) + 1) for q in places]
    if t == 0:
        return lax.ppermute(own[0], "bin", hops), token
    arrays = [own[t - q] for q in places]

    def body(flag_ref, come_ref, _, *refs):
        for i, q in enumerate(places):

            @pl.when(flag_ref[2] == q)
            def _():
                value = refs[i][...]
                refs[-1][...] = value if q == 0 else value + come_ref[...]

    send = kernel_call(
        body,
        shape(*come.shape),
        0.02,
        limit=1,
        in_specs=[SMEM_SPEC, VMEM_SPEC, ANY_SPEC] + [VMEM_SPEC] * len(arrays),
        out_specs=VMEM_SPEC,
    )(flags, come, token, *arrays)
    return lax.ppermute(send, "bin", hops), send


def line_end(flags, come, token):
    def body(flag_ref, _, *refs):
        out = refs[-1]

        @pl.when(flag_ref[2] == 0)
        def _():
            out[...] = jnp.zeros(out.shape, F32)

        for d in range(len(come)):

            @pl.when(flag_ref[2] == d + 1)
            def _():
                out[...] = refs[d][...]

    end = kernel_call(
        body,
        shape(*come[0].shape),
        0.02,
        limit=1,
        in_specs=[SMEM_SPEC, ANY_SPEC] + [VMEM_SPEC] * len(come),
        out_specs=VMEM_SPEC,
    )(flags, token, *come)
    return end, swap(end, "bin", 1)


def split(x):
    high = x.astype(BF16)
    return high, (x - high.astype(F32)).astype(BF16)


def shares(loadings, sums, ids, cols, me, token):
    width_all, genes = loadings.shape
    width = width_all // len(ids)
    steps = 6
    step = genes // steps
    extra = width_all // HALVES
    arrays = [x for pair in sums for terms in pair for x in terms]

    def body(me_ref, load_ref, *refs):
        out_ref, tiny, load, gram = refs[-4:]
        firsts = [pl.multiple_of((k ^ me_ref[0]) * width, width) for k in ids]

        @pl.when(pl.program_id(0) == 0)
        def _():
            behind = slice(cols, cols + extra)
            for i in range(len(sums) * HALVES):
                own, end, other = refs[3 * i : 3 * i + 3]
                j, h = i // HALVES, i % HALVES
                gram[j * width : (j + 1) * width, h * extra : (h + 1) * extra] = own[:, behind] + (
                    end[:, behind] + other[:, behind]
                )
            low = gram[...]
            row = lax.broadcasted_iota(jnp.int32, low.shape, 0) // width
            col = lax.broadcasted_iota(jnp.int32, low.shape, 1) // width
            gram[...] = jnp.where(col <= row, low, low.T)

        for j, first in enumerate(firsts):
            load[j * width : (j + 1) * width, :] = load_ref[pl.ds(first, width), :]
        value = load[...]
        (gram_hi, gram_lo), (hi, lo) = split(gram[...]), split(value)
        value = value / (dot(gram_hi, hi, PLAIN) + (dot(gram_hi, lo, PLAIN) + dot(gram_lo, hi, PLAIN)))
        for j, first in enumerate(firsts):
            out_ref[pl.ds(first, width), :] = value[j * width : (j + 1) * width]

    block = pl.BlockSpec((width_all, step), lambda i, f: (0, i))
    return kernel_call(
        body,
        (shape(width_all, genes), shape(8, 128)),
        0.02,
        limit=12,
        grid_spec=pltpu.PrefetchScalarGridSpec(
            num_scalar_prefetch=1,
            grid=(steps,),
            in_specs=[block] + [VMEM_SPEC] * len(arrays) + [ANY_SPEC],
            out_specs=(block, VMEM_SPEC),
            scratch_shapes=[
                pltpu.VMEM((width_all, step), F32),
                pltpu.VMEM((width_all, width_all), F32),
            ],
        ),
    )(me, loadings, *arrays, token)


def new_loadings(share, parts, k, width, me, before, token):
    width_all, genes = share.shape
    halves = sorted(parts)
    cols = genes // HALVES
    arrays = [x for h in halves for x in parts[h]]

    def body(me_ref, share_ref, _, *refs):
        out_ref = refs[-2]
        at = pl.ds(pl.multiple_of((k ^ me_ref[0]) * width, width), width)
        for i, h in enumerate(halves):
            own, end, other = refs[3 * i : 3 * i + 3]
            here = slice(h * cols, (h + 1) * cols)
            total = own[:, :cols] + (end[:, :cols] + other[:, :cols])
            out_ref[:, i * cols : (i + 1) * cols] = share_ref[at, here] * total

    operands = [me, share, token] + arrays
    specs = [VMEM_SPEC, ANY_SPEC] + [VMEM_SPEC] * len(arrays)
    aliases = {}
    if before is not None:
        operands.append(before)
        specs.append(ANY_SPEC)
        aliases = {len(operands) - 1: 0}
    column = 0 if len(halves) == HALVES else halves[0]
    return kernel_call(
        body,
        (pltpu.HBM((width_all, genes), F32), shape(8, 128)),
        0.02,
        limit=6,
        grid_spec=pltpu.PrefetchScalarGridSpec(
            num_scalar_prefetch=1,
            grid=(1,),
            in_specs=specs,
            out_specs=(
                pl.BlockSpec((width, len(halves) * cols), lambda i, m: (k ^ m[0], column)),
                VMEM_SPEC,
            ),
        ),
        input_output_aliases=aliases,
    )(*operands)


def on_device(counts, factors, loadings, position, edge_codes):
    bins, genes_n = lax.axis_size("bin"), lax.axis_size("gene")
    line = bins // 2
    me, bin_me = lax.axis_index("gene"), lax.axis_index("bin")
    rows, width_all = factors.shape
    width = width_all // genes_n
    scalar = lambda x: jnp.asarray(x, jnp.int32).reshape(1)
    me1, bin1 = scalar(me), scalar(bin_me)
    core, chip = bin1 & 1, bin1 >> 1
    flags = jnp.concatenate([me1, core, jnp.where(core == 0, chip, line - 1 - chip)])
    bits = [1 << b for b in range(genes_n.bit_length() - 1)]

    counts = pltpu.with_memory_space_constraint(counts, pltpu.HBM)
    payload = pack(factors, position, me1, width, bins)
    got = lax.all_to_all(payload, "bin", split_axis=0, concat_axis=0, tiled=True)
    in_hbm = lambda x: pltpu.with_memory_space_constraint(x, pltpu.HBM)

    orders = (bits, bits[::-1])
    token, load = payload, pltpu.with_memory_space_constraint(loadings, pltpu.HBM)
    parts, keeps, gram = [None, None], [None, None], None
    third = rows // 3
    numer_parts = ((0, third), (third, rows - third))
    for half in (1, 0):
        bit = orders[half][0]
        send_ids = [k for k in range(genes_n) if k & bit]
        keeps[half] = [k for k in range(genes_n) if not k & bit]
        send, keep, *made = numer_part(
            counts, load, gram, me1, genes_n, numer_parts[half], send_ids, token
        )
        load, gram = made or (load, gram)
        token = keep
        parts[half] = [keep, swap(send, "gene", bit)]

    def scatter_more(half, bit, token):
        out_ids = [i for i, k in enumerate(keeps[half]) if k & bit]
        in_ids = [i for i, k in enumerate(keeps[half]) if not k & bit]
        keeps[half] = [keeps[half][i] for i in in_ids]
        parts[half] = [in_hbm(x) for x in parts[half]]
        send = picked_sum(parts[half], out_ids, token)
        if len(in_ids) > 1:
            parts[half] = [picked_sum(parts[half], in_ids, send)]
        parts[half] = parts[half] + [swap(send, "gene", bit)]
        return send

    grid, first, last, cell = to_grid(got, edge_codes, bin1, token)
    above = lax.ppermute(last, "bin", [(i, i + 1) for i in range(bins - 1)])
    below = lax.ppermute(first, "bin", [(i + 1, i) for i in range(bins - 1)])
    token = grid
    for i in range(1, len(bits)):
        for half in (1, 0):
            token = scatter_more(half, orders[half][i], token)
    smooth = from_grid(grid, above, below, cell, edge_codes, bins, token)
    back = lax.all_to_all(smooth, "bin", split_axis=0, concat_axis=0, tiled=True)
    numer, plain = plain_terms(*[[in_hbm(x) for x in p] for p in parts], in_hbm(factors), smooth)
    own_block = new_factors(*[in_hbm(x) for x in (payload, back, numer, plain)])

    ids = sorted(range(genes_n), key=lambda k: (bin(k).count("1"), k))
    groups = [[k for k in ids if bin(k).count("1") == n] for n in range(len(bits) + 1)]
    chunks = len(ids)
    blocks = {0: own_block}
    for k in bits:
        blocks[k] = swap(own_block, "gene", k)

    coming = {}

    def come_on(group, token):
        axes = [(k & -k, 1 << (k.bit_length() - 1)) for k in group]
        sources = [(blocks[k ^ bit], j) for k, pair in zip(group, axes) for j, bit in enumerate(pair)]
        outs = sent_on(sources, token)
        for i, (k, pair) in enumerate(zip(group, axes)):
            coming[k] = [swap(outs[2 * i + j], "gene", bit) for j, bit in enumerate(pair)]
        return outs[-1]

    pending = [[None] * len(groups) for _ in range(HALVES)]
    own = [{} for _ in range(HALVES)]
    come = [[] for _ in range(HALVES)]
    ends = [{} for _ in range(HALVES)]

    def product(g, half, *tokens):
        upto = ids.index(groups[g][-1]) + 1
        n_old = upto - len(groups[g])
        parts = cross_part([blocks[k] for k in ids[:upto]], n_old, held, half, width_all, tokens)
        pending[half][g] = (parts, [swap(part, "bin", 1) for part in parts])
        return parts[-1]

    def own_chunks(g, half, token):
        arrays = both_cores(*pending[half][g], token)
        for k, array in zip(groups[g], arrays):
            own[half][ids.index(k)] = array
        return arrays[-1]

    def slot(half, t, token):
        before = come[half][-1] if come[half] else None
        got, token = line_slot(flags, t, chunks, own[half], before, token)
        come[half].append(got)
        return token

    def end(c, half, token):
        ends[half][c] = line_end(flags, come[half][c : c + line - 1], token)
        return ends[half][c][0]

    def final(c, before, token, halves=range(HALVES)):
        sums = {h: (own[h][c],) + ends[h][c] for h in halves}
        return new_loadings(share, sums, ids[c], width, me1, before, token)

    def both(step, *args):
        nonlocal token
        for half in range(HALVES):
            token = step(*args, half, token)

    def awaited(arrays, token):
        return tiny_token(list(arrays) + [token])

    made = first_cross(own_block, counts, width_all, own_block)
    parts, held = made[:HALVES], made[HALVES:]
    for half in range(HALVES):
        pending[half][0] = ((parts[half],), [swap(parts[half], "bin", 1)])
    token = awaited([blocks[k] for k in bits], parts[-1])
    if len(groups) > 2:
        token = come_on(groups[2], token)
    for half in range(HALVES):
        token = own_chunks(0, half, token)
        token = slot(half, 0, token)
    both(product, 1)
    firsts = {ids.index(group[0]): g for g, group in enumerate(groups)}
    last_slot = chunks + line - 3
    for t in range(1, last_slot + 1):
        if t in firsts and firsts[t] + 1 < len(groups):
            later = groups[firsts[t] + 1]
            for k, block in zip(later, joined([coming[k] for k in later], token)):
                blocks[k] = token = block
            token = awaited([come[half][-1] for half in range(HALVES)], token)
        for half in range(HALVES):
            if t in firsts:
                token = own_chunks(firsts[t], half, token)
            token = slot(half, t, token)
        g = firsts.get(t, len(groups)) + 1
        if g < len(groups):
            both(product, g)
            if g + 1 < len(groups):
                token = come_on(groups[g + 1], token)
        if t == chunks - 1:
            factors_new, token = turned_back([blocks[k] for k in ids], ids, width, me1, token)
        c = t - (line - 1)
        if c - 1 in ends[0]:
            token = awaited([ends[half][c - 1][1] for half in range(HALVES)], token)
        if 0 <= c < chunks:
            both(end, c)
    rest = [c for c in range(chunks) if c not in ends[0]]
    for c in rest:
        both(end, c)
    sums = [[(own[h][c],) + ends[h][c] for h in range(HALVES)] for c in range(chunks)]
    loadings_new = None
    share, token = shares(loadings, sums, ids, counts.shape[1] // HALVES, me1, token)
    for c in range(chunks - 1):
        loadings_new, token = final(c, loadings_new, token)
    for half in range(HALVES):
        loadings_new, token = final(chunks - 1, loadings_new, token, [half])
    return factors_new, loadings_new


def solution(mesh):
    placed = (P("bin", "gene"), P("bin", None), P(None, "gene"), P("bin"), P("bin", None))
    return jax.shard_map(
        on_device,
        mesh=mesh,
        in_specs=placed,
        out_specs=(P("bin", None), P(None, "gene")),
        check_vma=False,
    )
```

```python
import jax
import jax.numpy as jnp
from jax import lax
from jax.experimental import pallas as pl
from jax.experimental.pallas import tpu as pltpu
from jax.sharding import PartitionSpec as P

K = 256
G = 18432
PENALTY = float(G * K) / 64.0
EXTRA = 8
HALVES = 2
STEP = 512
READS = 2
MIB = 1024 * 1024
MINOR = (((1,), (1,)), ((), ()))
PLAIN = (((1,), (0,)), ((), ()))
F32 = jnp.float32
BF16 = jnp.bfloat16
ANY_SPEC = pl.BlockSpec(memory_space=pl.ANY)
VMEM_SPEC = pl.BlockSpec(memory_space=pltpu.VMEM)
SMEM_SPEC = pl.BlockSpec(memory_space=pltpu.SMEM)


def dot(a, b, dims, precision=None):
    return lax.dot_general(a, b, dims, precision=precision, preferred_element_type=F32)


def kernel_call(body, out_shape, us, limit=10, **kw):
    return pl.pallas_call(
        body,
        out_shape=out_shape,
        compiler_params=pltpu.CompilerParams(vmem_limit_bytes=limit * MIB),
        cost_estimate=pl.CostEstimate(flops=0, bytes_accessed=int(us * 3.69e6), transcendentals=0),
        **kw,
    )


def shape(*dims, dtype=F32):
    return jax.ShapeDtypeStruct(dims, dtype)


def pack(factors, position, me, width, bins):
    rows, width_all = factors.shape
    group = rows // bins
    lanes = 128 if width_all % 128 == 0 and 128 % width == 0 else width_all

    def body(me_ref, fac_ref, pos_ref, out_ref, turned):
        turned[...] = fac_ref[...].T
        first = pl.multiple_of(lax.rem(me_ref[0] * width, lanes), width)
        out_ref[0, :width, :] = turned[pl.ds(first, width), :]
        out_ref[0, width:, :] = jnp.broadcast_to(pos_ref[0], (EXTRA, group))

    grid_spec = pltpu.PrefetchScalarGridSpec(
        num_scalar_prefetch=1,
        grid=(bins,),
        in_specs=[
            pl.BlockSpec((group, lanes), lambda t, m: (t, m[0] * width // lanes)),
            pl.BlockSpec((1, 1, group), lambda t, m: (t, 0, 0)),
        ],
        out_specs=pl.BlockSpec((1, width + EXTRA, group), lambda t, m: (t, 0, 0)),
        scratch_shapes=[pltpu.VMEM((lanes, group), F32)],
    )
    return kernel_call(
        body, shape(bins, width + EXTRA, group), 3, grid_spec=grid_spec
    )(me, factors, position.astype(F32).reshape(bins, 1, group))


def to_grid(got, edge_codes, bin_me, token):
    bins, wide, group = got.shape
    width = wide - EXTRA
    grid_rows, grid_cols = edge_codes.shape
    rows = bins * group
    per = 4

    def body(me_ref, got_ref, code_ref, _, grid_ref, first_ref, last_ref, cell_ref, masked):
        block = jnp.concatenate([got_ref[s] for s in range(bins)], axis=1)
        cell = block[width : width + 1].astype(jnp.int32) - me_ref[0] * rows
        cell_ref[...] = cell
        at_row, at_col = cell // grid_cols, cell % grid_cols
        col_hot = jnp.where(
            lax.broadcasted_iota(jnp.int32, (grid_cols, rows), 0) == at_col, 1.0, 0.0
        ).astype(BF16)
        values = block[:width]
        high = values.astype(BF16)
        both = jnp.concatenate([high, (values - high.astype(F32)).astype(BF16)], axis=0)
        scale = code_ref[...].astype(F32) / 8.0
        for r in range(grid_rows):
            at = r % per * 2 * width
            if at == 0:
                for i in range(per):
                    mask = jnp.where(at_row == r + i, 1.0, 0.0).astype(BF16)
                    masked[i * 2 * width : (i + 1) * 2 * width, :] = both * mask
                placed = dot(masked[...], col_hot, MINOR)
            line = placed[at : at + width] + placed[at + width : at + 2 * width]
            row_scale = scale[r : r + 1]
            weighted = jnp.concatenate(
                [line * row_scale, jnp.broadcast_to(row_scale, (EXTRA, grid_cols))], axis=0
            )
            grid_ref[r] = weighted
            if r == 0:
                first_ref[...] = weighted
            if r == grid_rows - 1:
                last_ref[...] = weighted

    return kernel_call(
        body,
        (
            shape(grid_rows, wide, grid_cols),
            shape(wide, grid_cols),
            shape(wide, grid_cols),
            shape(1, rows, dtype=jnp.int32),
        ),
        3,
        limit=12,
        in_specs=[SMEM_SPEC, VMEM_SPEC, VMEM_SPEC, ANY_SPEC],
        out_specs=(VMEM_SPEC,) * 4,
        scratch_shapes=[pltpu.VMEM((per * 2 * width, rows), BF16)],
    )(bin_me, got, edge_codes, token)


def from_grid(grid, above, below, cell, edge_codes, bins, token):
    grid_rows, wide, grid_cols = grid.shape
    rows = cell.shape[1]
    group = rows // bins

    def body(grid_ref, above_ref, below_ref, cell_ref, code_ref, _, out_ref, halves):
        scale = code_ref[...].astype(F32) / 8.0
        lane = lax.broadcasted_iota(jnp.int32, (wide, grid_cols), 1)
        for r in range(grid_rows):
            here = grid_ref[r]
            upper = above_ref[...] if r == 0 else grid_ref[r - 1]
            lower = below_ref[...] if r == grid_rows - 1 else grid_ref[r + 1]
            left = jnp.where(lane == 0, 0.0, pltpu.roll(here, 1, 1))
            right = jnp.where(lane == grid_cols - 1, 0.0, pltpu.roll(here, grid_cols - 1, 1))
            value = scale[r : r + 1] * (left + right + 0.5 * (upper + lower))
            high = value.astype(BF16)
            halves[r * wide : (r + 1) * wide, :grid_cols] = high
            halves[r * wide : (r + 1) * wide, grid_cols:] = (value - high.astype(F32)).astype(BF16)
        cell = cell_ref[...]
        at_row, at_col = cell // grid_cols, cell % grid_cols
        for s in range(bins // 2):
            lo, hi = 2 * s * group, (2 * s + 2) * group
            hot = jnp.where(
                lax.broadcasted_iota(jnp.int32, (grid_cols, hi - lo), 0) == at_col[:, lo:hi], 1.0, 0.0
            ).astype(BF16)
            lines = dot(halves[...], jnp.concatenate([hot, hot], axis=0), PLAIN)
            row_here = at_row[:, lo:hi]
            total = jnp.zeros((wide, hi - lo), F32)
            for r in range(grid_rows):
                total = total + jnp.where(row_here == r, lines[r * wide : (r + 1) * wide], 0.0)
            out_ref[2 * s] = total[:, :group]
            out_ref[2 * s + 1] = total[:, group:]

    return kernel_call(
        body,
        shape(bins, wide, group),
        4,
        in_specs=[VMEM_SPEC] * 5 + [ANY_SPEC],
        out_specs=VMEM_SPEC,
        scratch_shapes=[pltpu.VMEM((grid_rows * wide, 2 * grid_cols), BF16)],
    )(grid, above, below, cell, edge_codes, token)


def numer_part(counts, loadings, gram, me, genes_n, part, send_ids, token):
    rows, genes = counts.shape
    first_call = loadings.dtype == F32
    width_all = loadings.shape[0] if first_call else loadings.shape[1]
    width = width_all // genes_n
    start, some_rows = part
    piece = STEP // 2
    pieces = some_rows // piece
    keep_ids = [k for k in range(genes_n) if k not in send_ids]
    total_cols = some_rows + (not first_call) * width_all

    def body(me_ref, counts_ref, *refs):
        firsts = [pl.multiple_of((k ^ me_ref[0]) * width, width) for k in range(genes_n)]
        if first_call:
            load_ref, _, send_ref, keep_ref, load_t, gram_ref, held, sems, load_bf, load_f = refs
        else:
            load_t, gram_ref, _, send_ref, keep_ref, held, sems = refs
        copies = [
            pltpu.make_async_copy(
                counts_ref.at[pl.ds(start + i * piece, piece), :],
                held.at[pl.ds(i * piece, piece), :],
                sems.at[i],
            )
            for i in range(pieces)
        ]

        def put(part, cols):
            for i, k in enumerate(send_ids):
                send_ref[i, :, cols] = part[k * width : (k + 1) * width]
            for i, k in enumerate(keep_ids):
                keep_ref[i, :, cols] = part[k * width : (k + 1) * width]

        if first_call:
            reads = [
                pltpu.make_async_copy(
                    load_ref.at[pl.ds(first, width), :],
                    load_f.at[pl.ds(k * width, width), :],
                    sems.at[pieces + k],
                )
                for k, first in enumerate(firsts)
            ]
            for copy in reads + copies:
                copy.start()
            for k, copy in enumerate(reads):
                copy.wait()
                here = slice(k * width, (k + 1) * width)
                load_bf[here, :] = load_f[here, :].astype(BF16)
            load_t[...] = load_bf[...].T
            local = dot(load_bf[...], load_t[...], PLAIN)
            for k, first in enumerate(firsts):
                gram_ref[pl.ds(first, width), :] = local[k * width : (k + 1) * width]
        else:
            for copy in copies:
                copy.start()
            put(gram_ref[...].T, slice(some_rows, total_cols))
        for i in range(0, pieces, 2):
            copies[i].wait()
            copies[i + 1].wait()
            at = slice(i * piece, (i + 2) * piece)
            put(dot(held[at, :], load_t[...], PLAIN).T, at)

    outs = (shape(genes_n // 2, width, total_cols),) * 2
    scratch = [pltpu.VMEM((some_rows, genes), BF16), pltpu.SemaphoreType.DMA((pieces + genes_n,))]
    if first_call:
        outs += (shape(genes, width_all, dtype=BF16), shape(width_all, width_all))
        scratch += [
            pltpu.VMEM((width_all, genes), BF16),
            pltpu.VMEM((width_all, genes), F32),
        ]
    loads = [loadings] if first_call else [loadings, gram]
    return kernel_call(
        body,
        outs,
        7,
        limit=40,
        in_specs=[SMEM_SPEC, ANY_SPEC]
        + [ANY_SPEC if first_call else VMEM_SPEC] * len(loads)
        + [ANY_SPEC],
        out_specs=(VMEM_SPEC,) * len(outs),
        scratch_shapes=scratch,
    )(me, counts, *loads, token)


def swap(block, axis, bit):
    return lax.ppermute(block, axis, [(i, i ^ bit) for i in range(lax.axis_size(axis))])


def picked_sum(arrays, ids, token):
    _, width, cols = arrays[0].shape
    first, step = ids[0], (ids[1] - ids[0] if len(ids) > 1 else 1)

    def body(*refs):
        total = refs[0][...]
        for ref in refs[1:-2]:
            total = total + ref[...]
        refs[-1][...] = total

    return kernel_call(
        body,
        shape(len(ids), width, cols),
        0.02,
        grid=(len(ids),),
        in_specs=[pl.BlockSpec((1, width, cols), lambda i: (first + step * i, 0, 0))] * len(arrays)
        + [ANY_SPEC],
        out_specs=pl.BlockSpec((1, width, cols), lambda i: (i, 0, 0)),
    )(*arrays, token)


def plain_terms(first, second, factors, token):
    rows, width_all = factors.shape
    width = first[0].shape[1]
    third = rows // 3
    n = len(first)

    def body(*refs):
        fac_ref, _, numer_ref, plain_ref, gram = refs[2 * n :]

        def total(part, cols):
            out = part[0][0, :, cols]
            for ref in part[1:]:
                out = out + ref[0, :, cols]
            return out

        @pl.when(pl.program_id(0) == 0)
        def _():
            gram[...] = total(refs[:n], slice(third, third + width_all))
            numer_ref[...] = total(refs[:n], slice(0, third))

        for i in (1, 2):

            @pl.when(pl.program_id(0) == i)
            def _():
                numer_ref[...] = total(refs[n : 2 * n], slice((i - 1) * third, i * third))

        plain_ref[...] = dot(fac_ref[...], gram[...], MINOR, lax.Precision.HIGHEST).T

    out_spec = pl.BlockSpec((width, third), lambda i: (0, i))
    arrays = list(first) + list(second)
    return kernel_call(
        body,
        (pltpu.HBM((width, rows), F32),) * 2,
        4,
        limit=24,
        grid=(3,),
        in_specs=[pl.BlockSpec((1,) + x.shape[1:], lambda i: (0, 0, 0)) for x in arrays]
        + [pl.BlockSpec((third, width_all), lambda i: (i, 0)), ANY_SPEC],
        out_specs=(out_spec, out_spec),
        scratch_shapes=[pltpu.VMEM((width, width_all), F32)],
    )(*arrays, factors, token)


def new_factors(payload, back, numer, plain):
    bins, wide, group = payload.shape
    width = wide - EXTRA

    def body(pay_ref, back_ref, numer_ref, plain_ref, out_ref):
        pay = jnp.concatenate([pay_ref[0], pay_ref[1]], axis=1)
        got = jnp.concatenate([back_ref[0], back_ref[1]], axis=1)
        fac, smooth, degree = pay[:width], got[:width], got[width : width + 1]
        out_ref[...] = (
            fac * (numer_ref[...] + PENALTY * smooth) / (plain_ref[...] + PENALTY * degree * fac)
        )

    pair = pl.BlockSpec((2, wide, group), lambda i: (i, 0, 0))
    cols = pl.BlockSpec((width, 2 * group), lambda i: (0, i))
    return kernel_call(
        body,
        shape(width, bins * group),
        0.02,
        grid=(bins // 2,),
        in_specs=[pair, pair, cols, cols],
        out_specs=cols,
    )(payload, back, numer, plain)


def sent_on(sources, token):
    n = len(sources)
    width, rows = sources[0][0].shape
    half_rows = rows // 2

    def body(*refs):
        for (_, half), src, dst in zip(sources, refs[:n], refs[n + 1 :]):
            dst[...] = src[:, half * half_rows : (half + 1) * half_rows]

    return kernel_call(
        body,
        (shape(width, half_rows),) * n,
        0.02,
        limit=1,
        in_specs=[VMEM_SPEC] * n + [ANY_SPEC],
        out_specs=(VMEM_SPEC,) * n,
    )(*[block for block, _ in sources], token)


def joined(halves, token):
    n = len(halves)
    width, half_rows = halves[0][0].shape

    def body(*refs):
        for i in range(n):
            for j in range(2):
                refs[2 * n + 1 + i][:, j * half_rows : (j + 1) * half_rows] = refs[2 * i + j][...]

    return kernel_call(
        body,
        (shape(width, 2 * half_rows),) * n,
        0.02,
        limit=1,
        in_specs=[VMEM_SPEC] * (2 * n) + [ANY_SPEC],
        out_specs=(VMEM_SPEC,) * n,
    )(*[x for pair in halves for x in pair], token)


def turned_back(blocks, ids, width, me, token):
    rows = blocks[0].shape[1]
    width_all = len(ids) * width
    step = 384
    steps = rows // step

    def body(me_ref, *refs):
        out_ref, _, block = refs[-3:]
        for ref, k in zip(refs, ids):
            block[pl.ds(pl.multiple_of((k ^ me_ref[0]) * width, width), width), :] = ref[...]
        out_ref[...] = block[...].T

    grid_spec = pltpu.PrefetchScalarGridSpec(
        num_scalar_prefetch=1,
        grid=(steps,),
        in_specs=[pl.BlockSpec((width, step), lambda i, m: (0, i))] * len(ids) + [ANY_SPEC],
        out_specs=(pl.BlockSpec((step, width_all), lambda i, m: (i, 0)), VMEM_SPEC),
        scratch_shapes=[pltpu.VMEM((width_all, step), F32)],
    )
    outs = (pltpu.HBM((rows, width_all), F32), shape(8, 128))
    return kernel_call(body, outs, 0.02, limit=8, grid_spec=grid_spec)(me, *blocks, token)


def put_rounded(fac, refs, width):
    for j, ref in enumerate(refs):
        fac[j * width : (j + 1) * width, :] = ref[...].astype(BF16)


def near_products(new, fac, width_all):
    near = dot(new, fac, MINOR)
    if near.shape[1] < width_all:
        near = jnp.concatenate([near, jnp.zeros((near.shape[0], width_all - near.shape[1]), F32)], axis=1)
    return near


def first_cross(block, counts, width_all, token):
    width, rows = block.shape
    genes = counts.shape[1]
    cols, extra = genes // HALVES, width_all // HALVES
    step = STEP
    steps = rows // step

    def body(counts_ref, block_ref, _, *refs):
        outs, held, (fac, sems) = refs[:HALVES], refs[HALVES : HALVES + steps], refs[HALVES + steps :]
        copies = [
            pltpu.make_async_copy(
                counts_ref.at[pl.ds(i * step, step), :], held[i], sems.at[i]
            )
            for i in range(steps)
        ]
        for copy in copies:
            copy.start()
        put_rounded(fac, [block_ref], width)
        near = near_products(fac[...], fac[...], width_all)
        for h, out in enumerate(outs):
            out[:, cols:] = near[:, h * extra : (h + 1) * extra]
        for i, copy in enumerate(copies):
            copy.wait()
            at = slice(i * step, (i + 1) * step)
            for h, out in enumerate(outs):
                part = dot(fac[:, at], held[i][:, h * cols : (h + 1) * cols], PLAIN)
                out[:, :cols] = part if i == 0 else out[:, :cols] + part

    return kernel_call(
        body,
        (shape(width, cols + extra),) * HALVES + (pltpu.VMEM((step, genes), BF16),) * steps,
        0.02,
        limit=8,
        in_specs=[ANY_SPEC, VMEM_SPEC, ANY_SPEC],
        out_specs=(VMEM_SPEC,) * (HALVES + steps),
        scratch_shapes=[pltpu.VMEM((width, rows), BF16), pltpu.SemaphoreType.DMA((steps,))],
    )(counts, block, token)


def cross_part(blocks, n_old, held, half, width_all, tokens):
    width, rows = blocks[0].shape
    cols, extra = held[0].shape[1] // HALVES, width_all // HALVES
    steps = 3
    step = cols // steps
    n = len(blocks) - n_old

    def body(*refs):
        pieces, refs = refs[: len(held)], refs[len(held) :]
        outs, fac = refs[-1 - n : -1], refs[-1]
        put_rounded(fac, refs[: len(blocks)], width)
        new = fac[n_old * width :, :]

        def put(part, where):
            for j, out in enumerate(outs):
                out[:, where] = part[j * width : (j + 1) * width]

        for i in range(steps):
            at = slice(half * cols + i * step, half * cols + (i + 1) * step)
            part = None
            for j, piece in enumerate(pieces):
                here = slice(j * piece.shape[0], (j + 1) * piece.shape[0])
                more = dot(new[:, here], piece[:, at], PLAIN)
                part = more if part is None else part + more
            put(part, slice(i * step, (i + 1) * step))
        near = near_products(new, fac[...], width_all)
        put(near[:, half * extra : (half + 1) * extra], slice(cols, cols + extra))

    return kernel_call(
        body,
        (shape(width, cols + extra),) * n,
        0.02,
        limit=8,
        in_specs=[VMEM_SPEC] * (len(held) + len(blocks)) + [ANY_SPEC] * len(tokens),
        out_specs=(VMEM_SPEC,) * n,
        scratch_shapes=[pltpu.VMEM((len(blocks) * width, rows), BF16)],
    )(*held, *blocks, *tokens)


def tiny_token(arrays):
    def body(*refs):
        refs[-1][...] = jnp.zeros(refs[-1].shape, F32)

    return kernel_call(
        body, shape(8, 128), 0.02, limit=1, in_specs=[ANY_SPEC] * len(arrays), out_specs=VMEM_SPEC
    )(*arrays)


def both_cores(parts, came, token):
    n = len(parts)

    def body(*refs):
        for a, b, out in zip(refs[:n], refs[n : 2 * n], refs[2 * n + 1 :]):
            out[...] = a[...] + b[...]

    return kernel_call(
        body,
        tuple(shape(*part.shape) for part in parts),
        0.02,
        limit=1,
        in_specs=[VMEM_SPEC] * (2 * n) + [ANY_SPEC],
        out_specs=(VMEM_SPEC,) * n,
    )(*parts, *came, token)


def line_slot(flags, t, chunks, own, come, token):
    line = lax.axis_size("bin") // 2
    places = [q for q in range(line - 1) if 0 <= t - q < chunks]
    hops = [(2 * q, 2 * q + 2) for q in places]
    hops += [(2 * (line - 1 - q) + 1, 2 * (line - 2 - q) + 1) for q in places]
    if t == 0:
        return lax.ppermute(own[0], "bin", hops), token
    arrays = [own[t - q] for q in places]

    def body(flag_ref, come_ref, _, *refs):
        for i, q in enumerate(places):

            @pl.when(flag_ref[2] == q)
            def _():
                value = refs[i][...]
                refs[-1][...] = value if q == 0 else value + come_ref[...]

    send = kernel_call(
        body,
        shape(*come.shape),
        0.02,
        limit=1,
        in_specs=[SMEM_SPEC, VMEM_SPEC, ANY_SPEC] + [VMEM_SPEC] * len(arrays),
        out_specs=VMEM_SPEC,
    )(flags, come, token, *arrays)
    return lax.ppermute(send, "bin", hops), send


def line_end(flags, come, token):
    def body(flag_ref, _, *refs):
        out = refs[-1]

        @pl.when(flag_ref[2] == 0)
        def _():
            out[...] = jnp.zeros(out.shape, F32)

        for d in range(len(come)):

            @pl.when(flag_ref[2] == d + 1)
            def _():
                out[...] = refs[d][...]

    end = kernel_call(
        body,
        shape(*come[0].shape),
        0.02,
        limit=1,
        in_specs=[SMEM_SPEC, ANY_SPEC] + [VMEM_SPEC] * len(come),
        out_specs=VMEM_SPEC,
    )(flags, token, *come)
    return end, swap(end, "bin", 1)


def split(x):
    high = x.astype(BF16)
    return high, (x - high.astype(F32)).astype(BF16)


def new_loadings(loadings, sums, ids, me, token):
    width_all, genes = loadings.shape
    width = width_all // len(ids)
    cols, extra = genes // HALVES, width_all // HALVES
    per = 3
    step = cols // per
    arrays = [x for pair in sums for terms in pair for x in terms]

    def body(me_ref, load_ref, *refs):
        out_ref, load, gram, cross = refs[-4:]
        at = pl.program_id(0)
        firsts = [pl.multiple_of((k ^ me_ref[0]) * width, width) for k in ids]
        terms = lambda j, h: refs[3 * (j * HALVES + h) : 3 * (j * HALVES + h) + 3]

        @pl.when(at == 0)
        def _():
            behind = slice(cols, cols + extra)
            for j in range(len(ids)):
                for h in range(HALVES):
                    own, end, other = terms(j, h)
                    gram[j * width : (j + 1) * width, h * extra : (h + 1) * extra] = own[:, behind] + (
                        end[:, behind] + other[:, behind]
                    )
            low = gram[...]
            row = lax.broadcasted_iota(jnp.int32, low.shape, 0) // width
            col = lax.broadcasted_iota(jnp.int32, low.shape, 1) // width
            gram[...] = jnp.where(col <= row, low, low.T)

        for h in range(HALVES):

            @pl.when(at // per == h)
            def _():
                here = pl.ds(pl.multiple_of((at - h * per) * step, step), step)
                for j in range(len(ids)):
                    own, end, other = terms(j, h)
                    cross[j * width : (j + 1) * width, :] = own[:, here] + (end[:, here] + other[:, here])

        for j, first in enumerate(firsts):
            load[j * width : (j + 1) * width, :] = load_ref[pl.ds(first, width), :]
        value = load[...]
        (gram_hi, gram_lo), (hi, lo) = split(gram[...]), split(value)
        below = dot(gram_hi, hi, PLAIN) + (dot(gram_hi, lo, PLAIN) + dot(gram_lo, hi, PLAIN))
        value = value * cross[...] / below
        for j, first in enumerate(firsts):
            out_ref[pl.ds(first, width), :] = value[j * width : (j + 1) * width]

    block = pl.BlockSpec((width_all, step), lambda i, f: (0, i))
    return kernel_call(
        body,
        pltpu.HBM((width_all, genes), F32),
        0.02,
        limit=16,
        grid_spec=pltpu.PrefetchScalarGridSpec(
            num_scalar_prefetch=1,
            grid=(HALVES * per,),
            in_specs=[block] + [VMEM_SPEC] * len(arrays) + [ANY_SPEC],
            out_specs=block,
            scratch_shapes=[
                pltpu.VMEM((width_all, step), F32),
                pltpu.VMEM((width_all, width_all), F32),
                pltpu.VMEM((width_all, step), F32),
            ],
        ),
    )(me, loadings, *arrays, token)


def on_device(counts, factors, loadings, position, edge_codes):
    bins, genes_n = lax.axis_size("bin"), lax.axis_size("gene")
    line = bins // 2
    me, bin_me = lax.axis_index("gene"), lax.axis_index("bin")
    rows, width_all = factors.shape
    width = width_all // genes_n
    scalar = lambda x: jnp.asarray(x, jnp.int32).reshape(1)
    me1, bin1 = scalar(me), scalar(bin_me)
    core, chip = bin1 & 1, bin1 >> 1
    flags = jnp.concatenate([me1, core, jnp.where(core == 0, chip, line - 1 - chip)])
    bits = [1 << b for b in range(genes_n.bit_length() - 1)]

    counts = pltpu.with_memory_space_constraint(counts, pltpu.HBM)
    payload = pack(factors, position, me1, width, bins)
    got = lax.all_to_all(payload, "bin", split_axis=0, concat_axis=0, tiled=True)
    in_hbm = lambda x: pltpu.with_memory_space_constraint(x, pltpu.HBM)

    orders = (bits, bits[::-1])
    token, load = payload, pltpu.with_memory_space_constraint(loadings, pltpu.HBM)
    parts, keeps, gram = [None, None], [None, None], None
    third = rows // 3
    numer_parts = ((0, third), (third, rows - third))
    for half in (1, 0):
        bit = orders[half][0]
        send_ids = [k for k in range(genes_n) if k & bit]
        keeps[half] = [k for k in range(genes_n) if not k & bit]
        send, keep, *made = numer_part(
            counts, load, gram, me1, genes_n, numer_parts[half], send_ids, token
        )
        load, gram = made or (load, gram)
        token = keep
        parts[half] = [keep, swap(send, "gene", bit)]

    def scatter_more(half, bit, token):
        out_ids = [i for i, k in enumerate(keeps[half]) if k & bit]
        in_ids = [i for i, k in enumerate(keeps[half]) if not k & bit]
        keeps[half] = [keeps[half][i] for i in in_ids]
        parts[half] = [in_hbm(x) for x in parts[half]]
        send = picked_sum(parts[half], out_ids, token)
        if len(in_ids) > 1:
            parts[half] = [picked_sum(parts[half], in_ids, send)]
        parts[half] = parts[half] + [swap(send, "gene", bit)]
        return send

    grid, first, last, cell = to_grid(got, edge_codes, bin1, token)
    above = lax.ppermute(last, "bin", [(i, i + 1) for i in range(bins - 1)])
    below = lax.ppermute(first, "bin", [(i + 1, i) for i in range(bins - 1)])
    token = grid
    for i in range(1, len(bits)):
        for half in (1, 0):
            token = scatter_more(half, orders[half][i], token)
    smooth = from_grid(grid, above, below, cell, edge_codes, bins, token)
    back = lax.all_to_all(smooth, "bin", split_axis=0, concat_axis=0, tiled=True)
    numer, plain = plain_terms(*[[in_hbm(x) for x in p] for p in parts], in_hbm(factors), smooth)
    own_block = new_factors(*[in_hbm(x) for x in (payload, back, numer, plain)])

    ids = sorted(range(genes_n), key=lambda k: (bin(k).count("1"), k))
    groups = [[k for k in ids if bin(k).count("1") == n] for n in range(len(bits) + 1)]
    chunks = len(ids)
    blocks = {0: own_block}
    for k in bits:
        blocks[k] = swap(own_block, "gene", k)

    coming = {}

    def come_on(group, token):
        axes = [(k & -k, 1 << (k.bit_length() - 1)) for k in group]
        sources = [(blocks[k ^ bit], j) for k, pair in zip(group, axes) for j, bit in enumerate(pair)]
        outs = sent_on(sources, token)
        for i, (k, pair) in enumerate(zip(group, axes)):
            coming[k] = [swap(outs[2 * i + j], "gene", bit) for j, bit in enumerate(pair)]
        return outs[-1]

    pending = [[None] * len(groups) for _ in range(HALVES)]
    own = [{} for _ in range(HALVES)]
    come = [[] for _ in range(HALVES)]
    ends = [{} for _ in range(HALVES)]

    def product(g, half, *tokens):
        upto = ids.index(groups[g][-1]) + 1
        n_old = upto - len(groups[g])
        parts = cross_part([blocks[k] for k in ids[:upto]], n_old, held, half, width_all, tokens)
        pending[half][g] = (parts, [swap(part, "bin", 1) for part in parts])
        return parts[-1]

    def own_chunks(g, half, token):
        arrays = both_cores(*pending[half][g], token)
        for k, array in zip(groups[g], arrays):
            own[half][ids.index(k)] = array
        return arrays[-1]

    def slot(half, t, token):
        before = come[half][-1] if come[half] else None
        got, token = line_slot(flags, t, chunks, own[half], before, token)
        come[half].append(got)
        return token

    def end(c, half, token):
        ends[half][c] = line_end(flags, come[half][c : c + line - 1], token)
        return ends[half][c][0]

    def both(step, *args):
        nonlocal token
        for half in range(HALVES):
            token = step(*args, half, token)

    def awaited(arrays, token):
        return tiny_token(list(arrays) + [token])

    made = first_cross(own_block, counts, width_all, own_block)
    parts, held = made[:HALVES], made[HALVES:]
    for half in range(HALVES):
        pending[half][0] = ((parts[half],), [swap(parts[half], "bin", 1)])
    token = awaited([blocks[k] for k in bits], parts[-1])
    if len(groups) > 2:
        token = come_on(groups[2], token)
    for half in range(HALVES):
        token = own_chunks(0, half, token)
        token = slot(half, 0, token)
    both(product, 1)
    firsts = {ids.index(group[0]): g for g, group in enumerate(groups)}
    last_slot = chunks + line - 3
    for t in range(1, last_slot + 1):
        if t in firsts and firsts[t] + 1 < len(groups):
            later = groups[firsts[t] + 1]
            for k, block in zip(later, joined([coming[k] for k in later], token)):
                blocks[k] = token = block
            for half in range(HALVES):
                token = awaited([come[half][-1]], token)
        for half in range(HALVES):
            if t in firsts:
                token = own_chunks(firsts[t], half, token)
            token = slot(half, t, token)
        g = firsts.get(t, len(groups)) + 1
        if g < len(groups):
            both(product, g)
            if g + 1 < len(groups):
                token = come_on(groups[g + 1], token)
        if t == chunks - 1:
            factors_new, token = turned_back([blocks[k] for k in ids], ids, width, me1, token)
        c = t - (line - 1)
        if c - 1 in ends[0]:
            token = awaited([ends[half][c - 1][1] for half in range(HALVES)], token)
        if 0 <= c < chunks:
            both(end, c)
    rest = [c for c in range(chunks) if c not in ends[0]]
    for c in rest:
        both(end, c)
    sums = [[(own[h][c],) + ends[h][c] for h in range(HALVES)] for c in range(chunks)]
    loadings_new = new_loadings(loadings, sums, ids, me1, token)
    return factors_new, loadings_new


def solution(mesh):
    placed = (P("bin", "gene"), P("bin", None), P(None, "gene"), P("bin"), P("bin", None))
    return jax.shard_map(
        on_device,
        mesh=mesh,
        in_specs=placed,
        out_specs=(P("bin", None), P(None, "gene")),
        check_vma=False,
    )
```

```python
import jax
import jax.numpy as jnp
from jax import lax
from jax.experimental import pallas as pl
from jax.experimental.pallas import tpu as pltpu
from jax.sharding import PartitionSpec as P

K = 256
G = 18432
PENALTY = float(G * K) / 64.0
EXTRA = 8
HALVES = 2
STEP = 512
READS = 2
MIB = 1024 * 1024
MINOR = (((1,), (1,)), ((), ()))
PLAIN = (((1,), (0,)), ((), ()))
F32 = jnp.float32
BF16 = jnp.bfloat16
ANY_SPEC = pl.BlockSpec(memory_space=pl.ANY)
VMEM_SPEC = pl.BlockSpec(memory_space=pltpu.VMEM)
SMEM_SPEC = pl.BlockSpec(memory_space=pltpu.SMEM)


def dot(a, b, dims, precision=None):
    return lax.dot_general(a, b, dims, precision=precision, preferred_element_type=F32)


def kernel_call(body, out_shape, us, limit=10, **kw):
    return pl.pallas_call(
        body,
        out_shape=out_shape,
        compiler_params=pltpu.CompilerParams(vmem_limit_bytes=limit * MIB),
        cost_estimate=pl.CostEstimate(flops=0, bytes_accessed=int(us * 3.69e6), transcendentals=0),
        **kw,
    )


def shape(*dims, dtype=F32):
    return jax.ShapeDtypeStruct(dims, dtype)


def pack(factors, position, me, width, bins):
    rows, width_all = factors.shape
    group = rows // bins
    lanes = 128 if width_all % 128 == 0 and 128 % width == 0 else width_all

    def body(me_ref, fac_ref, pos_ref, out_ref, turned):
        turned[...] = fac_ref[...].T
        first = pl.multiple_of(lax.rem(me_ref[0] * width, lanes), width)
        out_ref[0, :width, :] = turned[pl.ds(first, width), :]
        out_ref[0, width:, :] = jnp.broadcast_to(pos_ref[0], (EXTRA, group))

    grid_spec = pltpu.PrefetchScalarGridSpec(
        num_scalar_prefetch=1,
        grid=(bins,),
        in_specs=[
            pl.BlockSpec((group, lanes), lambda t, m: (t, m[0] * width // lanes)),
            pl.BlockSpec((1, 1, group), lambda t, m: (t, 0, 0)),
        ],
        out_specs=pl.BlockSpec((1, width + EXTRA, group), lambda t, m: (t, 0, 0)),
        scratch_shapes=[pltpu.VMEM((lanes, group), F32)],
    )
    return kernel_call(
        body, shape(bins, width + EXTRA, group), 3, grid_spec=grid_spec
    )(me, factors, position.astype(F32).reshape(bins, 1, group))


def to_grid(got, edge_codes, bin_me, token):
    bins, wide, group = got.shape
    width = wide - EXTRA
    grid_rows, grid_cols = edge_codes.shape
    rows = bins * group
    per = 4

    def body(me_ref, got_ref, code_ref, _, grid_ref, first_ref, last_ref, cell_ref, masked):
        block = jnp.concatenate([got_ref[s] for s in range(bins)], axis=1)
        cell = block[width : width + 1].astype(jnp.int32) - me_ref[0] * rows
        cell_ref[...] = cell
        at_row, at_col = cell // grid_cols, cell % grid_cols
        col_hot = jnp.where(
            lax.broadcasted_iota(jnp.int32, (grid_cols, rows), 0) == at_col, 1.0, 0.0
        ).astype(BF16)
        values = block[:width]
        high = values.astype(BF16)
        both = jnp.concatenate([high, (values - high.astype(F32)).astype(BF16)], axis=0)
        scale = code_ref[...].astype(F32) / 8.0
        for r in range(grid_rows):
            at = r % per * 2 * width
            if at == 0:
                for i in range(per):
                    mask = jnp.where(at_row == r + i, 1.0, 0.0).astype(BF16)
                    masked[i * 2 * width : (i + 1) * 2 * width, :] = both * mask
                placed = dot(masked[...], col_hot, MINOR)
            line = placed[at : at + width] + placed[at + width : at + 2 * width]
            row_scale = scale[r : r + 1]
            weighted = jnp.concatenate(
                [line * row_scale, jnp.broadcast_to(row_scale, (EXTRA, grid_cols))], axis=0
            )
            grid_ref[r] = weighted
            if r == 0:
                first_ref[...] = weighted
            if r == grid_rows - 1:
                last_ref[...] = weighted

    return kernel_call(
        body,
        (
            shape(grid_rows, wide, grid_cols),
            shape(wide, grid_cols),
            shape(wide, grid_cols),
            shape(1, rows, dtype=jnp.int32),
        ),
        3,
        limit=12,
        in_specs=[SMEM_SPEC, VMEM_SPEC, VMEM_SPEC, ANY_SPEC],
        out_specs=(VMEM_SPEC,) * 4,
        scratch_shapes=[pltpu.VMEM((per * 2 * width, rows), BF16)],
    )(bin_me, got, edge_codes, token)


def from_grid(grid, above, below, cell, edge_codes, bins, token):
    grid_rows, wide, grid_cols = grid.shape
    rows = cell.shape[1]
    group = rows // bins

    def body(grid_ref, above_ref, below_ref, cell_ref, code_ref, _, out_ref, halves):
        scale = code_ref[...].astype(F32) / 8.0
        lane = lax.broadcasted_iota(jnp.int32, (wide, grid_cols), 1)
        for r in range(grid_rows):
            here = grid_ref[r]
            upper = above_ref[...] if r == 0 else grid_ref[r - 1]
            lower = below_ref[...] if r == grid_rows - 1 else grid_ref[r + 1]
            left = jnp.where(lane == 0, 0.0, pltpu.roll(here, 1, 1))
            right = jnp.where(lane == grid_cols - 1, 0.0, pltpu.roll(here, grid_cols - 1, 1))
            value = scale[r : r + 1] * (left + right + 0.5 * (upper + lower))
            high = value.astype(BF16)
            halves[r * wide : (r + 1) * wide, :grid_cols] = high
            halves[r * wide : (r + 1) * wide, grid_cols:] = (value - high.astype(F32)).astype(BF16)
        cell = cell_ref[...]
        at_row, at_col = cell // grid_cols, cell % grid_cols
        for s in range(bins // 2):
            lo, hi = 2 * s * group, (2 * s + 2) * group
            hot = jnp.where(
                lax.broadcasted_iota(jnp.int32, (grid_cols, hi - lo), 0) == at_col[:, lo:hi], 1.0, 0.0
            ).astype(BF16)
            lines = dot(halves[...], jnp.concatenate([hot, hot], axis=0), PLAIN)
            row_here = at_row[:, lo:hi]
            total = jnp.zeros((wide, hi - lo), F32)
            for r in range(grid_rows):
                total = total + jnp.where(row_here == r, lines[r * wide : (r + 1) * wide], 0.0)
            out_ref[2 * s] = total[:, :group]
            out_ref[2 * s + 1] = total[:, group:]

    return kernel_call(
        body,
        shape(bins, wide, group),
        4,
        in_specs=[VMEM_SPEC] * 5 + [ANY_SPEC],
        out_specs=VMEM_SPEC,
        scratch_shapes=[pltpu.VMEM((grid_rows * wide, 2 * grid_cols), BF16)],
    )(grid, above, below, cell, edge_codes, token)


def numer_part(counts, loadings, gram, me, genes_n, part, send_ids, token):
    rows, genes = counts.shape
    first_call = loadings.dtype == F32
    width_all = loadings.shape[0] if first_call else loadings.shape[1]
    width = width_all // genes_n
    start, some_rows = part
    piece = STEP // 2
    pieces = some_rows // piece
    keep_ids = [k for k in range(genes_n) if k not in send_ids]
    total_cols = some_rows + (not first_call) * width_all

    def body(me_ref, counts_ref, *refs):
        firsts = [pl.multiple_of((k ^ me_ref[0]) * width, width) for k in range(genes_n)]
        if first_call:
            load_ref, _, send_ref, keep_ref, load_t, gram_ref, held, sems, load_bf, load_f = refs
        else:
            load_t, gram_ref, _, send_ref, keep_ref, held, sems = refs
        copies = [
            pltpu.make_async_copy(
                counts_ref.at[pl.ds(start + i * piece, piece), :],
                held.at[pl.ds(i * piece, piece), :],
                sems.at[i],
            )
            for i in range(pieces)
        ]

        def put(part, cols):
            for i, k in enumerate(send_ids):
                send_ref[i, :, cols] = part[k * width : (k + 1) * width]
            for i, k in enumerate(keep_ids):
                keep_ref[i, :, cols] = part[k * width : (k + 1) * width]

        if first_call:
            reads = [
                pltpu.make_async_copy(
                    load_ref.at[pl.ds(first, width), :],
                    load_f.at[pl.ds(k * width, width), :],
                    sems.at[pieces + k],
                )
                for k, first in enumerate(firsts)
            ]
            for copy in reads + copies:
                copy.start()
            for k, copy in enumerate(reads):
                copy.wait()
                here = slice(k * width, (k + 1) * width)
                load_bf[here, :] = load_f[here, :].astype(BF16)
            load_t[...] = load_bf[...].T
            local = dot(load_bf[...], load_t[...], PLAIN)
            for k, first in enumerate(firsts):
                gram_ref[pl.ds(first, width), :] = local[k * width : (k + 1) * width]
        else:
            for copy in copies:
                copy.start()
            put(gram_ref[...].T, slice(some_rows, total_cols))
        for i in range(0, pieces, 2):
            copies[i].wait()
            copies[i + 1].wait()
            at = slice(i * piece, (i + 2) * piece)
            put(dot(held[at, :], load_t[...], PLAIN).T, at)

    outs = (shape(genes_n // 2, width, total_cols),) * 2
    scratch = [pltpu.VMEM((some_rows, genes), BF16), pltpu.SemaphoreType.DMA((pieces + genes_n,))]
    if first_call:
        outs += (shape(genes, width_all, dtype=BF16), shape(width_all, width_all))
        scratch += [
            pltpu.VMEM((width_all, genes), BF16),
            pltpu.VMEM((width_all, genes), F32),
        ]
    loads = [loadings] if first_call else [loadings, gram]
    return kernel_call(
        body,
        outs,
        7,
        limit=40,
        in_specs=[SMEM_SPEC, ANY_SPEC]
        + [ANY_SPEC if first_call else VMEM_SPEC] * len(loads)
        + [ANY_SPEC],
        out_specs=(VMEM_SPEC,) * len(outs),
        scratch_shapes=scratch,
    )(me, counts, *loads, token)


def swap(block, axis, bit):
    return lax.ppermute(block, axis, [(i, i ^ bit) for i in range(lax.axis_size(axis))])


def picked_sum(arrays, ids, token):
    _, width, cols = arrays[0].shape
    first, step = ids[0], (ids[1] - ids[0] if len(ids) > 1 else 1)

    def body(*refs):
        total = refs[0][...]
        for ref in refs[1:-2]:
            total = total + ref[...]
        refs[-1][...] = total

    return kernel_call(
        body,
        shape(len(ids), width, cols),
        0.02,
        grid=(len(ids),),
        in_specs=[pl.BlockSpec((1, width, cols), lambda i: (first + step * i, 0, 0))] * len(arrays)
        + [ANY_SPEC],
        out_specs=pl.BlockSpec((1, width, cols), lambda i: (i, 0, 0)),
    )(*arrays, token)


def plain_terms(first, second, factors, token):
    rows, width_all = factors.shape
    width = first[0].shape[1]
    third = rows // 3
    n = len(first)

    def body(*refs):
        fac_ref, _, numer_ref, plain_ref, gram = refs[2 * n :]

        def total(part, cols):
            out = part[0][0, :, cols]
            for ref in part[1:]:
                out = out + ref[0, :, cols]
            return out

        @pl.when(pl.program_id(0) == 0)
        def _():
            gram[...] = total(refs[:n], slice(third, third + width_all))
            numer_ref[...] = total(refs[:n], slice(0, third))

        for i in (1, 2):

            @pl.when(pl.program_id(0) == i)
            def _():
                numer_ref[...] = total(refs[n : 2 * n], slice((i - 1) * third, i * third))

        plain_ref[...] = dot(fac_ref[...], gram[...], MINOR, lax.Precision.HIGHEST).T

    out_spec = pl.BlockSpec((width, third), lambda i: (0, i))
    arrays = list(first) + list(second)
    return kernel_call(
        body,
        (pltpu.HBM((width, rows), F32),) * 2,
        4,
        limit=24,
        grid=(3,),
        in_specs=[pl.BlockSpec((1,) + x.shape[1:], lambda i: (0, 0, 0)) for x in arrays]
        + [pl.BlockSpec((third, width_all), lambda i: (i, 0)), ANY_SPEC],
        out_specs=(out_spec, out_spec),
        scratch_shapes=[pltpu.VMEM((width, width_all), F32)],
    )(*arrays, factors, token)


def new_factors(payload, back, numer, plain):
    bins, wide, group = payload.shape
    width = wide - EXTRA

    def body(pay_ref, back_ref, numer_ref, plain_ref, out_ref):
        pay = jnp.concatenate([pay_ref[0], pay_ref[1]], axis=1)
        got = jnp.concatenate([back_ref[0], back_ref[1]], axis=1)
        fac, smooth, degree = pay[:width], got[:width], got[width : width + 1]
        out_ref[...] = (
            fac * (numer_ref[...] + PENALTY * smooth) / (plain_ref[...] + PENALTY * degree * fac)
        )

    pair = pl.BlockSpec((2, wide, group), lambda i: (i, 0, 0))
    cols = pl.BlockSpec((width, 2 * group), lambda i: (0, i))
    return kernel_call(
        body,
        shape(width, bins * group),
        0.02,
        grid=(bins // 2,),
        in_specs=[pair, pair, cols, cols],
        out_specs=cols,
    )(payload, back, numer, plain)


def sent_on(sources, token):
    n = len(sources)
    width, rows = sources[0][0].shape
    half_rows = rows // 2

    def body(*refs):
        for (_, half), src, dst in zip(sources, refs[:n], refs[n + 1 :]):
            dst[...] = src[:, half * half_rows : (half + 1) * half_rows]

    return kernel_call(
        body,
        (shape(width, half_rows),) * n,
        0.02,
        limit=1,
        in_specs=[VMEM_SPEC] * n + [ANY_SPEC],
        out_specs=(VMEM_SPEC,) * n,
    )(*[block for block, _ in sources], token)


def joined(halves, token):
    n = len(halves)
    width, half_rows = halves[0][0].shape

    def body(*refs):
        for i in range(n):
            for j in range(2):
                refs[2 * n + 1 + i][:, j * half_rows : (j + 1) * half_rows] = refs[2 * i + j][...]

    return kernel_call(
        body,
        (shape(width, 2 * half_rows),) * n,
        0.02,
        limit=1,
        in_specs=[VMEM_SPEC] * (2 * n) + [ANY_SPEC],
        out_specs=(VMEM_SPEC,) * n,
    )(*[x for pair in halves for x in pair], token)


def turned_back(blocks, ids, width, me, token):
    rows = blocks[0].shape[1]
    width_all = len(ids) * width
    step = 384
    steps = rows // step

    def body(me_ref, *refs):
        out_ref, _, block = refs[-3:]
        for ref, k in zip(refs, ids):
            block[pl.ds(pl.multiple_of((k ^ me_ref[0]) * width, width), width), :] = ref[...]
        out_ref[...] = block[...].T

    grid_spec = pltpu.PrefetchScalarGridSpec(
        num_scalar_prefetch=1,
        grid=(steps,),
        in_specs=[pl.BlockSpec((width, step), lambda i, m: (0, i))] * len(ids) + [ANY_SPEC],
        out_specs=(pl.BlockSpec((step, width_all), lambda i, m: (i, 0)), VMEM_SPEC),
        scratch_shapes=[pltpu.VMEM((width_all, step), F32)],
    )
    outs = (pltpu.HBM((rows, width_all), F32), shape(8, 128))
    return kernel_call(body, outs, 0.02, limit=8, grid_spec=grid_spec)(me, *blocks, token)


def put_rounded(fac, refs, width):
    for j, ref in enumerate(refs):
        fac[j * width : (j + 1) * width, :] = ref[...].astype(BF16)


def near_products(new, fac, width_all):
    near = dot(new, fac, MINOR)
    if near.shape[1] < width_all:
        near = jnp.concatenate([near, jnp.zeros((near.shape[0], width_all - near.shape[1]), F32)], axis=1)
    return near


def first_cross(block, counts, width_all, token):
    width, rows = block.shape
    genes = counts.shape[1]
    cols, extra = genes // HALVES, width_all // HALVES
    step = STEP
    steps = rows // step

    def body(counts_ref, block_ref, _, *refs):
        outs, held, (fac, sems) = refs[:HALVES], refs[HALVES : HALVES + steps], refs[HALVES + steps :]
        copies = [
            pltpu.make_async_copy(
                counts_ref.at[pl.ds(i * step, step), :], held[i], sems.at[i]
            )
            for i in range(steps)
        ]
        for copy in copies:
            copy.start()
        put_rounded(fac, [block_ref], width)
        near = near_products(fac[...], fac[...], width_all)
        for h, out in enumerate(outs):
            out[:, cols:] = near[:, h * extra : (h + 1) * extra]
        for i, copy in enumerate(copies):
            copy.wait()
            at = slice(i * step, (i + 1) * step)
            for h, out in enumerate(outs):
                part = dot(fac[:, at], held[i][:, h * cols : (h + 1) * cols], PLAIN)
                out[:, :cols] = part if i == 0 else out[:, :cols] + part

    return kernel_call(
        body,
        (shape(width, cols + extra),) * HALVES + (pltpu.VMEM((step, genes), BF16),) * steps,
        0.02,
        limit=8,
        in_specs=[ANY_SPEC, VMEM_SPEC, ANY_SPEC],
        out_specs=(VMEM_SPEC,) * (HALVES + steps),
        scratch_shapes=[pltpu.VMEM((width, rows), BF16), pltpu.SemaphoreType.DMA((steps,))],
    )(counts, block, token)


def cross_part(blocks, n_old, held, half, width_all, tokens):
    width, rows = blocks[0].shape
    cols, extra = held[0].shape[1] // HALVES, width_all // HALVES
    steps = 3
    step = cols // steps
    n = len(blocks) - n_old

    def body(*refs):
        pieces, refs = refs[: len(held)], refs[len(held) :]
        outs, fac = refs[-1 - n : -1], refs[-1]
        put_rounded(fac, refs[: len(blocks)], width)
        new = fac[n_old * width :, :]

        def put(part, where):
            for j, out in enumerate(outs):
                out[:, where] = part[j * width : (j + 1) * width]

        for i in range(steps):
            at = slice(half * cols + i * step, half * cols + (i + 1) * step)
            part = None
            for j, piece in enumerate(pieces):
                here = slice(j * piece.shape[0], (j + 1) * piece.shape[0])
                more = dot(new[:, here], piece[:, at], PLAIN)
                part = more if part is None else part + more
            put(part, slice(i * step, (i + 1) * step))
        near = near_products(new, fac[...], width_all)
        put(near[:, half * extra : (half + 1) * extra], slice(cols, cols + extra))

    return kernel_call(
        body,
        (shape(width, cols + extra),) * n,
        0.02,
        limit=8,
        in_specs=[VMEM_SPEC] * (len(held) + len(blocks)) + [ANY_SPEC] * len(tokens),
        out_specs=(VMEM_SPEC,) * n,
        scratch_shapes=[pltpu.VMEM((len(blocks) * width, rows), BF16)],
    )(*held, *blocks, *tokens)


def tiny_token(arrays):
    def body(*refs):
        refs[-1][...] = jnp.zeros(refs[-1].shape, F32)

    return kernel_call(
        body, shape(8, 128), 0.02, limit=1, in_specs=[ANY_SPEC] * len(arrays), out_specs=VMEM_SPEC
    )(*arrays)


def both_cores(parts, came, token):
    n = len(parts)

    def body(*refs):
        for a, b, out in zip(refs[:n], refs[n : 2 * n], refs[2 * n + 1 :]):
            out[...] = a[...] + b[...]

    return kernel_call(
        body,
        tuple(shape(*part.shape) for part in parts),
        0.02,
        limit=1,
        in_specs=[VMEM_SPEC] * (2 * n) + [ANY_SPEC],
        out_specs=(VMEM_SPEC,) * n,
    )(*parts, *came, token)


def line_slot(flags, t, chunks, own, come, token):
    line = lax.axis_size("bin") // 2
    places = [q for q in range(line - 1) if 0 <= t - q < chunks]
    hops = [(2 * q, 2 * q + 2) for q in places]
    hops += [(2 * (line - 1 - q) + 1, 2 * (line - 2 - q) + 1) for q in places]
    if t == 0:
        return lax.ppermute(own[0], "bin", hops), token
    arrays = [own[t - q] for q in places]

    def body(flag_ref, come_ref, _, *refs):
        for i, q in enumerate(places):

            @pl.when(flag_ref[2] == q)
            def _():
                value = refs[i][...]
                refs[-1][...] = value if q == 0 else value + come_ref[...]

    send = kernel_call(
        body,
        shape(*come.shape),
        0.02,
        limit=1,
        in_specs=[SMEM_SPEC, VMEM_SPEC, ANY_SPEC] + [VMEM_SPEC] * len(arrays),
        out_specs=VMEM_SPEC,
    )(flags, come, token, *arrays)
    return lax.ppermute(send, "bin", hops), send


def line_end(flags, come, token):
    def body(flag_ref, _, *refs):
        out = refs[-1]

        @pl.when(flag_ref[2] == 0)
        def _():
            out[...] = jnp.zeros(out.shape, F32)

        for d in range(len(come)):

            @pl.when(flag_ref[2] == d + 1)
            def _():
                out[...] = refs[d][...]

    end = kernel_call(
        body,
        shape(*come[0].shape),
        0.02,
        limit=1,
        in_specs=[SMEM_SPEC, ANY_SPEC] + [VMEM_SPEC] * len(come),
        out_specs=VMEM_SPEC,
    )(flags, token, *come)
    return end, swap(end, "bin", 1)


def split(x):
    high = x.astype(BF16)
    return high, (x - high.astype(F32)).astype(BF16)


def new_loadings(loadings, sums, ids, me, token):
    width_all, genes = loadings.shape
    width = width_all // len(ids)
    cols, extra = genes // HALVES, width_all // HALVES
    per = 3
    step = cols // per
    arrays = [x for pair in sums for terms in pair for x in terms]

    def body(me_ref, load_ref, *refs):
        out_ref, load, gram, cross = refs[-4:]
        at = pl.program_id(0)
        firsts = [pl.multiple_of((k ^ me_ref[0]) * width, width) for k in ids]
        terms = lambda j, h: refs[3 * (j * HALVES + h) : 3 * (j * HALVES + h) + 3]

        @pl.when(at == 0)
        def _():
            behind = slice(cols, cols + extra)
            for j in range(len(ids)):
                for h in range(HALVES):
                    own, end, other = terms(j, h)
                    gram[j * width : (j + 1) * width, h * extra : (h + 1) * extra] = own[:, behind] + (
                        end[:, behind] + other[:, behind]
                    )
            low = gram[...]
            row = lax.broadcasted_iota(jnp.int32, low.shape, 0) // width
            col = lax.broadcasted_iota(jnp.int32, low.shape, 1) // width
            gram[...] = jnp.where(col <= row, low, low.T)

        for h in range(HALVES):

            @pl.when(at // per == h)
            def _():
                here = pl.ds(pl.multiple_of((at - h * per) * step, step), step)
                for j in range(len(ids)):
                    own, end, other = terms(j, h)
                    cross[j * width : (j + 1) * width, :] = own[:, here] + (end[:, here] + other[:, here])

        for j, first in enumerate(firsts):
            load[j * width : (j + 1) * width, :] = load_ref[pl.ds(first, width), :]
        value = load[...]
        (gram_hi, gram_lo), (hi, lo) = split(gram[...]), split(value)
        below = dot(gram_hi, hi, PLAIN) + (dot(gram_hi, lo, PLAIN) + dot(gram_lo, hi, PLAIN))
        value = value * cross[...] / below
        for j, first in enumerate(firsts):
            out_ref[pl.ds(first, width), :] = value[j * width : (j + 1) * width]

    block = pl.BlockSpec((width_all, step), lambda i, f: (0, i))
    return kernel_call(
        body,
        pltpu.HBM((width_all, genes), F32),
        0.02,
        limit=16,
        grid_spec=pltpu.PrefetchScalarGridSpec(
            num_scalar_prefetch=1,
            grid=(HALVES * per,),
            in_specs=[block] + [VMEM_SPEC] * len(arrays) + [ANY_SPEC],
            out_specs=block,
            scratch_shapes=[
                pltpu.VMEM((width_all, step), F32),
                pltpu.VMEM((width_all, width_all), F32),
                pltpu.VMEM((width_all, step), F32),
            ],
        ),
    )(me, loadings, *arrays, token)


def on_device(counts, factors, loadings, position, edge_codes):
    bins, genes_n = lax.axis_size("bin"), lax.axis_size("gene")
    line = bins // 2
    me, bin_me = lax.axis_index("gene"), lax.axis_index("bin")
    rows, width_all = factors.shape
    width = width_all // genes_n
    scalar = lambda x: jnp.asarray(x, jnp.int32).reshape(1)
    me1, bin1 = scalar(me), scalar(bin_me)
    core, chip = bin1 & 1, bin1 >> 1
    flags = jnp.concatenate([me1, core, jnp.where(core == 0, chip, line - 1 - chip)])
    bits = [1 << b for b in range(genes_n.bit_length() - 1)]

    counts = pltpu.with_memory_space_constraint(counts, pltpu.HBM)
    payload = pack(factors, position, me1, width, bins)
    got = lax.all_to_all(payload, "bin", split_axis=0, concat_axis=0, tiled=True)
    in_hbm = lambda x: pltpu.with_memory_space_constraint(x, pltpu.HBM)

    orders = (bits, bits[::-1])
    token, load = payload, pltpu.with_memory_space_constraint(loadings, pltpu.HBM)
    parts, keeps, gram = [None, None], [None, None], None
    third = rows // 3
    numer_parts = ((0, third), (third, rows - third))
    for half in (1, 0):
        bit = orders[half][0]
        send_ids = [k for k in range(genes_n) if k & bit]
        keeps[half] = [k for k in range(genes_n) if not k & bit]
        send, keep, *made = numer_part(
            counts, load, gram, me1, genes_n, numer_parts[half], send_ids, token
        )
        load, gram = made or (load, gram)
        token = keep
        parts[half] = [keep, swap(send, "gene", bit)]

    def scatter_more(half, bit, token):
        out_ids = [i for i, k in enumerate(keeps[half]) if k & bit]
        in_ids = [i for i, k in enumerate(keeps[half]) if not k & bit]
        keeps[half] = [keeps[half][i] for i in in_ids]
        parts[half] = [in_hbm(x) for x in parts[half]]
        send = picked_sum(parts[half], out_ids, token)
        if len(in_ids) > 1:
            parts[half] = [picked_sum(parts[half], in_ids, send)]
        parts[half] = parts[half] + [swap(send, "gene", bit)]
        return send

    grid, first, last, cell = to_grid(got, edge_codes, bin1, token)
    above = lax.ppermute(last, "bin", [(i, i + 1) for i in range(bins - 1)])
    below = lax.ppermute(first, "bin", [(i + 1, i) for i in range(bins - 1)])
    token = grid
    for i in range(1, len(bits)):
        for half in (1, 0):
            token = scatter_more(half, orders[half][i], token)
    smooth = from_grid(grid, above, below, cell, edge_codes, bins, token)
    back = lax.all_to_all(smooth, "bin", split_axis=0, concat_axis=0, tiled=True)
    numer, plain = plain_terms(*[[in_hbm(x) for x in p] for p in parts], in_hbm(factors), smooth)
    own_block = new_factors(*[in_hbm(x) for x in (payload, back, numer, plain)])

    ids = sorted(range(genes_n), key=lambda k: (bin(k).count("1"), k))
    groups = [[k for k in ids if bin(k).count("1") == n] for n in range(len(bits) + 1)]
    chunks = len(ids)
    blocks = {0: own_block}
    for k in bits:
        blocks[k] = swap(own_block, "gene", k)

    coming = {}

    def come_on(group, token):
        axes = [(k & -k, 1 << (k.bit_length() - 1)) for k in group]
        sources = [(blocks[k ^ bit], j) for k, pair in zip(group, axes) for j, bit in enumerate(pair)]
        outs = sent_on(sources, token)
        for i, (k, pair) in enumerate(zip(group, axes)):
            coming[k] = [swap(outs[2 * i + j], "gene", bit) for j, bit in enumerate(pair)]
        return outs[-1]

    pending = [[None] * len(groups) for _ in range(HALVES)]
    own = [{} for _ in range(HALVES)]
    come = [[] for _ in range(HALVES)]
    ends = [{} for _ in range(HALVES)]

    def product(g, half, *tokens):
        upto = ids.index(groups[g][-1]) + 1
        n_old = upto - len(groups[g])
        parts = cross_part([blocks[k] for k in ids[:upto]], n_old, held, half, width_all, tokens)
        pending[half][g] = (parts, [swap(part, "bin", 1) for part in parts])
        return parts[-1]

    def own_chunks(g, half, token):
        arrays = both_cores(*pending[half][g], token)
        for k, array in zip(groups[g], arrays):
            own[half][ids.index(k)] = array
        return arrays[-1]

    def slot(half, t, token):
        before = come[half][-1] if come[half] else None
        got, token = line_slot(flags, t, chunks, own[half], before, token)
        come[half].append(got)
        return token

    def end(c, half, token):
        ends[half][c] = line_end(flags, come[half][c : c + line - 1], token)
        return ends[half][c][0]

    def both(step, *args):
        nonlocal token
        for half in range(HALVES):
            token = step(*args, half, token)

    def awaited(arrays, token):
        return tiny_token(list(arrays) + [token])

    made = first_cross(own_block, counts, width_all, own_block)
    parts, held = made[:HALVES], made[HALVES:]
    for half in range(HALVES):
        pending[half][0] = ((parts[half],), [swap(parts[half], "bin", 1)])
    token = awaited([blocks[k] for k in bits], parts[-1])
    if len(groups) > 2:
        token = come_on(groups[2], token)
    for half in range(HALVES):
        token = own_chunks(0, half, token)
        token = slot(half, 0, token)
    both(product, 1)
    firsts = {ids.index(group[0]): g for g, group in enumerate(groups)}
    last_slot = chunks + line - 3
    for t in range(1, last_slot + 1):
        if t in firsts and firsts[t] + 1 < len(groups):
            later = groups[firsts[t] + 1]
            for k, block in zip(later, joined([coming[k] for k in later], token)):
                blocks[k] = token = block
            for half in range(HALVES):
                token = awaited([come[half][-1]], token)
        for half in range(HALVES):
            if t in firsts:
                token = own_chunks(firsts[t], half, token)
            token = slot(half, t, token)
        g = firsts.get(t, len(groups)) + 1
        if g < len(groups):
            both(product, g)
            if g + 1 < len(groups):
                token = come_on(groups[g + 1], token)
        if t == last_slot - 1:
            factors_new, token = turned_back([blocks[k] for k in ids], ids, width, me1, token)
        due = range(1) if t == last_slot - 1 else range(1, t - line + 2) if t == last_slot else []
        for c in due:
            if c - 1 in ends[0]:
                token = awaited([ends[half][c - 1][1] for half in range(HALVES)], token)
            both(end, c)
    rest = [c for c in range(chunks) if c not in ends[0]]
    for c in rest:
        both(end, c)
    sums = [[(own[h][c],) + ends[h][c] for h in range(HALVES)] for c in range(chunks)]
    loadings_new = new_loadings(loadings, sums, ids, me1, token)
    return factors_new, loadings_new


def solution(mesh):
    placed = (P("bin", "gene"), P("bin", None), P(None, "gene"), P("bin"), P("bin", None))
    return jax.shard_map(
        on_device,
        mesh=mesh,
        in_specs=placed,
        out_specs=(P("bin", None), P(None, "gene")),
        check_vma=False,
    )
```
